32 devices in a mesh: wide: 8 (over y, x, core), narrow: 4 (over z).
Axes of the slice: x: 2, y: 2, z: 4, core: 2. Of those that a mesh axis runs over, the one named last changes fastest.
Arguments:
- tokens: bfloat16 [768, 24576], P('narrow', 'wide'), may hold values from -6 to 6
- lengths: int32 [192], P('wide'), may hold values from 64 to 128
- masked: int32 [192, 128], P('wide'), may hold values 0 or 1
- cotangent: bfloat16 [768, 24576], P('narrow', 'wide'), may hold values from -6 to 6
- mask_vector: float32 [768], P('narrow'), may hold values from -4 to 4
- gain_one: float32 [2, 768], P(None, 'narrow'), may hold values from 0.5 to 1.5
- in_first: bfloat16 [2, 4, 73728], P(None, 'narrow'), may hold values from -0.4375 to 0.4375
- in_second: bfloat16 [2, 4, 147456], P(None, 'narrow'), may hold values from -0.3125 to 0.3125
- short_taps: float32 [2, 3, 4, 384], P(None, None, 'narrow'), may hold values from -3.5 to 3.5
- skip_gain: float32 [2, 768], P(None, 'narrow'), may hold values from -4 to 4
- decay_rates: float32 [2, 768], P(None, 'narrow'), may hold values from 0.00390625 to 0.03125
- filter_one: float32 [2, 5, 128], replicated, may hold values from -2.5 to 2.5
- filter_bias: float32 [2, 128], replicated, may hold values from -3.140625 to 3.140625
- filter_two: float32 [2, 128, 128], replicated, may hold values from -0.5 to 0.5
- filter_three: float32 [2, 768, 128], P(None, 'narrow'), may hold values from -0.5 to 0.5
- out_first: bfloat16 [2, 4, 36864], P(None, 'narrow'), may hold values from -0.4375 to 0.4375
- out_second: bfloat16 [2, 4, 36864], P(None, 'narrow'), may hold values from -0.4375 to 0.4375
- gain_two: float32 [2, 768], P(None, 'narrow'), may hold values from 0.5 to 1.5
- up_first: bfloat16 [2, 4, 36864], P(None, 'narrow'), may hold values from -0.4375 to 0.4375
- up_second: bfloat16 [2, 4, 294912], P(None, 'narrow'), may hold values from -0.4375 to 0.4375
- down_first: bfloat16 [2, 4, 147456], P(None, 'narrow'), may hold values from -0.21875 to 0.21875
- down_second: bfloat16 [2, 4, 36864], P(None, 'narrow'), may hold values from -0.4375 to 0.4375
Outputs:
- mixed_out: bfloat16 [768, 24576], P('narrow', 'wide')
- grad_tokens: float32 [768, 24576], P('narrow', 'wide')
- grad_mask_vector: float32 [768], P('narrow')
- grad_gain_one: float32 [2, 768], P(None, 'narrow')
- grad_in_first: float32 [2, 4, 73728], P(None, 'narrow')
- grad_in_second: float32 [2, 4, 147456], P(None, 'narrow')
- grad_short_taps: float32 [2, 3, 4, 384], P(None, None, 'narrow')
- grad_skip_gain: float32 [2, 768], P(None, 'narrow')
- grad_decay_rates: float32 [2, 768], P(None, 'narrow')
- grad_filter_one: float32 [2, 5, 128], replicated
- grad_filter_bias: float32 [2, 128], replicated
- grad_filter_two: float32 [2, 128, 128], replicated
- grad_filter_three: float32 [2, 768, 128], P(None, 'narrow')
- grad_out_first: float32 [2, 4, 36864], P(None, 'narrow')
- grad_out_second: float32 [2, 4, 36864], P(None, 'narrow')
- grad_gain_two: float32 [2, 768], P(None, 'narrow')
- grad_up_first: float32 [2, 4, 36864], P(None, 'narrow')
- grad_up_second: float32 [2, 4, 294912], P(None, 'narrow')
- grad_down_first: float32 [2, 4, 147456], P(None, 'narrow')
- grad_down_second: float32 [2, 4, 36864], P(None, 'narrow')
The draws below stay inside these ranges and needn't reach their ends.
Inputs may be any that keep to these rules, and one draw needn't show every extreme that they name: lengths[s] positions of sequence s are real tokens; the others are padding. 1 marks a masked position.
All inputs are finite; a program needn't handle non-finite values. No bound on the sum of `masked` on one device may be relied on, other than what follows from the above.
Results may differ from the reference program's by a relative error of at most 0.025.
Values may be sent and summed in bfloat16 or wider, within the bound.
No kernel may reach another device: no remote copies, remote signals or barrier semaphores. Data moves between devices by JAX's collectives and lax.ppermute only.
A program may use at most 384 MiB of HBM per device.

```python
import math
import jax
import jax.numpy as jnp
from jax import lax

D = 768
ORDER = 128
BLOCKS = 4
EMBED = 5
LENGTH = 128
LAYERS = 2
SEQ_DEV = 24
BLOCK_W = 192
FF_BLOCK = 768
SEQS = 192
TOKENS = 24576


def place_ends(drawn, own_key, low, top_value):
    extent = drawn.shape
    place = [jax.random.randint(jax.random.fold_in(own_key, axis), (), 0, extent[axis]) for axis in range(len(extent))]
    drawn = drawn.at[tuple(place)].set(low)
    longest = extent.index(max(extent))
    place[longest] = (place[longest] + 1) % extent[longest]
    return drawn.at[tuple(place)].set(top_value)


def block_scale(own_key, shape, cuts, smallest, high):
    def one(dim, parts):
        draws = jax.random.uniform(jax.random.fold_in(jax.random.fold_in(own_key, 6), dim), (parts,), jnp.float32, smallest / len(cuts), high / len(cuts))
        return jnp.repeat(jnp.exp(draws), shape[dim] // parts).reshape((-1,) + (1,) * (len(shape) - dim - 1))

    loudness = one(*cuts[0])
    for cut in cuts[1:]:
        loudness = loudness * one(*cut)
    return loudness


def scatter_about(stream_key, extent, width, bound, pieces=(), held_as=jnp.bfloat16):
    entries = width * jax.random.normal(stream_key, extent, jnp.float32)
    if pieces:
        entries = entries * block_scale(stream_key, extent, pieces, -0.22, 0.18)
    return jnp.clip(entries, -bound, bound).astype(held_as)


def setup_inputs(seed: int = 0) -> dict:
    streams_of = jax.random.split(jax.random.key(seed), 23)
    return {
        "tokens": scatter_about(streams_of[0], (D, TOKENS), 1.0, 6.0, ((0, 4), (1, 8))),
        "lengths": place_ends(jax.random.randint(streams_of[1], (SEQS,), LENGTH // 2, LENGTH + 1), jax.random.fold_in(streams_of[1], 1), LENGTH // 2, LENGTH).astype(jnp.int32),
        "masked": place_ends((jax.random.randint(streams_of[2], (SEQS, LENGTH), 0, 10) < 3).astype(jnp.int32), jax.random.fold_in(streams_of[2], 1), 0, 1),
        "cotangent": scatter_about(streams_of[3], (D, TOKENS), 1.0, 6.0, ((0, 4), (1, 8))),
        "mask_vector": scatter_about(streams_of[4], (D,), 1.0, 4.0, ((0, 4),), jnp.float32),
        "gain_one": jnp.clip(1.0 + 0.1 * jax.random.normal(streams_of[5], (LAYERS, D), jnp.float32), 0.5, 1.5),
        "in_first": scatter_about(streams_of[6], (LAYERS, BLOCKS, BLOCK_W * 2 * BLOCK_W), BLOCK_W ** -0.5, 0.4375, ((1, 4),)),
        "in_second": scatter_about(streams_of[7], (LAYERS, BLOCKS, 4 * BLOCK_W * BLOCK_W), (2 * BLOCK_W) ** -0.5, 0.3125, ((1, 4),)),
        "short_taps": scatter_about(streams_of[8], (LAYERS, 3, BLOCKS, 2 * BLOCK_W), 3 ** -0.5, 3.5, ((2, 4),), jnp.float32),
        "skip_gain": scatter_about(streams_of[9], (LAYERS, D), 1.0, 4.0, ((1, 4),), jnp.float32),
        "decay_rates": jnp.clip(jnp.exp(math.log(0.03125) - 2.0794415 * jax.random.uniform(streams_of[10], (LAYERS, D), jnp.float32) ** block_scale(streams_of[10], (LAYERS, D), ((1, 4),), -0.2, 0.2)), 0.00390625, 0.03125),
        "filter_one": scatter_about(streams_of[11], (LAYERS, EMBED, ORDER), EMBED ** -0.5, 2.5, (), jnp.float32),
        "filter_bias": jnp.clip(jax.random.uniform(streams_of[12], (LAYERS, ORDER), jnp.float32, -3.140625, 3.140625), -3.140625, 3.140625),
        "filter_two": scatter_about(streams_of[13], (LAYERS, ORDER, ORDER), ORDER ** -0.5, 0.5, (), jnp.float32),
        "filter_three": scatter_about(streams_of[14], (LAYERS, D, ORDER), ORDER ** -0.5, 0.5, ((1, 4),), jnp.float32),
        "out_first": scatter_about(streams_of[15], (LAYERS, BLOCKS, BLOCK_W * BLOCK_W), BLOCK_W ** -0.5, 0.4375, ((1, 4),)),
        "out_second": scatter_about(streams_of[16], (LAYERS, BLOCKS, BLOCK_W * BLOCK_W), BLOCK_W ** -0.5, 0.4375, ((1, 4),)),
        "gain_two": jnp.clip(1.0 + 0.1 * jax.random.normal(streams_of[17], (LAYERS, D), jnp.float32), 0.5, 1.5),
        "up_first": scatter_about(streams_of[18], (LAYERS, BLOCKS, BLOCK_W * BLOCK_W), BLOCK_W ** -0.5, 0.4375, ((1, 4),)),
        "up_second": scatter_about(streams_of[19], (LAYERS, BLOCKS, BLOCK_W * 2 * FF_BLOCK), BLOCK_W ** -0.5, 0.4375, ((1, 4),)),
        "down_first": scatter_about(streams_of[20], (LAYERS, BLOCKS, FF_BLOCK * BLOCK_W), FF_BLOCK ** -0.5, 0.21875, ((1, 4),)),
        "down_second": scatter_about(streams_of[21], (LAYERS, BLOCKS, BLOCK_W * BLOCK_W), BLOCK_W ** -0.5, 0.4375, ((1, 4),)),
    }


epsilon = 1e-05
highest = lax.Precision.HIGHEST

@jax.custom_vjp
def low(v):
    return lax.optimization_barrier(v.astype(jnp.bfloat16)).astype(jnp.float32)

@jax.custom_vjp
def low_back(v):
    return v

def low_keep(v):
    return (low(v), None)

def low_pass(kept, grad):
    return (grad,)

def back_keep(v):
    return (v, None)

def back_low(kept, grad):
    return (low(grad),)
low.defvjp(low_keep, low_pass)
low_back.defvjp(back_keep, back_low)

def round_both(values):
    return low(low_back(values))

def filter_table(weight_one, bias_one, weight_two, weight_three, decay_rate):
    lag_values = jnp.arange(-(LENGTH - 1), LENGTH).astype(weight_one.dtype)
    relative = lag_values / LENGTH
    features = jnp.stack([relative, jnp.cos(math.pi * relative), jnp.sin(math.pi * relative), jnp.cos(37.0 * math.pi * relative), jnp.sin(37.0 * math.pi * relative)], axis=1)
    hidden_one = jnp.sin(jnp.dot(features, weight_one, precision=highest) + bias_one)
    hidden_two = jnp.sin(jnp.dot(hidden_one, weight_two, precision=highest))
    shaped = jnp.dot(hidden_two, weight_three.T, precision=highest)
    envelope = jnp.exp(-jnp.abs(lag_values)[:, None] * decay_rate[None, :])
    return shaped * envelope / math.sqrt(LENGTH)

def monarch(row_block, factor_one, factor_two):
    tok_rows = row_block.shape[0]
    blocks = factor_one.shape[0]
    inner_width = factor_one.shape[2]
    split_rows = row_block.reshape(tok_rows, blocks, factor_one.shape[1])
    middle = round_both(jnp.einsum('tbi,bik->tbk', split_rows, factor_one, precision=highest))
    middle = middle.reshape(tok_rows, blocks, blocks, inner_width // blocks)
    middle = jnp.transpose(middle, (0, 2, 1, 3)).reshape(tok_rows, blocks, inner_width)
    result = jnp.einsum('tck,cko->tco', middle, factor_two, precision=highest)
    return low_back(result.reshape(tok_rows, -1))

def layer_norm(row_block, gain_row):
    centre = row_block - lax.optimization_barrier(jnp.mean(row_block, axis=1, keepdims=True))
    spread = lax.optimization_barrier(jnp.mean(centre * centre, axis=1, keepdims=True))
    return centre * lax.rsqrt(spread + epsilon) * gain_row

def long_convolution(signal, kernel):
    circular = jnp.concatenate([kernel[LENGTH - 1:], jnp.zeros((1, kernel.shape[1]), kernel.dtype), kernel[:LENGTH - 1]], axis=0)
    spectrum = jnp.fft.rfft(signal, n=2 * LENGTH, axis=1) * jnp.fft.rfft(circular, axis=0)[None]
    return jnp.fft.irfft(spectrum, n=2 * LENGTH, axis=1)[:, :LENGTH]

def mixer_layer(row_block, padding, params, kernel):
    gain_one, in_first, in_second, short_taps, skip_gain, out_first, out_second, gain_two, up_first, up_second, down_first, down_second = params
    seqs_here = padding.shape[0]
    blocks = in_first.shape[0]
    block_width = in_first.shape[1]
    ff_block = down_first.shape[1]
    normed = low(layer_norm(row_block, gain_one))
    mixed_rows = monarch(normed, in_first, in_second).reshape(seqs_here, LENGTH, blocks, 2, block_width)
    mixed_rows = mixed_rows * padding[:, :, None, None, None]
    tap_table = short_taps.reshape(3, blocks, 2, block_width)
    padded = jnp.pad(mixed_rows, ((0, 0), (1, 1), (0, 0), (0, 0), (0, 0)))
    smoothed = tap_table[0] * padded[:, :-2] + tap_table[1] * padded[:, 1:-1] + tap_table[2] * padded[:, 2:]
    signal = smoothed[:, :, :, 0].reshape(seqs_here, LENGTH, blocks * block_width)
    gating = smoothed[:, :, :, 1].reshape(seqs_here, LENGTH, blocks * block_width)
    convolved = long_convolution(signal, kernel) + skip_gain * signal
    gated_rows = low((convolved * gating).reshape(-1, blocks * block_width))
    middle = row_block + monarch(gated_rows, out_first, out_second)
    normed_two = low(layer_norm(middle, gain_two))
    gate_up = monarch(normed_two, up_first, up_second).reshape(-1, blocks, 2, ff_block)
    activated = low((jax.nn.gelu(gate_up[:, :, 0]) * gate_up[:, :, 1]).reshape(-1, blocks * ff_block))
    return middle + monarch(activated, down_first, down_second)

def forward(tokens, mask_vector, gain_one, in_first, in_second, short_taps, skip_gain, decay_rates, filter_one, filter_bias, filter_two, filter_three, out_first, out_second, gain_two, up_first, up_second, down_first, down_second, padding, chosen):
    kernels = [filter_table(filter_one[layer_at], filter_bias[layer_at], filter_two[layer_at], filter_three[layer_at], decay_rates[layer_at]) for layer_at in range(LAYERS)]
    penalty = 2.0 * math.sqrt(TOKENS) * sum((jnp.sum(kernel_item * kernel_item) for kernel_item in kernels))
    start_rows = tokens.T * (1.0 - chosen) + chosen * mask_vector[None, :]
    groups = SEQS // SEQ_DEV
    grouped = start_rows.reshape(groups, SEQ_DEV * LENGTH, D)
    grouped_pad = padding.reshape(groups, SEQ_DEV, LENGTH)
    stacked = (gain_one, in_first.reshape(LAYERS, BLOCKS, BLOCK_W, 2 * BLOCK_W), in_second.reshape(LAYERS, BLOCKS, 2 * BLOCK_W, 2 * BLOCK_W), short_taps, skip_gain, out_first.reshape(LAYERS, BLOCKS, BLOCK_W, BLOCK_W), out_second.reshape(LAYERS, BLOCKS, BLOCK_W, BLOCK_W), gain_two, up_first.reshape(LAYERS, BLOCKS, BLOCK_W, BLOCK_W), up_second.reshape(LAYERS, BLOCKS, BLOCK_W, 2 * FF_BLOCK), down_first.reshape(LAYERS, BLOCKS, FF_BLOCK, BLOCK_W), down_second.reshape(LAYERS, BLOCKS, BLOCK_W, BLOCK_W))

    def group_pass(group_in):
        row_block, pad_rows = group_in
        for layer_at in range(LAYERS):
            params = tuple((weight_item[layer_at] for weight_item in stacked))
            row_block = mixer_layer(row_block, pad_rows, params, kernels[layer_at])
        return row_block
    result = lax.map(jax.checkpoint(group_pass), (grouped, grouped_pad))
    return (result.reshape(TOKENS, D).T, penalty)

def reference(tokens, lengths, masked, cotangent, mask_vector, gain_one, in_first, in_second, short_taps, skip_gain, decay_rates, filter_one, filter_bias, filter_two, filter_three, out_first, out_second, gain_two, up_first, up_second, down_first, down_second):
    positions = jnp.arange(LENGTH).astype(jnp.int32)
    padding = (positions[None, :] < lengths[:, None]).astype(jnp.float32)
    chosen = masked.reshape(TOKENS, 1).astype(jnp.float32)
    floats = tuple((weight_item.astype(jnp.float32) for weight_item in (tokens, mask_vector, gain_one, in_first, in_second, short_taps, skip_gain, decay_rates, filter_one, filter_bias, filter_two, filter_three, out_first, out_second, gain_two, up_first, up_second, down_first, down_second)))

    def objective(*arrays):
        return forward(*arrays, padding, chosen)
    (outputs, penalty), pull_back = jax.vjp(objective, *floats)
    gradients = pull_back((cotangent.astype(jnp.float32), jnp.ones_like(penalty)))
    return (outputs.astype(jnp.bfloat16), gradients[0], gradients[1], gradients[2], gradients[3], gradients[4], gradients[5], gradients[6], gradients[7], gradients[8], gradients[9], gradients[10], gradients[11], gradients[12], gradients[13], gradients[14], gradients[15], gradients[16], gradients[17], gradients[18])
```

```python
import math
import functools
import numpy as np
import jax
import jax.numpy as jnp
from jax import lax
from jax.experimental import pallas as pl
from jax.experimental.pallas import tpu as pltpu
from jax.sharding import PartitionSpec as P

F32 = jnp.float32
BF16 = jnp.bfloat16
D = 768
LENGTH = 128
LAYERS = 2
BLOCK_W = 192
FF_BLOCK = 768
BLOCKS = 4
EPSILON = 1e-05
HIGHEST = lax.Precision.HIGHEST
GAIN_ONE, GAIN_TWO, SKIP, TAP_X, TAP_G, MASK, DECAY = 0, 1, 2, 3, 6, 9, 10
IN_ONE, IN_TWO, OUT_ROWS, PARAM_ROWS = 0, 192, 576, 768
UP_ONE, UP_TWO, DOWN_ONE = 0, 192, 960
MIX_ROWS, FF_USED, FF_ROWS, IN_GRAD_ROWS = 1024, 1344, 1408, 640
PIECE_ROWS = {"ff": 176, "conv": 48, "in": 80}
FINISH_ORDER = (("ff", "conv", "in"),) * LAYERS


def nn(a, b):
    return lax.dot_general(a, b, (((1,), (0,)), ((), ())), preferred_element_type=F32)


def nt(a, b):
    return lax.dot_general(a, b, (((1,), (1,)), ((), ())), preferred_element_type=F32)


def tn(a, b):
    return lax.dot_general(a, b, (((0,), (0,)), ((), ())), preferred_element_type=F32)


def spectrum_tables():
    time = np.arange(2 * LENGTH)
    freq = np.arange(LENGTH)
    angle = 2.0 * np.pi * np.outer(time, freq) / (2 * LENGTH)
    ahead = np.concatenate([np.cos(angle), -np.sin(angle)], axis=1)
    ahead[:, LENGTH] = np.cos(np.pi * time)
    scale = np.full((2 * LENGTH,), 2.0 / (2 * LENGTH))
    scale[0] = scale[LENGTH] = 1.0 / (2 * LENGTH)
    return ahead.astype(np.float32), (ahead * scale[None, :]).T.astype(np.float32)


def lanes_of(shape):
    return lax.broadcasted_iota(jnp.int32, shape, 1)


def later(v, lane):
    return jnp.where(lane == 0, 0.0, pltpu.roll(v, 1, 1))


def earlier(v, lane):
    return jnp.where(lane == LENGTH - 1, 0.0, pltpu.roll(v, LENGTH - 1, 1))


def norm_rows(parts):
    total = sum(jnp.sum(p, axis=0, keepdims=True) for p in parts)
    squares = sum(jnp.sum(p * p, axis=0, keepdims=True) for p in parts)
    mean = total / D
    inv = lax.rsqrt(squares / D - mean * mean + EPSILON)
    return mean, inv


def block(ref, b, width=BLOCK_W):
    return ref[pl.ds(b * width, width), :]


def fwd_mix_kernel(first, seqs, *refs):
    idx, own, rel_a, rel_b, *refs = refs
    if first:
        *parts, chosen_ref = refs[: BLOCKS + 1]
        refs = refs[BLOCKS + 1 :]
    else:
        h_ref, *refs = refs
    pad, hidden, ahead_full, ahead, back, *refs = refs
    if first:
        h_ref, *refs = refs
    q1, proj, conv, gated, q2, middle, stats, cols, kspec, w, normed, xs, gs, sem = refs
    fetch_table(idx, own, rel_a, rel_b, w, sem)
    make_params(w, hidden, ahead_full, cols, kspec)
    if first:
        keep = chosen_ref[0:1, :]
        for k, part in enumerate(parts):
            rows = pl.ds(pl.multiple_of(block_of(idx, k) * BLOCK_W, BLOCK_W), BLOCK_W)
            h_ref[rows, :] = part[...].astype(F32) * (1.0 - keep) + keep * cols[rows, MASK : MASK + 1]
    mean, inv = norm_rows([block(h_ref, b) for b in range(BLOCKS)])
    stats[0:1, :] = mean
    stats[1:2, :] = inv
    for b in range(BLOCKS):
        rows = pl.ds(b * BLOCK_W, BLOCK_W)
        normed[rows, :] = ((h_ref[rows, :] - mean) * inv * cols[rows, GAIN_ONE : GAIN_ONE + 1]).astype(BF16)
    for b in range(BLOCKS):
        inner = tn(w[b, IN_ONE : IN_ONE + 192, :], block(normed, b)).astype(BF16)
        for c in range(BLOCKS):
            q1[c, 96 * b : 96 * b + 96, :] = inner[96 * c : 96 * c + 96]
    lane = lanes_of((BLOCK_W, LENGTH))
    row_lane = lanes_of((BLOCK_W, LENGTH))
    for c in range(BLOCKS):
        rows = pl.ds(c * BLOCK_W, BLOCK_W)
        value = tn(w[c, IN_TWO : IN_TWO + 384, :], q1[c]) * pad[0:1, :]
        proj[c] = value.astype(BF16)
        for s in range(seqs):
            here = slice(s * LENGTH, (s + 1) * LENGTH)
            for part, tap, out in ((0, TAP_X, xs), (192, TAP_G, gs)):
                v = value[part : part + 192, here]
                out[:, here] = (
                    cols[rows, tap : tap + 1] * later(v, lane)
                    + cols[rows, tap + 1 : tap + 2] * v
                    + cols[rows, tap + 2 : tap + 3] * earlier(v, lane)
                )
        signal = jnp.concatenate([xs[:, s * LENGTH : (s + 1) * LENGTH] for s in range(seqs)], axis=0)
        spec = nn(signal.astype(BF16), ahead[...])
        k_re = kspec[rows, 0:LENGTH]
        k_im = kspec[rows, LENGTH : 2 * LENGTH]
        k_off = jnp.where(row_lane == 0, 0.0, k_im)
        k_im = jnp.where(row_lane == 0, k_im, k_re)
        made = []
        for s in range(seqs):
            re = spec[s * 192 : s * 192 + 192, 0:LENGTH]
            im = spec[s * 192 : s * 192 + 192, LENGTH : 2 * LENGTH]
            made.append(
                jnp.concatenate([re * k_re - im * k_off, re * k_off + im * k_im], axis=1).astype(BF16)
            )
        y = nn(jnp.concatenate(made, axis=0), back[...])
        for s in range(seqs):
            here = slice(s * LENGTH, (s + 1) * LENGTH)
            value = y[s * 192 : s * 192 + 192] + cols[rows, SKIP : SKIP + 1] * xs[:, here]
            conv[rows, here] = value.astype(BF16)
            gated[rows, here] = (value * gs[:, here]).astype(BF16)
    for b in range(BLOCKS):
        inner = tn(w[b, OUT_ROWS : OUT_ROWS + 192, 0:192], block(gated, b)).astype(BF16)
        for c in range(BLOCKS):
            q2[c, 48 * b : 48 * b + 48, :] = inner[48 * c : 48 * c + 48]
    for c in range(BLOCKS):
        rows = pl.ds(c * BLOCK_W, BLOCK_W)
        middle[rows, :] = h_ref[rows, :] + tn(w[c, OUT_ROWS : OUT_ROWS + 192, 192:384], q2[c])


def gelu_parts(v):
    inner = math.sqrt(2.0 / math.pi) * (v + 0.044715 * (v * v * v))
    return jnp.tanh(inner)


def fwd_ff_kernel(last, idx, own, rel_a, rel_b, middle, cols, q3, gate_up, q4, h_next, stats, w, normed, act, sem):
    fetch_table(idx, own, rel_a, rel_b, w, sem)
    mean, inv = norm_rows([block(middle, b) for b in range(BLOCKS)])
    stats[0:1, :] = mean
    stats[1:2, :] = inv
    for b in range(BLOCKS):
        rows = pl.ds(b * BLOCK_W, BLOCK_W)
        normed[rows, :] = ((middle[rows, :] - mean) * inv * cols[rows, GAIN_TWO : GAIN_TWO + 1]).astype(BF16)
    for b in range(BLOCKS):
        inner = tn(w[b, UP_ONE : UP_ONE + 192, 0:192], block(normed, b)).astype(BF16)
        for c in range(BLOCKS):
            q3[c, 48 * b : 48 * b + 48, :] = inner[48 * c : 48 * c + 48]
    for c in range(BLOCKS):
        for half in range(2):
            ups = []
            for piece in (half, half + 2):
                ups.append(tn(w[c, UP_TWO + 192 * piece : UP_TWO + 192 * piece + 192, :], q3[c]))
            gate, up = ups
            gate_up[c, 384 * half : 384 * half + 384, :] = gate.astype(BF16)
            gate_up[c, 768 + 384 * half : 768 + 384 * half + 384, :] = up.astype(BF16)
            act[384 * half : 384 * half + 384, :] = (
                0.5 * gate * (1.0 + gelu_parts(gate)) * up
            ).astype(BF16)
        inner = (
            tn(w[c, DOWN_ONE : DOWN_ONE + 384, 0:192], act[0:384, :])
            + tn(w[c, DOWN_ONE : DOWN_ONE + 384, 192:384], act[384:768, :])
        ).astype(BF16)
        for to in range(BLOCKS):
            q4[to, 48 * c : 48 * c + 48, :] = inner[48 * to : 48 * to + 48]
    for c in range(BLOCKS):
        rows = pl.ds(c * BLOCK_W, BLOCK_W)
        value = middle[rows, :] + tn(w[c, UP_ONE : UP_ONE + 192, 192:384], q4[c])
        if last:
            h_next[(c - idx[0]) & (BLOCKS - 1)] = value.astype(BF16)
        else:
            h_next[rows, :] = value


def bwd_ff_kernel(last, idx, own, rel_a, rel_b, *refs):
    parts = refs[: BLOCKS if last else 1]
    q4, gate_up, q3, middle, stats, cols, g_mid, g_out, small, w, g_w, g_low, gi4, gi3, g_gu, g_n, sem = refs[len(parts) :]
    fetch_table(idx, own, rel_a, rel_b, w, sem)
    mean = stats[0:1, :]
    inv = stats[1:2, :]
    if last:
        for k, part in enumerate(parts):
            g_low[pl.ds(pl.multiple_of(block_of(idx, k) * BLOCK_W, BLOCK_W), BLOCK_W), :] = part[...]
        g_top = g_low
    else:
        (g_top,) = parts
        for c in range(BLOCKS):
            g_low[c * 192 : c * 192 + 192, :] = block(g_top, c).astype(BF16)
    for b in range(BLOCKS):
        g_w[b, FF_USED:FF_ROWS, :] = jnp.zeros((FF_ROWS - FF_USED, 384), BF16)
    for c in range(BLOCKS):
        gt = block(g_low, c)
        g_w[c, UP_ONE : UP_ONE + 192, 192:384] = nt(q4[c], gt).astype(BF16)
        gq = nn(w[c, UP_ONE : UP_ONE + 192, 192:384], gt).astype(BF16)
        for b in range(BLOCKS):
            gi4[b, 48 * c : 48 * c + 48, :] = gq[48 * b : 48 * b + 48]
    rate = math.sqrt(2.0 / math.pi)
    for b in range(BLOCKS):
        for half in range(2):
            span = slice(192 * half, 192 * half + 192)
            gate = gate_up[b, 384 * half : 384 * half + 384, :].astype(F32)
            up = gate_up[b, 768 + 384 * half : 768 + 384 * half + 384, :].astype(F32)
            ga = nn(w[b, DOWN_ONE : DOWN_ONE + 384, span], gi4[b])
            square = gate * gate
            t = jnp.tanh(rate * gate * (1.0 + 0.044715 * square))
            rise = 0.5 * (1.0 + t)
            gelu = gate * rise
            slope = rise + 0.5 * gelu_slope(gate, square, t, rate)
            act = (gelu * up).astype(BF16)
            g_w[b, DOWN_ONE : DOWN_ONE + 384, span] = nt(act, gi4[b]).astype(BF16)
            g_gu[384 * half : 384 * half + 384, :] = (ga * up * slope).astype(BF16)
            g_gu[768 + 384 * half : 768 + 384 * half + 384, :] = (ga * gelu).astype(BF16)
        gq = None
        for piece in range(4):
            rows = slice(UP_TWO + 192 * piece, UP_TWO + 192 * piece + 192)
            gg = g_gu[384 * piece : 384 * piece + 384, :]
            g_w[b, rows, :] = nt(q3[b], gg).astype(BF16)
            term = nn(w[b, rows, :], gg)
            gq = term if gq is None else gq + term
        gq = gq.astype(BF16)
        for to in range(BLOCKS):
            gi3[to, 48 * b : 48 * b + 48, :] = gq[48 * to : 48 * to + 48]
    norm_back(
        middle, mean, inv, cols, GAIN_TWO, w, slice(UP_ONE, UP_ONE + 192), slice(0, 192), gi3, g_n, g_w, small, 1, g_top, g_mid
    )
    send_pieces(g_w, g_out, idx, sem)


def gelu_slope(gate, square, t, rate):
    return gate * (1.0 - t * t) * (rate * (1.0 + 3.0 * 0.044715 * square))


def row_sums(place, values):
    lanes = values.shape[1]
    part = values[:, 0:LENGTH]
    for at in range(LENGTH, lanes, LENGTH):
        part = part + values[:, at : at + LENGTH]
    high = part.astype(BF16)
    low = (part - high.astype(F32)).astype(BF16)
    pick = (lax.broadcasted_iota(jnp.int32, (16, LENGTH), 0) == place).astype(F32).astype(BF16)
    return nt(pick, high) + nt(pick, low)


def norm_back(h, mean, inv, cols, gain_at, w, w_rows, w_lanes, gi, g_n, g_w, small, place, g_in, g_out):
    plain = cross = 0.0
    for b in range(BLOCKS):
        rows = pl.ds(b * 192, 192)
        gain = cols[rows, gain_at : gain_at + 1]
        xh = (h[rows, :] - mean) * inv
        gn = nn(w[b, w_rows, w_lanes], gi[b])
        g_w[b, w_rows, w_lanes] = nt((xh * gain).astype(BF16), gi[b]).astype(BF16)
        gx = gn * xh
        small[b] = row_sums(place, gx)
        g_n[rows, :] = gn * gain
        plain = plain + jnp.sum(gn * gain, axis=0, keepdims=True)
        cross = cross + jnp.sum(gx * gain, axis=0, keepdims=True)
    plain = plain / D
    cross = cross / D
    for b in range(BLOCKS):
        rows = pl.ds(b * 192, 192)
        xh = (h[rows, :] - mean) * inv
        g_out[rows, :] = g_in[rows, :].astype(F32) + inv * (g_n[rows, :] - plain - xh * cross)


def bwd_conv_kernel(
    seqs, idx, own, rel_a, rel_b, g_mid, q2, gated, conv, proj, pad, cols, kspec, ahead, back, small_ff, gv, g_out, w, g_w, gi2, gcs, xs, sem
):
    fetch_table(idx, own, rel_a, rel_b, w, sem)
    for c in range(BLOCKS):
        gt = block(g_mid, c).astype(BF16)
        g_w[c, 0:192, 192:384] = nt(q2[c], gt).astype(BF16)
        gq = nn(w[c, OUT_ROWS : OUT_ROWS + 192, 192:384], gt).astype(BF16)
        for b in range(BLOCKS):
            gi2[b, 48 * c : 48 * c + 48, :] = gq[48 * b : 48 * b + 48]
    lane = lanes_of((BLOCK_W, LENGTH))
    first_lane = lane == 0
    for b in range(BLOCKS):
        rows = pl.ds(b * 192, 192)
        g_gated = nn(w[b, OUT_ROWS : OUT_ROWS + 192, 0:192], gi2[b])
        g_w[b, 0:192, 0:192] = nt(block(gated, b), gi2[b]).astype(BF16)
        sums = [0.0] * 7
        for s in range(seqs):
            here = slice(s * LENGTH, (s + 1) * LENGTH)
            v = proj[b, 0:192, here].astype(F32)
            xs[:, here] = (
                cols[rows, TAP_X : TAP_X + 1] * later(v, lane)
                + cols[rows, TAP_X + 1 : TAP_X + 2] * v
                + cols[rows, TAP_X + 2 : TAP_X + 3] * earlier(v, lane)
            )
            v = proj[b, 192:384, here].astype(F32)
            after, before = later(v, lane), earlier(v, lane)
            gate = (
                cols[rows, TAP_G : TAP_G + 1] * after
                + cols[rows, TAP_G + 1 : TAP_G + 2] * v
                + cols[rows, TAP_G + 2 : TAP_G + 3] * before
            )
            gg = g_gated[:, here]
            gcs[:, here] = gg * gate
            z = gg * conv[rows, here].astype(F32)
            sums[4] = sums[4] + z * after
            sums[5] = sums[5] + z * v
            sums[6] = sums[6] + z * before
            gv[b, 192:384, here] = (
                (
                    cols[rows, TAP_G : TAP_G + 1] * earlier(z, lane)
                    + cols[rows, TAP_G + 1 : TAP_G + 2] * z
                    + cols[rows, TAP_G + 2 : TAP_G + 3] * later(z, lane)
                )
                * pad[0:1, here]
            ).astype(BF16)
            sums[0] = sums[0] + gcs[:, here] * xs[:, here]
        stacked = jnp.concatenate(
            [ref[:, s * LENGTH : (s + 1) * LENGTH] for ref in (xs, gcs) for s in range(seqs)], axis=0
        )
        spec = nn(stacked.astype(BF16), ahead[...])
        k_re = kspec[rows, 0:LENGTH]
        k_im = kspec[rows, LENGTH : 2 * LENGTH]
        k_off = jnp.where(first_lane, 0.0, k_im)
        k_im = jnp.where(first_lane, k_im, k_re)
        made = []
        p_re = p_im = p_off = 0.0
        for s in range(seqs):
            x_re = spec[s * 192 : s * 192 + 192, 0:LENGTH]
            x_im = spec[s * 192 : s * 192 + 192, LENGTH : 2 * LENGTH]
            at = (seqs + s) * 192
            g_re = spec[at : at + 192, 0:LENGTH]
            g_im = spec[at : at + 192, LENGTH : 2 * LENGTH]
            p_re = p_re + g_re * x_re
            p_im = p_im + g_im * x_im
            p_off = p_off + (g_im * x_re - g_re * x_im)
            made.append(
                jnp.concatenate([g_re * k_re + g_im * k_off, g_im * k_im - g_re * k_off], axis=1).astype(BF16)
            )
        g_w[b, 192:384, 0:128] = jnp.where(first_lane, p_re, p_re + p_im).astype(BF16)
        g_w[b, 192:384, 128:256] = jnp.where(first_lane, p_im, p_off).astype(BF16)
        y = nn(jnp.concatenate(made, axis=0), back[...])
        for s in range(seqs):
            here = slice(s * LENGTH, (s + 1) * LENGTH)
            z = y[s * 192 : s * 192 + 192] + cols[rows, SKIP : SKIP + 1] * gcs[:, here]
            v = proj[b, 0:192, here].astype(F32)
            sums[1] = sums[1] + z * later(v, lane)
            sums[2] = sums[2] + z * v
            sums[3] = sums[3] + z * earlier(v, lane)
            gv[b, 0:192, here] = (
                (
                    cols[rows, TAP_X : TAP_X + 1] * earlier(z, lane)
                    + cols[rows, TAP_X + 1 : TAP_X + 2] * z
                    + cols[rows, TAP_X + 2 : TAP_X + 3] * later(z, lane)
                )
                * pad[0:1, here]
            ).astype(BF16)
        table = small_ff[b]
        for at, value in enumerate(sums):
            table = table + row_sums(2 + at, value)
        table = table.astype(BF16)
        g_w[b, 192:208, 256:384] = table[:, 0:128]
        g_w[b, 208:224, 256:320] = table[:, 128:192]
        g_w[b, 208:224, 320:384] = jnp.zeros((16, 64), BF16)
        g_w[b, 224:384, 256:384] = jnp.zeros((160, 128), BF16)
    send_pieces(g_w, g_out, idx, sem)


def bwd_in_kernel(first, *refs):
    refs = list(refs)
    idx, own, rel_a, rel_b, gv, g_mid, q1, h, stats, cols = refs[:10]
    refs = refs[10:]
    chosen = refs.pop(0) if first else None
    g_out, g_send, w, g_w, gi1, g_n, small, sem = refs[:8]
    g_h = refs[8] if first else g_out
    fetch_table(idx, own, rel_a, rel_b, w, sem)
    mean = stats[0:1, :]
    inv = stats[1:2, :]
    for c in range(BLOCKS):
        g_w[c, IN_TWO : IN_TWO + 384, :] = nt(q1[c], gv[c]).astype(BF16)
        gq = nn(w[c, IN_TWO : IN_TWO + 384, :], gv[c]).astype(BF16)
        for b in range(BLOCKS):
            gi1[b, 96 * c : 96 * c + 96, :] = gq[96 * b : 96 * b + 96]
    norm_back(
        h, mean, inv, cols, GAIN_ONE, w, slice(IN_ONE, IN_ONE + 192), slice(0, 384), gi1, g_n, g_w, small, 0, g_mid, g_h
    )
    for b in range(BLOCKS):
        rows = pl.ds(b * 192, 192)
        table = small[b]
        if first:
            value = g_h[rows, :]
            masked = value * chosen[0:1, :]
            table = table + row_sums(1, masked)
            g_out[(b - idx[0]) & (BLOCKS - 1)] = (value - masked).astype(BF16)
        g_w[b, 576:592, 0:192] = table.astype(BF16)
        g_w[b, 576:592, 192:384] = jnp.zeros((16, 192), BF16)
        g_w[b, 592:640, :] = jnp.zeros((48, 384), BF16)
    send_pieces(g_w, g_send, idx, sem)


def piece_rows(idx, core, chip, rows):
    return pl.ds(pl.multiple_of((idx[1] ^ (2 * chip + core)) * rows, 16), rows)


def block_of(idx, k):
    return (idx[0] - k) & (BLOCKS - 1)


def run_copies(pairs, sem):
    copies = [pltpu.make_async_copy(source, target, sem.at[at]) for at, (source, target) in enumerate(pairs)]
    for copy in copies:
        copy.start()
    for copy in copies:
        copy.wait()


def send_pieces(table, out, idx, sem):
    rows = out.shape[3]
    run_copies(
        [
            (table.at[block_of(idx, k), piece_rows(idx, core, chip, rows), :], out.at[core, chip, k])
            for core in range(2)
            for chip in range(4)
            for k in range(BLOCKS)
        ],
        sem,
    )


def fetch_table(idx, own, rel_a, rel_b, table, sem):
    rows = rel_a.shape[2]
    run_copies(
        [(own, table.at[idx[0]])]
        + [
            (rel.at[chip, k - 1], table.at[block_of(idx, k), piece_rows(idx, core, chip, rows), :])
            for core, rel in enumerate((rel_a, rel_b))
            for chip in range(4)
            for k in range(1, BLOCKS)
        ],
        sem,
    )


def make_params(w, hidden, ahead_full, cols, kspec):
    place = lanes_of((BLOCK_W, 2 * LENGTH))
    lag = jnp.where(place < LENGTH, place, 2 * LENGTH - place).astype(F32)
    for b in range(BLOCKS):
        rows = pl.ds(b * BLOCK_W, BLOCK_W)
        packed = w[b, PARAM_ROWS : PARAM_ROWS + BLOCK_W, :].astype(F32)
        three = packed[:, 256:384]
        cols[rows, :] = three + pltpu.roll(three, 128 - 16, 1) + pltpu.roll(three, 128 - 32, 1)
        shaped_rows = lax.dot_general(
            packed[:, 0:128] + packed[:, 128:256],
            hidden[...],
            (((1,), (1,)), ((), ())),
            precision=HIGHEST,
            preferred_element_type=F32,
        )
        envelope = jnp.exp(-lag * cols[rows, DECAY : DECAY + 1])
        table = jnp.where(place == LENGTH, 0.0, shaped_rows * envelope * (1.0 / math.sqrt(LENGTH)))
        kspec[rows, :] = lax.dot_general(
            table, ahead_full[...], (((1,), (0,)), ((), ())), precision=HIGHEST, preferred_element_type=F32
        )


def fold_back(lines, wide, count):
    low = lanes_of((count // 2, 128)) < 64
    one, two, three = (lines[pl.ds(j, count // 2, stride=3), :] for j in range(3))
    three = pltpu.roll(three, 64, 1)
    wide[0, pl.ds(0, count // 2, stride=2), :] = one
    wide[1, pl.ds(0, count // 2, stride=2), :] = two
    wide[0, pl.ds(1, count // 2, stride=2), :] = jnp.where(low, pltpu.roll(two, 64, 1), three)
    wide[1, pl.ds(1, count // 2, stride=2), :] = three


def fold_out(wide, out, count):
    low = lanes_of((count // 2, 128)) < 64
    half = count // 2
    even_a = wide[0, pl.ds(0, half, stride=2), :]
    even_b = wide[1, pl.ds(0, half, stride=2), :]
    odd_a = pltpu.roll(wide[0, pl.ds(1, half, stride=2), :], 64, 1)
    odd_b = pltpu.roll(wide[1, pl.ds(1, half, stride=2), :], 64, 1)
    out[pl.ds(0, half, stride=3), :] = even_a
    out[pl.ds(1, half, stride=3), :] = jnp.where(low, even_b, odd_a)
    out[pl.ds(2, half, stride=3), :] = jnp.where(low, odd_a, odd_b)


def spread_lines(flat, layer, count, lanes, lines):
    rows = flat.shape[1]
    lines[0:rows, :] = flat[layer].astype(F32)
    return [lines[pl.ds(j, count, stride=lanes), :] for j in range(lanes)]


def narrow_lines(flat, layer, count, lines, wide):
    rows = flat.shape[1]
    lines[0:rows, :] = flat[layer].astype(F32)
    fold_back(lines, wide, count)
    return jnp.concatenate([wide[0, 0:count, :], wide[1, 0:count, 0:64]], axis=1).astype(BF16)


def own_piece(idx, table, out, layer):
    rows = out.shape[1]
    out[layer] = table[layer, pl.ds(pl.multiple_of(idx[1] * rows, 16), rows), :]


def pack_mix_kernel(idx, in_one, in_two, out_one, out_two, params, table, out, lines, wide):
    for layer in range(LAYERS):
        for flat, start, count in ((in_one, IN_ONE, 192), (in_two, IN_TWO, 384)):
            for j, part in enumerate(spread_lines(flat, layer, count, 3, lines)):
                table[layer, start : start + count, 128 * j : 128 * j + 128] = part.astype(BF16)
        table[layer, OUT_ROWS : OUT_ROWS + 192, 0:192] = narrow_lines(out_one, layer, 192, lines, wide)
        table[layer, OUT_ROWS : OUT_ROWS + 192, 192:384] = narrow_lines(out_two, layer, 192, lines, wide)
        last = params[layer, :, 128:256]
        high = last.astype(BF16)
        rows = slice(PARAM_ROWS, PARAM_ROWS + BLOCK_W)
        table[layer, rows, 0:128] = high
        table[layer, rows, 128:256] = (last - high.astype(F32)).astype(BF16)
        left = params[layer, :, 0:128]
        terms = jnp.zeros((BLOCK_W, 128), F32)
        for at in range(3):
            part = left.astype(BF16).astype(F32)
            left = left - part
            terms = terms + (pltpu.roll(part, 16 * at, 1) if at else part)
        table[layer, rows, 256:384] = terms.astype(BF16)
        table[layer, PARAM_ROWS + BLOCK_W : MIX_ROWS, :] = jnp.zeros((MIX_ROWS - PARAM_ROWS - BLOCK_W, 384), BF16)
        own_piece(idx, table, out, layer)


def pack_ff_kernel(idx, up_one, up_two, down_one, down_two, table, out, lines, wide):
    for layer in range(LAYERS):
        table[layer, UP_ONE : UP_ONE + 192, 0:192] = narrow_lines(up_one, layer, 192, lines, wide)
        table[layer, UP_ONE : UP_ONE + 192, 192:384] = narrow_lines(down_two, layer, 192, lines, wide)
        for j, part in enumerate(spread_lines(up_two, layer, 192, 12, lines)):
            at = UP_TWO + 192 * (j // 3)
            table[layer, at : at + 192, 128 * (j % 3) : 128 * (j % 3) + 128] = part.astype(BF16)
        down = narrow_lines(down_one, layer, 768, lines, wide)
        table[layer, DOWN_ONE : DOWN_ONE + 384, 0:192] = down[0:384]
        table[layer, DOWN_ONE : DOWN_ONE + 384, 192:384] = down[384:768]
        table[layer, FF_USED:FF_ROWS, :] = jnp.zeros((FF_ROWS - FF_USED, 384), BF16)
        own_piece(idx, table, out, layer)


def finish_kernel(idx, *refs):
    pieces = refs[: 2 * len(FINISH_ORDER)]
    refs = refs[2 * len(FINISH_ORDER) :]
    in_one, in_two, out_one, out_two, up_one, up_two, down_one, down_two, small = refs[:9]
    ff, conv, inp, wide, sem = refs[9:]
    tables = {"ff": ff, "conv": conv, "in": inp}
    pairs = []
    for at, group in enumerate(FINISH_ORDER):
        for core in range(2):
            rel = pieces[2 * at + core]
            first = 0
            for name in group:
                rows = PIECE_ROWS[name]
                for chip in range(4):
                    pairs.append(
                        (
                            rel.at[chip, pl.ds(first, rows), :],
                            tables[name].at[at, piece_rows(idx, core, chip, rows), :],
                        )
                    )
                first += rows
    run_copies(pairs, sem)

    def spread(out, layer, values, lanes, first):
        count = values.shape[0]
        for j in range(3):
            out[layer, pl.ds(first + j, count, stride=lanes), :] = values[:, 128 * j : 128 * j + 128].astype(F32)

    def narrow_of(out, layer, values):
        count = values.shape[0]
        wide[0, 0:count, :] = values[:, 0:128].astype(F32)
        wide[1, 0:count, 0:64] = values[:, 128:192].astype(F32)
        fold_out(wide, out.at[layer], count)

    for layer in range(LAYERS):
        spread(in_one, layer, inp[layer, IN_ONE : IN_ONE + 192, :], 3, 0)
        spread(in_two, layer, inp[layer, IN_TWO : IN_TWO + 384, :], 3, 0)
        for q in range(4):
            at = UP_TWO + 192 * q
            spread(up_two, layer, ff[layer, at : at + 192, :], 12, 3 * q)
        narrow_of(out_one, layer, conv[layer, 0:192, 0:192])
        narrow_of(out_two, layer, conv[layer, 0:192, 192:384])
        narrow_of(up_one, layer, ff[layer, UP_ONE : UP_ONE + 192, 0:192])
        narrow_of(down_two, layer, ff[layer, UP_ONE : UP_ONE + 192, 192:384])
        narrow_of(
            down_one,
            layer,
            jnp.concatenate(
                [ff[layer, DOWN_ONE : DOWN_ONE + 384, 0:192], ff[layer, DOWN_ONE : DOWN_ONE + 384, 192:384]], axis=0
            ),
        )
        small[layer, 0:16, 0:128] = conv[layer, 192:208, 256:384].astype(F32)
        small[layer, 0:16, 128:256] = conv[layer, 208:224, 256:384].astype(F32)
        small[layer, 16:32, 0:256] = inp[layer, 576:592, 0:256].astype(F32)


def join_kernel(first, idx, rel_a, rel_b, out, sem):
    rows = PIECE_ROWS["conv"]
    run_copies(
        [
            (rel.at[chip, pl.ds(first, rows), :], out.at[piece_rows(idx, core, chip, rows), :])
            for core, rel in enumerate((rel_a, rel_b))
            for chip in range(4)
        ],
        sem,
    )


ANY = pl.BlockSpec(memory_space=pl.ANY)
SCALARS = pl.BlockSpec(memory_space=pltpu.SMEM)
WHOLE = pl.BlockSpec(memory_space=pltpu.VMEM)


def shaped(dtype, *shape):
    return jax.ShapeDtypeStruct(shape, dtype)


def call(kernel, outs, scratch, in_specs, out_specs, micros, deps=()):
    count = len(in_specs)

    def body(*refs):
        kernel(*refs[:count], *refs[count + len(deps) :])

    made = pl.pallas_call(
        body,
        out_shape=outs,
        in_specs=list(in_specs) + [ANY] * len(deps),
        out_specs=out_specs,
        scratch_shapes=scratch,
        compiler_params=pltpu.CompilerParams(vmem_limit_bytes=56 << 20),
        cost_estimate=pl.CostEstimate(flops=int(micros * 1e9), bytes_accessed=1 << 20, transcendentals=0),
    )
    return lambda *arrays: made(*arrays, *deps)


def place_parts_kernel(idx, *refs):
    parts, out = refs[:BLOCKS], refs[BLOCKS]
    span = parts[0].shape[1]
    for k, part in enumerate(parts):
        out[:, pl.ds(pl.multiple_of(block_of(idx, k) * span, 128), span)] = part[...].astype(out.dtype)


def wide_shift(x, mask):
    return lax.ppermute(x, "wide", [(i, i ^ mask) for i in range(lax.axis_size("wide"))])


def narrow_shift(x, by):
    narrow = lax.axis_size("narrow")
    return lax.ppermute(x, "narrow", [(i, (i + by) % narrow) for i in range(narrow)])


def added(parts):
    return sum(p.astype(F32) for p in parts).astype(parts[0].dtype)


def after(x, *deps):
    return lax.optimization_barrier((x, deps))[0]


def exchange(parts):
    return [parts[0]] + [narrow_shift(parts[k], k) for k in range(1, BLOCKS)]


def over_blocks(piece):
    return jnp.stack([narrow_shift(piece, k) for k in range(1, BLOCKS)])


def over_chips(x):
    return jnp.stack([x] + [wide_shift(x, 2 * m) for m in range(1, 4)])


def reduce_core(table):
    return added([table[0], wide_shift(table[1], 1)])


def reduce_chips(half):
    total = added([half[0]] + [wide_shift(half[m], 2 * m) for m in range(1, 4)])
    groups = lax.axis_size("wide") // 8
    if groups > 1:
        total = added([total] + [wide_shift(total, 8 * g) for g in range(1, groups)])
    return total


def reduce_blocks(total):
    return added([total[0]] + [narrow_shift(total[k], -k) for k in range(1, BLOCKS)])


def join_rows(*tables):
    return jnp.concatenate(tables, axis=-2)


def filter_lags():
    place = jnp.arange(2 * LENGTH)
    return place, jnp.where(place < LENGTH, place, place - 2 * LENGTH).astype(F32)


def filter_hidden(weight_one, bias_one, weight_two):
    relative = filter_lags()[1] / LENGTH
    features = jnp.stack(
        [
            relative,
            jnp.cos(math.pi * relative),
            jnp.sin(math.pi * relative),
            jnp.cos(37.0 * math.pi * relative),
            jnp.sin(37.0 * math.pi * relative),
        ],
        axis=1,
    )
    hidden_one = jnp.sin(jnp.dot(features, weight_one, precision=HIGHEST) + bias_one)
    return jnp.sin(jnp.dot(hidden_one, weight_two, precision=HIGHEST))


def filter_table(weight_one, bias_one, weight_two, weight_three, decay_rate):
    place, lag = filter_lags()
    hidden_two = filter_hidden(weight_one, bias_one, weight_two)
    shaped_rows = lax.dot_general(
        weight_three, hidden_two, (((1,), (1,)), ((), ())), precision=HIGHEST, preferred_element_type=F32
    )
    envelope = jnp.exp(-jnp.abs(lag)[None, :] * decay_rate[:, None])
    return jnp.where(place[None, :] == LENGTH, 0.0, shaped_rows * envelope / math.sqrt(LENGTH))


def local(
    tokens,
    lengths,
    masked,
    cotangent,
    mask_vector,
    gain_one,
    in_first,
    in_second,
    short_taps,
    skip_gain,
    decay_rates,
    filter_one,
    filter_bias,
    filter_two,
    filter_three,
    out_first,
    out_second,
    gain_two,
    up_first,
    up_second,
    down_first,
    down_second,
):
    wide_count = lax.axis_size("wide")
    me = lax.axis_index("narrow")
    place = lax.axis_index("wide") & 7
    idx = jnp.stack([me, place]).astype(jnp.int32)
    seqs = lengths.shape[0] // BLOCKS
    span = seqs * LENGTH
    all_tokens = tokens.shape[1] * wide_count

    def token_parts(table):
        return [lax.dynamic_slice_in_dim(table, ((me + k) % BLOCKS) * span, span, 1) for k in range(BLOCKS)]

    def flat_lines(weight):
        return weight.reshape(LAYERS, weight.shape[2] // 128, 128)

    factors = [in_first, in_second, out_first, out_second, up_first, up_second, down_first, down_second]
    lines = [flat_lines(weight) for weight in factors]
    tokens_here = exchange(token_parts(tokens))

    columns = jnp.concatenate(
        [
            gain_one[:, None],
            gain_two[:, None],
            skip_gain[:, None],
            short_taps[:, :, 0, :BLOCK_W],
            short_taps[:, :, 0, BLOCK_W:],
            jnp.broadcast_to(mask_vector, (LAYERS, 1, BLOCK_W)),
            decay_rates[:, None],
            jnp.zeros((LAYERS, 5, BLOCK_W), F32),
        ],
        axis=1,
    )
    columns = jnp.pad(columns.transpose(0, 2, 1), ((0, 0), (0, 0), (0, 112)))
    params = jnp.concatenate([columns, filter_three], axis=2)

    def pack(kernel, count, rows, arrays, micros):
        return call(
            kernel,
            [shaped(BF16, LAYERS, rows, 384), shaped(BF16, LAYERS, rows // 8, 384)],
            [pltpu.VMEM((2304, 128), F32), pltpu.VMEM((2, 768, 128), F32)],
            [SCALARS] + [WHOLE] * count,
            [WHOLE] * 2,
            micros,
        )(idx, *arrays)

    mix, mix_piece = pack(pack_mix_kernel, 5, MIX_ROWS, lines[:4] + [params], 3)
    ff, ff_piece = pack(pack_ff_kernel, 4, FF_ROWS, lines[4:], 4)

    weights_mix, weights_ff = [None] * LAYERS, [None] * LAYERS
    previous = ()
    for layer in range(LAYERS):
        for own, piece, made in ((mix, mix_piece, weights_mix), (ff, ff_piece, weights_ff)):
            others = over_blocks(after(piece[layer], *previous))
            previous = (others,)
            chips = over_chips(others)
            made[layer] = (own[layer], chips, wide_shift(chips, 1))
    cotangent_here = exchange(token_parts(after(cotangent, *previous)))

    own_lengths = lax.dynamic_slice_in_dim(lengths, me * seqs, seqs, 0)
    own_masked = lax.dynamic_slice_in_dim(masked, me * seqs, seqs, 0)
    positions = jnp.arange(LENGTH, dtype=jnp.int32)
    pad = (positions[None, :] < own_lengths[:, None]).astype(F32).reshape(1, span)
    pad = jnp.broadcast_to(pad, (8, span))
    chosen = jnp.broadcast_to(own_masked.astype(F32).reshape(1, span), (8, span))

    ahead, back = spectrum_tables()
    ahead_low = jnp.asarray(ahead[:LENGTH]).astype(BF16)
    back_low = jnp.asarray(back[:, :LENGTH]).astype(BF16)
    ahead_full = jnp.asarray(ahead)
    hidden = [filter_hidden(filter_one[layer], filter_bias[layer], filter_two[layer]) for layer in range(LAYERS)]
    pulls = [
        jax.vjp(
            filter_table,
            filter_one[layer],
            filter_bias[layer],
            filter_two[layer],
            filter_three[layer],
            decay_rates[layer],
        )
        for layer in range(LAYERS)
    ]
    mix_scratch = pltpu.VMEM((BLOCKS, MIX_ROWS, 384), BF16)
    ff_scratch = pltpu.VMEM((BLOCKS, FF_ROWS, 384), BF16)
    fetched = pltpu.SemaphoreType.DMA((25,))
    sent = pltpu.SemaphoreType.DMA((32,))
    table_specs = [SCALARS, ANY, ANY, ANY]

    h = None
    saved = []
    for layer in range(LAYERS):
        first, last = layer == 0, layer == LAYERS - 1
        made = call(
            functools.partial(fwd_mix_kernel, first, seqs),
            ([shaped(F32, D, span)] if first else [])
            + [
                shaped(BF16, BLOCKS, 384, span),
                shaped(BF16, BLOCKS, 384, span),
                shaped(BF16, D, span),
                shaped(BF16, D, span),
                shaped(BF16, BLOCKS, 192, span),
                shaped(F32, D, span),
                shaped(F32, 8, span),
                shaped(F32, D, 128),
                shaped(F32, D, 256),
            ],
            [
                mix_scratch,
                pltpu.VMEM((D, span), BF16),
                pltpu.VMEM((BLOCK_W, span), F32),
                pltpu.VMEM((BLOCK_W, span), F32),
                fetched,
            ],
            table_specs + [WHOLE] * (BLOCKS + 1 if first else 1) + [WHOLE] * 5,
            [WHOLE] * (10 if first else 9),
            18,
        )(
            idx,
            *weights_mix[layer],
            *([*tokens_here, chosen] if first else [h]),
            pad,
            hidden[layer],
            ahead_full,
            ahead_low,
            back_low,
        )
        if first:
            h, *made = made
        q1, proj, conv, gated, q2, middle, stats_one, cols, kspec = made
        q3, gate_up, q4, h_next, stats_two = call(
            functools.partial(fwd_ff_kernel, last),
            [
                shaped(BF16, BLOCKS, 192, span),
                shaped(BF16, BLOCKS, 1536, span),
                shaped(BF16, BLOCKS, 192, span),
                shaped(BF16, BLOCKS, BLOCK_W, span) if last else shaped(F32, D, span),
                shaped(F32, 8, span),
            ],
            [ff_scratch, pltpu.VMEM((D, span), BF16), pltpu.VMEM((FF_BLOCK, span), BF16), fetched],
            table_specs + [WHOLE] * 2,
            [WHOLE] * 5,
            15,
        )(idx, *weights_ff[layer], middle, cols)
        saved.append((h, q1, proj, conv, gated, q2, middle, stats_one, cols, kspec, q3, gate_up, q4, stats_two))
        h = h_next

    def collect(parts, dtype):
        return call(
            place_parts_kernel,
            shaped(dtype, BLOCK_W, BLOCKS * span),
            [],
            [SCALARS] + [WHOLE] * BLOCKS,
            WHOLE,
            2,
        )(idx, *exchange([parts[k] for k in range(BLOCKS)]))

    mixed_out = collect(h, BF16)

    def back_ff(layer, g_top, deps):
        last = layer == LAYERS - 1
        h, q1, proj, conv, gated, q2, middle, stats_one, cols, kspec, q3, gate_up, q4, stats_two = saved[layer]
        return call(
            functools.partial(bwd_ff_kernel, last),
            [shaped(F32, D, span), shaped(BF16, 2, 4, BLOCKS, FF_ROWS // 8, 384), shaped(F32, BLOCKS, 16, BLOCK_W)],
            [
                ff_scratch,
                pltpu.VMEM((BLOCKS, FF_ROWS, 384), BF16),
                pltpu.VMEM((D, span), BF16),
                pltpu.VMEM((BLOCKS, 192, span), BF16),
                pltpu.VMEM((BLOCKS, 192, span), BF16),
                pltpu.VMEM((2 * FF_BLOCK, span), BF16),
                pltpu.VMEM((D, span), F32),
                sent,
            ],
            table_specs + [WHOLE] * (BLOCKS if last else 1) + [WHOLE] * 6,
            [WHOLE, ANY, WHOLE],
            27,
            deps,
        )(idx, *weights_ff[layer], *(g_top if last else [g_top]), q4, gate_up, q3, middle, stats_two, cols)

    def back_conv(layer, g_mid, small_ff, deps):
        h, q1, proj, conv, gated, q2, middle, stats_one, cols, kspec, q3, gate_up, q4, stats_two = saved[layer]
        return call(
            functools.partial(bwd_conv_kernel, seqs),
            [shaped(BF16, BLOCKS, 384, span), shaped(BF16, 2, 4, BLOCKS, 48, 384)],
            [
                mix_scratch,
                pltpu.VMEM((BLOCKS, 384, 384), BF16),
                pltpu.VMEM((BLOCKS, 192, span), BF16),
                pltpu.VMEM((BLOCK_W, span), F32),
                pltpu.VMEM((BLOCK_W, span), F32),
                sent,
            ],
            table_specs + [WHOLE] * 11,
            [WHOLE, ANY],
            23,
            deps,
        )(
            idx,
            *weights_mix[layer],
            g_mid,
            q2,
            gated,
            conv,
            proj,
            pad,
            cols,
            kspec,
            ahead_low,
            back_low,
            small_ff,
        )

    def back_in(layer, gv, g_mid, deps):
        first = layer == 0
        h, q1, proj, conv, gated, q2, middle, stats_one, cols, kspec, q3, gate_up, q4, stats_two = saved[layer]
        return call(
            functools.partial(bwd_in_kernel, first),
            [
                shaped(BF16, BLOCKS, BLOCK_W, span) if first else shaped(F32, D, span),
                shaped(BF16, 2, 4, BLOCKS, IN_GRAD_ROWS // 8, 384),
            ],
            [
                mix_scratch,
                pltpu.VMEM((BLOCKS, IN_GRAD_ROWS, 384), BF16),
                pltpu.VMEM((BLOCKS, 384, span), BF16),
                pltpu.VMEM((D, span), F32),
                pltpu.VMEM((BLOCKS, 16, BLOCK_W), F32),
                sent,
            ]
            + ([pltpu.VMEM((D, span), F32)] if first else []),
            table_specs + [WHOLE] * (7 if first else 6),
            [WHOLE, ANY],
            12,
            deps,
        )(idx, *weights_mix[layer], gv, g_mid, q1, h, stats_one, cols, *([chosen] if first else []))

    def spread(*tables):
        chips = over_chips(join_rows(*tables))
        return chips, wide_shift(chips, 1)

    g_mid, g_ff, small_ff = back_ff(1, cotangent_here, ())
    ff_one = reduce_core(g_ff)
    gv, g_conv = back_conv(1, g_mid, small_ff, ())
    conv_one = reduce_core(g_conv)
    g_top, g_in = back_in(1, gv, g_mid, (ff_one,))
    ff_one = reduce_chips(ff_one)
    in_one = reduce_core(g_in)

    g_mid, g_ff, small_ff = back_ff(0, g_top, (conv_one,))
    mix_one = join_rows(conv_one, in_one)
    ff_zero = reduce_core(g_ff)
    gv, g_conv = back_conv(0, g_mid, small_ff, (ff_one, mix_one))
    mix_one = reduce_chips(mix_one)
    ff_one = reduce_blocks(ff_one)
    conv_zero = reduce_core(g_conv)
    g_top, g_in = back_in(0, gv, g_mid, (ff_one, mix_one, ff_zero))
    grad_tokens = collect(g_top, F32)
    mix_one = reduce_blocks(mix_one)
    ff_zero = reduce_blocks(reduce_chips(ff_zero))
    mix_zero = reduce_blocks(reduce_chips(join_rows(conv_zero, reduce_core(g_in))))
    groups = [spread(ff_zero, mix_zero), spread(ff_one, mix_one)]

    filter_grads = []
    for layer in range(LAYERS):
        joined = call(
            functools.partial(join_kernel, PIECE_ROWS["ff"]),
            shaped(BF16, 384, 384),
            [pltpu.SemaphoreType.DMA((8,))],
            [SCALARS, ANY, ANY],
            WHOLE,
            2,
        )(idx, *groups[layer])
        g_kernel = jnp.dot(joined[192:384, 0:256].astype(F32), jnp.asarray(back), precision=HIGHEST)
        kernel, pull = pulls[layer]
        grads = pull(g_kernel + 4.0 * math.sqrt(all_tokens) * kernel)
        shared = jnp.concatenate([grads[2], grads[0], grads[1][None], jnp.zeros((2, 128), F32)], axis=0)
        shared = added([shared] + [narrow_shift(shared, k) for k in range(1, BLOCKS)])
        filter_grads.append((shared[128:133], shared[133], shared[0:128], grads[3], grads[4]))

    sizes = [weight.shape[2] // 128 for weight in factors]
    flat = call(
        finish_kernel,
        [shaped(F32, LAYERS, size, 128) for size in sizes] + [shaped(F32, LAYERS, 32, 256)],
        [
            pltpu.VMEM((LAYERS, FF_ROWS, 384), BF16),
            pltpu.VMEM((LAYERS, 384, 384), BF16),
            pltpu.VMEM((LAYERS, IN_GRAD_ROWS, 384), BF16),
            pltpu.VMEM((2, 768, 128), F32),
            pltpu.SemaphoreType.DMA((24 * LAYERS,)),
        ],
        [SCALARS] + [ANY] * (2 * LAYERS),
        [WHOLE] * 9,
        8,
    )(idx, *(part for group in groups for part in group))
    grads = [table.reshape(LAYERS, 1, table.shape[1] * 128) for table in flat[:8]]
    small = flat[8][:, :, :BLOCK_W]
    filt = [jnp.stack([filter_grads[layer][at] for layer in range(LAYERS)]) for at in range(5)]
    return (
        mixed_out,
        grad_tokens,
        small[0, 17],
        small[:, 16],
        grads[0],
        grads[1],
        jnp.concatenate([small[:, 3:6], small[:, 6:9]], axis=2)[:, :, None],
        small[:, 2],
        filt[4],
        filt[0],
        filt[1],
        filt[2],
        filt[3],
        grads[2],
        grads[3],
        small[:, 1],
        grads[4],
        grads[5],
        grads[6],
        grads[7],
    )


def solution(mesh):
    placed = (
        P("narrow", "wide"),
        P("wide"),
        P("wide", None),
        P("narrow", "wide"),
        P("narrow"),
        P(None, "narrow"),
        P(None, "narrow", None),
        P(None, "narrow", None),
        P(None, None, "narrow", None),
        P(None, "narrow"),
        P(None, "narrow"),
        P(),
        P(),
        P(),
        P(None, "narrow", None),
        P(None, "narrow", None),
        P(None, "narrow", None),
        P(None, "narrow"),
        P(None, "narrow", None),
        P(None, "narrow", None),
        P(None, "narrow", None),
        P(None, "narrow", None),
    )
    return jax.shard_map(
        local,
        mesh=mesh,
        in_specs=placed,
        out_specs=(
            P("narrow", "wide"),
            P("narrow", "wide"),
            P("narrow"),
            P(None, "narrow"),
            P(None, "narrow", None),
            P(None, "narrow", None),
            P(None, None, "narrow", None),
            P(None, "narrow"),
            P(None, "narrow"),
            P(),
            P(),
            P(),
            P(None, "narrow", None),
            P(None, "narrow", None),
            P(None, "narrow", None),
            P(None, "narrow"),
            P(None, "narrow", None),
            P(None, "narrow", None),
            P(None, "narrow", None),
            P(None, "narrow", None),
        ),
        check_vma=False,
    )
```

```python
import math
import functools
import numpy as np
import jax
import jax.numpy as jnp
from jax import lax
from jax.experimental import pallas as pl
from jax.experimental.pallas import tpu as pltpu
from jax.sharding import PartitionSpec as P

F32 = jnp.float32
BF16 = jnp.bfloat16
D = 768
LENGTH = 128
LAYERS = 2
BLOCK_W = 192
FF_BLOCK = 768
BLOCKS = 4
EPSILON = 1e-05
HIGHEST = lax.Precision.HIGHEST
GAIN_ONE, GAIN_TWO, SKIP, TAP_X, TAP_G, MASK, DECAY = 0, 1, 2, 3, 6, 9, 10
IN_ONE, IN_TWO, OUT_ROWS, PARAM_ROWS = 0, 192, 576, 768
UP_ONE, UP_TWO, DOWN_ONE = 0, 192, 960
MIX_ROWS, FF_USED, FF_ROWS, IN_GRAD_ROWS = 1024, 1344, 1408, 640
HIDDEN_ONE, HIDDEN_TWO, SLOPE_ONE, SLOPE_TWO = 0, 1, 2, 3
PIECE_ROWS = {"ff": 176, "conv": 48, "in": 80}


def nn(a, b):
    return lax.dot_general(a, b, (((1,), (0,)), ((), ())), preferred_element_type=F32)


def nt(a, b):
    return lax.dot_general(a, b, (((1,), (1,)), ((), ())), preferred_element_type=F32)


def tn(a, b):
    return lax.dot_general(a, b, (((0,), (0,)), ((), ())), preferred_element_type=F32)


def spectrum_tables():
    time = np.arange(2 * LENGTH)
    freq = np.arange(LENGTH)
    angle = 2.0 * np.pi * np.outer(time, freq) / (2 * LENGTH)
    ahead = np.concatenate([np.cos(angle), -np.sin(angle)], axis=1)
    ahead[:, LENGTH] = np.cos(np.pi * time)
    scale = np.full((2 * LENGTH,), 2.0 / (2 * LENGTH))
    scale[0] = scale[LENGTH] = 1.0 / (2 * LENGTH)
    return ahead.astype(np.float32), (ahead * scale[None, :]).T.astype(np.float32)


def lanes_of(shape):
    return lax.broadcasted_iota(jnp.int32, shape, 1)


def later(v, lane):
    return jnp.where(lane == 0, 0.0, pltpu.roll(v, 1, 1))


def earlier(v, lane):
    return jnp.where(lane == LENGTH - 1, 0.0, pltpu.roll(v, LENGTH - 1, 1))


def norm_rows(parts):
    total = sum(jnp.sum(p, axis=0, keepdims=True) for p in parts)
    squares = sum(jnp.sum(p * p, axis=0, keepdims=True) for p in parts)
    mean = total / D
    inv = lax.rsqrt(squares / D - mean * mean + EPSILON)
    return mean, inv


def block(ref, b, width=BLOCK_W):
    return ref[pl.ds(b * width, width), :]


def fwd_mix_kernel(first, seqs, *refs):
    idx, own, rel_a, rel_b, *refs = refs
    if first:
        *parts, chosen_ref = refs[: BLOCKS + 1]
        refs = refs[BLOCKS + 1 :]
    else:
        h_ref, *refs = refs
    pad, hidden, ahead_full, ahead, back, *refs = refs
    if first:
        h_ref, *refs = refs
    q1, proj, conv, gated, q2, middle, stats, cols, kspec, w, normed, xs, gs, sem = refs
    fetch_table(idx, own, rel_a, rel_b, w, sem)
    make_params(w, hidden, ahead_full, cols, kspec)
    if first:
        keep = chosen_ref[0:1, :]
        for k, part in enumerate(parts):
            rows = pl.ds(pl.multiple_of(block_of(idx, k) * BLOCK_W, BLOCK_W), BLOCK_W)
            h_ref[rows, :] = part[...].astype(F32) * (1.0 - keep) + keep * cols[rows, MASK : MASK + 1]
    mean, inv = norm_rows([block(h_ref, b) for b in range(BLOCKS)])
    stats[0:1, :] = mean
    stats[1:2, :] = inv
    for b in range(BLOCKS):
        rows = pl.ds(b * BLOCK_W, BLOCK_W)
        normed[rows, :] = ((h_ref[rows, :] - mean) * inv * cols[rows, GAIN_ONE : GAIN_ONE + 1]).astype(BF16)
    for b in range(BLOCKS):
        inner = tn(w[b, IN_ONE : IN_ONE + 192, :], block(normed, b)).astype(BF16)
        for c in range(BLOCKS):
            q1[c, 96 * b : 96 * b + 96, :] = inner[96 * c : 96 * c + 96]
    lane = lanes_of((BLOCK_W, LENGTH))
    row_lane = lanes_of((BLOCK_W, LENGTH))
    for c in range(BLOCKS):
        rows = pl.ds(c * BLOCK_W, BLOCK_W)
        value = tn(w[c, IN_TWO : IN_TWO + 384, :], q1[c]) * pad[0:1, :]
        proj[c] = value.astype(BF16)
        for s in range(seqs):
            here = slice(s * LENGTH, (s + 1) * LENGTH)
            for part, tap, out in ((0, TAP_X, xs), (192, TAP_G, gs)):
                v = value[part : part + 192, here]
                out[:, here] = (
                    cols[rows, tap : tap + 1] * later(v, lane)
                    + cols[rows, tap + 1 : tap + 2] * v
                    + cols[rows, tap + 2 : tap + 3] * earlier(v, lane)
                )
        signal = jnp.concatenate([xs[:, s * LENGTH : (s + 1) * LENGTH] for s in range(seqs)], axis=0)
        spec = nn(signal.astype(BF16), ahead[...])
        k_re = kspec[rows, 0:LENGTH]
        k_im = kspec[rows, LENGTH : 2 * LENGTH]
        k_off = jnp.where(row_lane == 0, 0.0, k_im)
        k_im = jnp.where(row_lane == 0, k_im, k_re)
        made = []
        for s in range(seqs):
            re = spec[s * 192 : s * 192 + 192, 0:LENGTH]
            im = spec[s * 192 : s * 192 + 192, LENGTH : 2 * LENGTH]
            made.append(
                jnp.concatenate([re * k_re - im * k_off, re * k_off + im * k_im], axis=1).astype(BF16)
            )
        y = nn(jnp.concatenate(made, axis=0), back[...])
        for s in range(seqs):
            here = slice(s * LENGTH, (s + 1) * LENGTH)
            value = y[s * 192 : s * 192 + 192] + cols[rows, SKIP : SKIP + 1] * xs[:, here]
            conv[rows, here] = value.astype(BF16)
            gated[rows, here] = (value * gs[:, here]).astype(BF16)
    for b in range(BLOCKS):
        inner = tn(w[b, OUT_ROWS : OUT_ROWS + 192, 0:192], block(gated, b)).astype(BF16)
        for c in range(BLOCKS):
            q2[c, 48 * b : 48 * b + 48, :] = inner[48 * c : 48 * c + 48]
    for c in range(BLOCKS):
        rows = pl.ds(c * BLOCK_W, BLOCK_W)
        middle[rows, :] = h_ref[rows, :] + tn(w[c, OUT_ROWS : OUT_ROWS + 192, 192:384], q2[c])


def gelu_parts(v):
    inner = math.sqrt(2.0 / math.pi) * (v + 0.044715 * (v * v * v))
    return jnp.tanh(inner)


def fwd_ff_kernel(last, idx, own, rel_a, rel_b, middle, cols, q3, gate_up, q4, h_next, stats, w, normed, act, sem):
    fetch_table(idx, own, rel_a, rel_b, w, sem)
    mean, inv = norm_rows([block(middle, b) for b in range(BLOCKS)])
    stats[0:1, :] = mean
    stats[1:2, :] = inv
    for b in range(BLOCKS):
        rows = pl.ds(b * BLOCK_W, BLOCK_W)
        normed[rows, :] = ((middle[rows, :] - mean) * inv * cols[rows, GAIN_TWO : GAIN_TWO + 1]).astype(BF16)
    for b in range(BLOCKS):
        inner = tn(w[b, UP_ONE : UP_ONE + 192, 0:192], block(normed, b)).astype(BF16)
        for c in range(BLOCKS):
            q3[c, 48 * b : 48 * b + 48, :] = inner[48 * c : 48 * c + 48]
    for c in range(BLOCKS):
        for half in range(2):
            ups = []
            for piece in (half, half + 2):
                ups.append(tn(w[c, UP_TWO + 192 * piece : UP_TWO + 192 * piece + 192, :], q3[c]))
            gate, up = ups
            gate_up[c, 384 * half : 384 * half + 384, :] = gate.astype(BF16)
            gate_up[c, 768 + 384 * half : 768 + 384 * half + 384, :] = up.astype(BF16)
            act[384 * half : 384 * half + 384, :] = (
                0.5 * gate * (1.0 + gelu_parts(gate)) * up
            ).astype(BF16)
        inner = (
            tn(w[c, DOWN_ONE : DOWN_ONE + 384, 0:192], act[0:384, :])
            + tn(w[c, DOWN_ONE : DOWN_ONE + 384, 192:384], act[384:768, :])
        ).astype(BF16)
        for to in range(BLOCKS):
            q4[to, 48 * c : 48 * c + 48, :] = inner[48 * to : 48 * to + 48]
    for c in range(BLOCKS):
        rows = pl.ds(c * BLOCK_W, BLOCK_W)
        value = middle[rows, :] + tn(w[c, UP_ONE : UP_ONE + 192, 192:384], q4[c])
        if last:
            h_next[c] = value.astype(BF16)
        else:
            h_next[rows, :] = value


def bwd_ff_kernel(last, idx, own, rel_a, rel_b, *refs):
    parts = refs[: BLOCKS if last else 1]
    q4, gate_up, q3, middle, stats, cols, g_mid, g_near, g_far, small, w, g_w, g_low, gi4, gi3, g_gu, g_n, sem = refs[len(parts) :]
    fetch_table(idx, own, rel_a, rel_b, w, sem)
    mean = stats[0:1, :]
    inv = stats[1:2, :]
    if last:
        for k, part in enumerate(parts):
            g_low[pl.ds(pl.multiple_of(block_of(idx, k) * BLOCK_W, BLOCK_W), BLOCK_W), :] = part[...]
        g_top = g_low
    else:
        (g_top,) = parts
        for c in range(BLOCKS):
            g_low[c * 192 : c * 192 + 192, :] = block(g_top, c).astype(BF16)
    for b in range(BLOCKS):
        g_w[b, FF_USED:FF_ROWS, :] = jnp.zeros((FF_ROWS - FF_USED, 384), BF16)
    for c in range(BLOCKS):
        gt = block(g_low, c)
        g_w[c, UP_ONE : UP_ONE + 192, 192:384] = nt(q4[c], gt).astype(BF16)
        gq = nn(w[c, UP_ONE : UP_ONE + 192, 192:384], gt).astype(BF16)
        for b in range(BLOCKS):
            gi4[b, 48 * c : 48 * c + 48, :] = gq[48 * b : 48 * b + 48]
    rate = math.sqrt(2.0 / math.pi)
    for b in range(BLOCKS):
        for half in range(2):
            span = slice(192 * half, 192 * half + 192)
            gate = gate_up[b, 384 * half : 384 * half + 384, :].astype(F32)
            up = gate_up[b, 768 + 384 * half : 768 + 384 * half + 384, :].astype(F32)
            ga = nn(w[b, DOWN_ONE : DOWN_ONE + 384, span], gi4[b])
            square = gate * gate
            t = jnp.tanh(rate * gate * (1.0 + 0.044715 * square))
            rise = 0.5 * (1.0 + t)
            gelu = gate * rise
            slope = rise + 0.5 * gelu_slope(gate, square, t, rate)
            act = (gelu * up).astype(BF16)
            g_w[b, DOWN_ONE : DOWN_ONE + 384, span] = nt(act, gi4[b]).astype(BF16)
            g_gu[384 * half : 384 * half + 384, :] = (ga * up * slope).astype(BF16)
            g_gu[768 + 384 * half : 768 + 384 * half + 384, :] = (ga * gelu).astype(BF16)
        gq = None
        for piece in range(4):
            rows = slice(UP_TWO + 192 * piece, UP_TWO + 192 * piece + 192)
            gg = g_gu[384 * piece : 384 * piece + 384, :]
            g_w[b, rows, :] = nt(q3[b], gg).astype(BF16)
            term = nn(w[b, rows, :], gg)
            gq = term if gq is None else gq + term
        gq = gq.astype(BF16)
        for to in range(BLOCKS):
            gi3[to, 48 * b : 48 * b + 48, :] = gq[48 * to : 48 * to + 48]
    norm_back(
        middle, mean, inv, cols, GAIN_TWO, w, slice(UP_ONE, UP_ONE + 192), slice(0, 192), gi3, g_n, g_w, small, 1, g_top, g_mid
    )
    send_pieces(g_w, (g_near, g_far), idx, sem)


def gelu_slope(gate, square, t, rate):
    return gate * (1.0 - t * t) * (rate * (1.0 + 3.0 * 0.044715 * square))


def row_sums(place, values):
    lanes = values.shape[1]
    part = values[:, 0:LENGTH]
    for at in range(LENGTH, lanes, LENGTH):
        part = part + values[:, at : at + LENGTH]
    high = part.astype(BF16)
    low = (part - high.astype(F32)).astype(BF16)
    pick = (lax.broadcasted_iota(jnp.int32, (16, LENGTH), 0) == place).astype(F32).astype(BF16)
    return nt(pick, high) + nt(pick, low)


def norm_back(h, mean, inv, cols, gain_at, w, w_rows, w_lanes, gi, g_n, g_w, small, place, g_in, g_out):
    plain = cross = 0.0
    for b in range(BLOCKS):
        rows = pl.ds(b * 192, 192)
        gain = cols[rows, gain_at : gain_at + 1]
        xh = (h[rows, :] - mean) * inv
        gn = nn(w[b, w_rows, w_lanes], gi[b])
        g_w[b, w_rows, w_lanes] = nt((xh * gain).astype(BF16), gi[b]).astype(BF16)
        gx = gn * xh
        small[b] = row_sums(place, gx)
        g_n[rows, :] = gn * gain
        plain = plain + jnp.sum(gn * gain, axis=0, keepdims=True)
        cross = cross + jnp.sum(gx * gain, axis=0, keepdims=True)
    plain = plain / D
    cross = cross / D
    for b in range(BLOCKS):
        rows = pl.ds(b * 192, 192)
        xh = (h[rows, :] - mean) * inv
        g_out[rows, :] = g_in[rows, :].astype(F32) + inv * (g_n[rows, :] - plain - xh * cross)


def bwd_conv_kernel(
    seqs, penalty, idx, own, rel_a, rel_b, g_mid, q2, gated, conv, proj, pad, cols, kspec, ahead, back, small_ff,
    filt, weight_two, features, back_full, gv, g_near, g_far, w, g_w, gi2, gcs, xs, sem
):
    fetch_table(idx, own, rel_a, rel_b, w, sem)
    for c in range(BLOCKS):
        gt = block(g_mid, c).astype(BF16)
        g_w[c, 0:192, 192:384] = nt(q2[c], gt).astype(BF16)
        gq = nn(w[c, OUT_ROWS : OUT_ROWS + 192, 192:384], gt).astype(BF16)
        for b in range(BLOCKS):
            gi2[b, 48 * c : 48 * c + 48, :] = gq[48 * b : 48 * b + 48]
    lane = lanes_of((BLOCK_W, LENGTH))
    first_lane = lane == 0
    for b in range(BLOCKS):
        rows = pl.ds(b * 192, 192)
        g_gated = nn(w[b, OUT_ROWS : OUT_ROWS + 192, 0:192], gi2[b])
        g_w[b, 0:192, 0:192] = nt(block(gated, b), gi2[b]).astype(BF16)
        sums = [0.0] * 7
        for s in range(seqs):
            here = slice(s * LENGTH, (s + 1) * LENGTH)
            v = proj[b, 0:192, here].astype(F32)
            xs[:, here] = (
                cols[rows, TAP_X : TAP_X + 1] * later(v, lane)
                + cols[rows, TAP_X + 1 : TAP_X + 2] * v
                + cols[rows, TAP_X + 2 : TAP_X + 3] * earlier(v, lane)
            )
            v = proj[b, 192:384, here].astype(F32)
            after, before = later(v, lane), earlier(v, lane)
            gate = (
                cols[rows, TAP_G : TAP_G + 1] * after
                + cols[rows, TAP_G + 1 : TAP_G + 2] * v
                + cols[rows, TAP_G + 2 : TAP_G + 3] * before
            )
            gg = g_gated[:, here]
            gcs[:, here] = gg * gate
            z = gg * conv[rows, here].astype(F32)
            sums[4] = sums[4] + z * after
            sums[5] = sums[5] + z * v
            sums[6] = sums[6] + z * before
            gv[b, 192:384, here] = (
                (
                    cols[rows, TAP_G : TAP_G + 1] * earlier(z, lane)
                    + cols[rows, TAP_G + 1 : TAP_G + 2] * z
                    + cols[rows, TAP_G + 2 : TAP_G + 3] * later(z, lane)
                )
                * pad[0:1, here]
            ).astype(BF16)
            sums[0] = sums[0] + gcs[:, here] * xs[:, here]
        stacked = jnp.concatenate(
            [ref[:, s * LENGTH : (s + 1) * LENGTH] for ref in (xs, gcs) for s in range(seqs)], axis=0
        )
        spec = nn(stacked.astype(BF16), ahead[...])
        k_re = kspec[rows, 0:LENGTH]
        k_im = kspec[rows, LENGTH : 2 * LENGTH]
        k_off = jnp.where(first_lane, 0.0, k_im)
        k_im = jnp.where(first_lane, k_im, k_re)
        made = []
        p_re = p_im = p_off = 0.0
        for s in range(seqs):
            x_re = spec[s * 192 : s * 192 + 192, 0:LENGTH]
            x_im = spec[s * 192 : s * 192 + 192, LENGTH : 2 * LENGTH]
            at = (seqs + s) * 192
            g_re = spec[at : at + 192, 0:LENGTH]
            g_im = spec[at : at + 192, LENGTH : 2 * LENGTH]
            p_re = p_re + g_re * x_re
            p_im = p_im + g_im * x_im
            p_off = p_off + (g_im * x_re - g_re * x_im)
            made.append(
                jnp.concatenate([g_re * k_re + g_im * k_off, g_im * k_im - g_re * k_off], axis=1).astype(BF16)
            )
        g_table = exact(
            jnp.concatenate(
                [jnp.where(first_lane, p_re, p_re + p_im), jnp.where(first_lane, p_im, p_off)], axis=1
            ),
            back_full[...],
            1,
            0,
        )
        last, envelope, table = filter_values(w, b, cols, filt[HIDDEN_TWO])
        g_table = g_table + penalty * table
        g_decay = -(g_table * table * filter_lag())
        g_shape = g_table * envelope
        g_w[b, 192:384, 0:128] = exact(g_shape, filt[HIDDEN_TWO], 1, 0).astype(BF16)
        term = exact(g_shape, last, 0, 0)
        g_hidden = term if b == 0 else g_hidden + term
        y = nn(jnp.concatenate(made, axis=0), back[...])
        for s in range(seqs):
            here = slice(s * LENGTH, (s + 1) * LENGTH)
            z = y[s * 192 : s * 192 + 192] + cols[rows, SKIP : SKIP + 1] * gcs[:, here]
            v = proj[b, 0:192, here].astype(F32)
            sums[1] = sums[1] + z * later(v, lane)
            sums[2] = sums[2] + z * v
            sums[3] = sums[3] + z * earlier(v, lane)
            gv[b, 0:192, here] = (
                (
                    cols[rows, TAP_X : TAP_X + 1] * earlier(z, lane)
                    + cols[rows, TAP_X + 1 : TAP_X + 2] * z
                    + cols[rows, TAP_X + 2 : TAP_X + 3] * later(z, lane)
                )
                * pad[0:1, here]
            ).astype(BF16)
        table = small_ff[b]
        for at, value in enumerate(sums + [g_decay]):
            table = table + row_sums(2 + at, value)
        table = table.astype(BF16)
        g_w[b, 192:208, 256:384] = table[:, 0:128]
        g_w[b, 208:224, 256:320] = table[:, 128:192]
        g_w[b, 208:224, 320:384] = jnp.zeros((16, 64), BF16)
        g_w[b, 224:384, 256:384] = jnp.zeros((160, 128), BF16)
    g_two = g_hidden * filt[SLOPE_TWO]
    g_one = exact(g_two, weight_two[...], 1, 1) * filt[SLOPE_ONE]
    g_weight_two = exact(filt[HIDDEN_ONE], g_two, 0, 0).astype(BF16)
    g_weight_one = exact(features[...], g_one, 0, 0)[0:16, :].astype(BF16)
    for b in range(BLOCKS):
        g_w[b, 192:320, 128:256] = g_weight_two
        g_w[b, 320:336, 128:256] = g_weight_one
        g_w[b, 336:384, 128:256] = jnp.zeros((48, 128), BF16)
    send_pieces(g_w, (g_near, g_far), idx, sem)


def bwd_in_kernel(first, *refs):
    refs = list(refs)
    idx, own, rel_a, rel_b, gv, g_mid, q1, h, stats, cols = refs[:10]
    refs = refs[10:]
    chosen = refs.pop(0) if first else None
    g_out, g_near, g_far, w, g_w, gi1, g_n, small, sem = refs[:9]
    g_h = refs[9] if first else g_out
    fetch_table(idx, own, rel_a, rel_b, w, sem)
    mean = stats[0:1, :]
    inv = stats[1:2, :]
    for c in range(BLOCKS):
        g_w[c, IN_TWO : IN_TWO + 384, :] = nt(q1[c], gv[c]).astype(BF16)
        gq = nn(w[c, IN_TWO : IN_TWO + 384, :], gv[c]).astype(BF16)
        for b in range(BLOCKS):
            gi1[b, 96 * c : 96 * c + 96, :] = gq[96 * b : 96 * b + 96]
    norm_back(
        h, mean, inv, cols, GAIN_ONE, w, slice(IN_ONE, IN_ONE + 192), slice(0, 384), gi1, g_n, g_w, small, 0, g_mid, g_h
    )
    for b in range(BLOCKS):
        rows = pl.ds(b * 192, 192)
        table = small[b]
        if first:
            value = g_h[rows, :]
            masked = value * chosen[0:1, :]
            table = table + row_sums(1, masked)
            g_out[b] = (value - masked).astype(BF16)
        g_w[b, 576:592, 0:192] = table.astype(BF16)
        g_w[b, 576:592, 192:384] = jnp.zeros((16, 192), BF16)
        g_w[b, 592:640, :] = jnp.zeros((48, 384), BF16)
    send_pieces(g_w, (g_near, g_far), idx, sem)


def piece_rows(idx, core, chip, rows):
    return pl.ds(pl.multiple_of((idx[1] ^ (2 * chip + core)) * rows, 16), rows)


def block_of(idx, k):
    return (idx[0] - k) & (BLOCKS - 1)


def run_copies(pairs, sem):
    copies = [pltpu.make_async_copy(source, target, sem.at[at]) for at, (source, target) in enumerate(pairs)]
    for copy in copies:
        copy.start()
    for copy in copies:
        copy.wait()


def send_pieces(table, outs, idx, sem):
    rows = outs[0].shape[2]
    run_copies(
        [
            (table.at[block_of(idx, k), piece_rows(idx, core, chip, rows), :], outs[core].at[chip, k])
            for core in range(2)
            for chip in range(4)
            for k in range(BLOCKS)
        ],
        sem,
    )


def fetch_table(idx, own, rel_a, rel_b, table, sem):
    rows = rel_a.shape[2]
    run_copies(
        [(own, table.at[idx[0]])]
        + [
            (rel.at[chip, k - 1], table.at[block_of(idx, k), piece_rows(idx, core, chip, rows), :])
            for core, rel in enumerate((rel_a, rel_b))
            for chip in range(4)
            for k in range(1, BLOCKS)
        ],
        sem,
    )


def exact(a, b, left, right):
    return lax.dot_general(
        a, b, (((left,), (right,)), ((), ())), precision=HIGHEST, preferred_element_type=F32
    )


def filter_lag():
    place = lanes_of((BLOCK_W, 2 * LENGTH))
    return jnp.where(place < LENGTH, place, 2 * LENGTH - place).astype(F32)


def filter_values(w, b, cols, hidden):
    packed = w[b, PARAM_ROWS : PARAM_ROWS + BLOCK_W, 0:256].astype(F32)
    last = packed[:, 0:128] + packed[:, 128:256]
    lag = filter_lag()
    envelope = jnp.exp(-lag * cols[b * BLOCK_W : (b + 1) * BLOCK_W, DECAY : DECAY + 1]) * (1.0 / math.sqrt(LENGTH))
    envelope = jnp.where(lag == LENGTH, 0.0, envelope)
    return last, envelope, exact(last, hidden, 1, 1) * envelope


def make_params(w, hidden, ahead_full, cols, kspec):
    for b in range(BLOCKS):
        rows = pl.ds(b * BLOCK_W, BLOCK_W)
        three = w[b, PARAM_ROWS : PARAM_ROWS + BLOCK_W, 256:384].astype(F32)
        cols[rows, :] = three + pltpu.roll(three, 128 - 16, 1) + pltpu.roll(three, 128 - 32, 1)
        kspec[rows, :] = exact(filter_values(w, b, cols, hidden[HIDDEN_TWO])[2], ahead_full[...], 1, 0)


def fold_back(lines, wide, count):
    low = lanes_of((count // 2, 128)) < 64
    one, two, three = (lines[pl.ds(j, count // 2, stride=3), :] for j in range(3))
    three = pltpu.roll(three, 64, 1)
    wide[0, pl.ds(0, count // 2, stride=2), :] = one
    wide[1, pl.ds(0, count // 2, stride=2), :] = two
    wide[0, pl.ds(1, count // 2, stride=2), :] = jnp.where(low, pltpu.roll(two, 64, 1), three)
    wide[1, pl.ds(1, count // 2, stride=2), :] = three


def fold_out(wide, out, count):
    low = lanes_of((count // 2, 128)) < 64
    half = count // 2
    even_a = wide[0, pl.ds(0, half, stride=2), :]
    even_b = wide[1, pl.ds(0, half, stride=2), :]
    odd_a = pltpu.roll(wide[0, pl.ds(1, half, stride=2), :], 64, 1)
    odd_b = pltpu.roll(wide[1, pl.ds(1, half, stride=2), :], 64, 1)
    out[pl.ds(0, half, stride=3), :] = even_a
    out[pl.ds(1, half, stride=3), :] = jnp.where(low, even_b, odd_a)
    out[pl.ds(2, half, stride=3), :] = jnp.where(low, odd_a, odd_b)


def spread_lines(flat, layer, count, lanes, lines):
    rows = flat.shape[1]
    lines[0:rows, :] = flat[layer].astype(F32)
    return [lines[pl.ds(j, count, stride=lanes), :] for j in range(lanes)]


def narrow_lines(flat, layer, count, lines, wide):
    rows = flat.shape[1]
    lines[0:rows, :] = flat[layer].astype(F32)
    fold_back(lines, wide, count)
    return jnp.concatenate([wide[0, 0:count, :], wide[1, 0:count, 0:64]], axis=1).astype(BF16)


def own_piece(idx, table, out):
    rows = out.shape[0]
    out[...] = table[pl.ds(pl.multiple_of(idx[1] * rows, 16), rows), :]


def pack_mix_kernel(
    idx, in_one, in_two, out_one, out_two, gain_one, gain_two, skip, taps, mask, decay, filter_three,
    table_a, table_b, piece_a, piece_b, lines, wide, cols,
):
    tables, pieces = (table_a, table_b), (piece_a, piece_b)
    eye = (
        lax.broadcasted_iota(jnp.int32, (16, 128), 0) == lax.broadcasted_iota(jnp.int32, (16, 128), 1)
    ).astype(F32)
    cols[...] = jnp.zeros((16, BLOCK_W), F32)
    for layer in range(LAYERS):
        table = tables[layer]
        for flat, start, count in ((in_one, IN_ONE, 192), (in_two, IN_TWO, 384)):
            for j, part in enumerate(spread_lines(flat, layer, count, 3, lines)):
                table[start : start + count, 128 * j : 128 * j + 128] = part.astype(BF16)
        table[OUT_ROWS : OUT_ROWS + 192, 0:192] = narrow_lines(out_one, layer, 192, lines, wide)
        table[OUT_ROWS : OUT_ROWS + 192, 192:384] = narrow_lines(out_two, layer, 192, lines, wide)
        last = filter_three[layer]
        high = last.astype(BF16)
        rows = slice(PARAM_ROWS, PARAM_ROWS + BLOCK_W)
        table[rows, 0:128] = high
        table[rows, 128:256] = (last - high.astype(F32)).astype(BF16)
        for at, source in ((GAIN_ONE, gain_one), (GAIN_TWO, gain_two), (SKIP, skip), (DECAY, decay)):
            cols[at : at + 1, :] = source[layer : layer + 1, :]
        cols[TAP_X : TAP_X + 3, :] = taps[layer, :, 0:BLOCK_W]
        cols[TAP_G : TAP_G + 3, :] = taps[layer, :, BLOCK_W : 2 * BLOCK_W]
        cols[MASK : MASK + 1, :] = mask[...]
        left = lax.dot_general(
            cols[...], eye, (((0,), (0,)), ((), ())), precision=HIGHEST, preferred_element_type=F32
        )
        terms = jnp.zeros((BLOCK_W, 128), F32)
        for at in range(3):
            part = left.astype(BF16).astype(F32)
            left = left - part
            terms = terms + (pltpu.roll(part, 16 * at, 1) if at else part)
        table[rows, 256:384] = terms.astype(BF16)
        table[PARAM_ROWS + BLOCK_W : MIX_ROWS, :] = jnp.zeros((MIX_ROWS - PARAM_ROWS - BLOCK_W, 384), BF16)
        own_piece(idx, table, pieces[layer])


def pack_ff_kernel(idx, up_one, up_two, down_one, down_two, table_a, table_b, piece_a, piece_b, lines, wide):
    tables, pieces = (table_a, table_b), (piece_a, piece_b)
    for layer in range(LAYERS):
        table = tables[layer]
        table[UP_ONE : UP_ONE + 192, 0:192] = narrow_lines(up_one, layer, 192, lines, wide)
        table[UP_ONE : UP_ONE + 192, 192:384] = narrow_lines(down_two, layer, 192, lines, wide)
        for j, part in enumerate(spread_lines(up_two, layer, 192, 12, lines)):
            at = UP_TWO + 192 * (j // 3)
            table[at : at + 192, 128 * (j % 3) : 128 * (j % 3) + 128] = part.astype(BF16)
        down = narrow_lines(down_one, layer, 768, lines, wide)
        table[DOWN_ONE : DOWN_ONE + 384, 0:192] = down[0:384]
        table[DOWN_ONE : DOWN_ONE + 384, 192:384] = down[384:768]
        table[FF_USED:FF_ROWS, :] = jnp.zeros((FF_ROWS - FF_USED, 384), BF16)
        own_piece(idx, table, pieces[layer])


def finish_kernel(layer, idx, *refs):
    pieces, refs = refs[:2], refs[2:]
    if layer == 0:
        other, refs = refs[9], refs[10:]
    in_one, in_two, out_one, out_two, up_one, up_two, down_one, down_two, three = refs[:9]
    rest, (ff, conv, inp, wide, sem) = refs[9:-5], refs[-5:]
    pairs = []
    for core, rel in enumerate(pieces):
        first = 0
        for name, table in (("ff", ff), ("conv", conv), ("in", inp)):
            rows = PIECE_ROWS[name]
            for chip in range(4):
                pairs.append((rel.at[chip, pl.ds(first, rows), :], table.at[piece_rows(idx, core, chip, rows), :]))
            first += rows
    run_copies(pairs, sem)

    def spread(out, values, lanes, first):
        count = values.shape[0]
        for j in range(3):
            out[pl.ds(first + j, count, stride=lanes), :] = values[:, 128 * j : 128 * j + 128].astype(F32)

    def narrow_of(out, values):
        count = values.shape[0]
        wide[0, 0:count, :] = values[:, 0:128].astype(F32)
        wide[1, 0:count, 0:64] = values[:, 128:192].astype(F32)
        fold_out(wide, out, count)

    spread(in_one, inp[IN_ONE : IN_ONE + 192, :], 3, 0)
    spread(in_two, inp[IN_TWO : IN_TWO + 384, :], 3, 0)
    for q in range(4):
        at = UP_TWO + 192 * q
        spread(up_two, ff[at : at + 192, :], 12, 3 * q)
    narrow_of(out_one, conv[0:192, 0:192])
    narrow_of(out_two, conv[0:192, 192:384])
    narrow_of(up_one, ff[UP_ONE : UP_ONE + 192, 0:192])
    narrow_of(down_two, ff[UP_ONE : UP_ONE + 192, 192:384])
    narrow_of(
        down_one,
        jnp.concatenate([ff[DOWN_ONE : DOWN_ONE + 384, 0:192], ff[DOWN_ONE : DOWN_ONE + 384, 192:384]], axis=0),
    )
    three[...] = conv[192:384, 0:128].astype(F32)
    if layer > 0:
        rest[0][0:192, :] = conv[192:384, 128:384].astype(F32)
        rest[0][192:208, :] = inp[576:592, 0:256].astype(F32)
        return
    g_gain_one, g_gain_two, g_skip, g_taps, g_decay, g_mask, g_one, g_bias, g_two = rest
    for at in range(LAYERS):
        if at:
            shared, small, last = other[0:192, 0:128], other[0:32, 128:256], other[192:208, 0:192]
        else:
            shared = conv[192:384, 128:256].astype(F32)
            small = conv[192:224, 256:384].astype(F32)
            last = inp[576:592, 0:192].astype(F32)
        small = jnp.concatenate([small[0:16], small[16:32, 0:64]], axis=1)
        here = slice(at, at + 1)
        g_gain_one[here, :] = last[0:1]
        g_gain_two[here, :] = small[1:2]
        g_skip[here, :] = small[2:3]
        g_taps[at, :, 0:192] = small[3:6]
        g_taps[at, :, 192:384] = small[6:9]
        g_decay[here, :] = small[9:10]
        g_two[at] = shared[0:128]
        g_one[at] = shared[128:133]
        g_bias[here, :] = shared[133:134]
        if at == 0:
            g_mask[...] = last[1:2]


ANY = pl.BlockSpec(memory_space=pl.ANY)
SCALARS = pl.BlockSpec(memory_space=pltpu.SMEM)
WHOLE = pl.BlockSpec(memory_space=pltpu.VMEM)


def shaped(dtype, *shape):
    return jax.ShapeDtypeStruct(shape, dtype)


def call(kernel, outs, scratch, in_specs, out_specs, micros, deps=(), aliases=None):
    count = len(in_specs)

    def body(*refs):
        kernel(*refs[:count], *refs[count + len(deps) :])

    made = pl.pallas_call(
        body,
        out_shape=outs,
        in_specs=list(in_specs) + [ANY] * len(deps),
        out_specs=out_specs,
        scratch_shapes=scratch,
        input_output_aliases=aliases or {},
        compiler_params=pltpu.CompilerParams(vmem_limit_bytes=56 << 20),
        cost_estimate=pl.CostEstimate(flops=int(micros * 1e9), bytes_accessed=1 << 20, transcendentals=0),
    )
    return lambda *arrays: made(*arrays, *deps)


def place_parts_kernel(table, out):
    span = table.shape[2]
    for b in range(BLOCKS):
        out[:, b * span : (b + 1) * span] = table[b].astype(out.dtype)


def wide_shift(x, mask):
    return lax.ppermute(x, "wide", [(i, i ^ mask) for i in range(lax.axis_size("wide"))])


def narrow_shift(x, by):
    narrow = lax.axis_size("narrow")
    return lax.ppermute(x, "narrow", [(i, (i + by) % narrow) for i in range(narrow)])


def added(parts):
    return sum(p.astype(F32) for p in parts).astype(parts[0].dtype)


def after(x, *deps):
    return lax.optimization_barrier((x, deps))[0]


def settle(*trees):
    return lax.optimization_barrier(trees)


def exchange(parts):
    return [parts[0]] + [narrow_shift(parts[k], k) for k in range(1, BLOCKS)]


def over_blocks(piece):
    return jnp.stack([narrow_shift(piece, k) for k in range(1, BLOCKS)])


def others_at_once(piece, me):
    moved = lax.all_to_all(jnp.stack([piece] * BLOCKS), "narrow", split_axis=0, concat_axis=0, tiled=True)
    return jnp.stack([lax.dynamic_index_in_dim(moved, (me - k) % BLOCKS, 0, keepdims=False) for k in range(1, BLOCKS)])


def over_chips(x):
    return jnp.stack([x] + [wide_shift(x, 2 * m) for m in range(1, 4)])


def reduce_core(near, far):
    moved = wide_shift(far, 1)
    return [added([near[m], moved[m]]) for m in range(4)]


def move_chips(half):
    return [half[0]] + [wide_shift(half[m], 2 * m) for m in range(1, 4)]


def add_chips(parts):
    total = [added([part[k] for part in parts]) for k in range(BLOCKS)]
    groups = lax.axis_size("wide") // 8
    if groups > 1:
        total = [added([t] + [wide_shift(t, 8 * g) for g in range(1, groups)]) for t in total]
    return total


def reduce_blocks(total):
    return added([total[0]] + [narrow_shift(total[k], -k) for k in range(1, BLOCKS)])


def blocks_at_once(total, me):
    table = jnp.stack(total)
    table = jnp.stack([lax.dynamic_index_in_dim(table, (me - b) % BLOCKS, 0, keepdims=False) for b in range(BLOCKS)])
    moved = lax.all_to_all(table, "narrow", split_axis=0, concat_axis=0, tiled=True)
    return [moved[b] for b in range(BLOCKS)]


def join_rows(*tables):
    return [jnp.concatenate(parts, axis=-2) for parts in zip(*tables)]


def filter_features():
    place = np.arange(2 * LENGTH)
    relative = np.where(place < LENGTH, place, place - 2 * LENGTH) / LENGTH
    table = np.zeros((2 * LENGTH, 128))
    for at, value in enumerate(
        (
            relative,
            np.cos(np.pi * relative),
            np.sin(np.pi * relative),
            np.cos(37.0 * np.pi * relative),
            np.sin(37.0 * np.pi * relative),
            np.ones_like(relative),
        )
    ):
        table[:, at] = value
    return jnp.asarray(table.astype(np.float32))


def filter_hidden(features, weight_one, bias_one, weight_two):
    one = jnp.dot(features[:, :5], weight_one, precision=HIGHEST) + bias_one
    hidden_one = jnp.sin(one)
    two = jnp.dot(hidden_one, weight_two, precision=HIGHEST)
    return jnp.stack([hidden_one, jnp.sin(two), jnp.cos(one), jnp.cos(two)])


def local(
    tokens,
    lengths,
    masked,
    cotangent,
    mask_vector,
    gain_one,
    in_first,
    in_second,
    short_taps,
    skip_gain,
    decay_rates,
    filter_one,
    filter_bias,
    filter_two,
    filter_three,
    out_first,
    out_second,
    gain_two,
    up_first,
    up_second,
    down_first,
    down_second,
):
    wide_count = lax.axis_size("wide")
    me = lax.axis_index("narrow")
    place = lax.axis_index("wide") & 7
    idx = jnp.stack([me, place]).astype(jnp.int32)
    seqs = lengths.shape[0] // BLOCKS
    span = seqs * LENGTH
    all_tokens = tokens.shape[1] * wide_count

    def token_parts(table):
        return [lax.dynamic_slice_in_dim(table, ((me + k) % BLOCKS) * span, span, 1) for k in range(BLOCKS)]

    def flat_lines(weight):
        return weight.reshape(LAYERS, weight.shape[2] // 128, 128)

    factors = [in_first, in_second, out_first, out_second, up_first, up_second, down_first, down_second]
    lines = [flat_lines(weight) for weight in factors]
    tokens_here = exchange(token_parts(tokens))

    def pack(kernel, rows, arrays, deps=(), scratch=()):
        return call(
            kernel,
            [shaped(BF16, rows, 384)] * LAYERS + [shaped(BF16, rows // 8, 384)] * LAYERS,
            [pltpu.VMEM((2304, 128), F32), pltpu.VMEM((2, 768, 128), F32)] + list(scratch),
            [SCALARS] + [WHOLE] * len(arrays),
            [WHOLE] * (2 * LAYERS),
            3,
            deps,
        )(idx, *arrays)

    per_feature = [gain_one, gain_two, skip_gain, short_taps[:, :, 0], mask_vector[None], decay_rates, filter_three]
    *mix, mix_zero, mix_one = pack(
        pack_mix_kernel, MIX_ROWS, lines[:4] + per_feature, scratch=[pltpu.VMEM((16, BLOCK_W), F32)]
    )
    *ff, ff_zero, ff_one = pack(pack_ff_kernel, FF_ROWS, lines[4:], (mix_zero,))

    parts = token_parts(tokens)
    near, across, far = (narrow_shift(parts[k], k) for k in range(1, BLOCKS))
    mix_zero = over_blocks(mix_zero)
    ff_zero = over_blocks(after(ff_zero, mix_zero))
    mix_chips = over_chips(after(mix_zero, near))
    mix_chips, ff_zero, across, far = settle(mix_chips, ff_zero, across, far)
    mix_zero = (mix[0], mix_chips, wide_shift(mix_chips, 1))
    tokens_here = [parts[0], near, across, far]
    mix_zero, tokens_here, ff_zero, mix_one = settle(mix_zero, tokens_here, ff_zero, mix_one)
    ff_chips = over_chips(ff_zero)
    mix_one = others_at_once(mix_one, me)

    own_lengths = lax.dynamic_slice_in_dim(lengths, me * seqs, seqs, 0)
    own_masked = lax.dynamic_slice_in_dim(masked, me * seqs, seqs, 0)
    positions = jnp.arange(LENGTH, dtype=jnp.int32)
    pad = (positions[None, :] < own_lengths[:, None]).astype(F32).reshape(1, span)
    pad = jnp.broadcast_to(pad, (8, span))
    chosen = jnp.broadcast_to(own_masked.astype(F32).reshape(1, span), (8, span))

    ahead, back = spectrum_tables()
    ahead_low = jnp.asarray(ahead[:LENGTH]).astype(BF16)
    back_low = jnp.asarray(back[:, :LENGTH]).astype(BF16)
    ahead_full = jnp.asarray(ahead)
    features = filter_features()
    back_full = jnp.asarray(back)
    hidden = [
        filter_hidden(features, filter_one[layer], filter_bias[layer], filter_two[layer]) for layer in range(LAYERS)
    ]
    penalty = 4.0 * math.sqrt(all_tokens) / (wide_count * BLOCKS)
    mix_scratch = pltpu.VMEM((BLOCKS, MIX_ROWS, 384), BF16)
    ff_scratch = pltpu.VMEM((BLOCKS, FF_ROWS, 384), BF16)
    fetched = pltpu.SemaphoreType.DMA((25,))
    sent = pltpu.SemaphoreType.DMA((32,))
    table_specs = [SCALARS, ANY, ANY, ANY]

    def ahead_mix(layer, table, h, deps=()):
        first = layer == 0
        return call(
            functools.partial(fwd_mix_kernel, first, seqs),
            ([shaped(F32, D, span)] if first else [])
            + [
                shaped(BF16, BLOCKS, 384, span),
                shaped(BF16, BLOCKS, 384, span),
                shaped(BF16, D, span),
                shaped(BF16, D, span),
                shaped(BF16, BLOCKS, 192, span),
                shaped(F32, D, span),
                shaped(F32, 8, span),
                shaped(F32, D, 128),
                shaped(F32, D, 256),
            ],
            [
                mix_scratch,
                pltpu.VMEM((D, span), BF16),
                pltpu.VMEM((BLOCK_W, span), F32),
                pltpu.VMEM((BLOCK_W, span), F32),
                fetched,
            ],
            table_specs + [WHOLE] * (BLOCKS + 1 if first else 1) + [WHOLE] * 5,
            [WHOLE] * (10 if first else 9),
            18,
            deps,
        )(idx, *table, *([*h, chosen] if first else [h]), pad, hidden[layer], ahead_full, ahead_low, back_low)

    def ahead_ff(layer, table, middle, cols, deps=()):
        last = layer == LAYERS - 1
        return call(
            functools.partial(fwd_ff_kernel, last),
            [
                shaped(BF16, BLOCKS, 192, span),
                shaped(BF16, BLOCKS, 1536, span),
                shaped(BF16, BLOCKS, 192, span),
                shaped(BF16, BLOCKS, BLOCK_W, span) if last else shaped(F32, D, span),
                shaped(F32, 8, span),
            ],
            [ff_scratch, pltpu.VMEM((D, span), BF16), pltpu.VMEM((FF_BLOCK, span), BF16), fetched],
            table_specs + [WHOLE] * 2,
            [WHOLE] * 5,
            15,
            deps,
        )(idx, *table, middle, cols)

    saved = []
    h, q1, proj, conv, gated, q2, middle, stats_one, cols, kspec = ahead_mix(0, mix_zero, tokens_here)
    parts = token_parts(cotangent)
    middle, ff_chips, mix_one, ff_one = settle(middle, ff_chips, mix_one, ff_one)
    ff_zero = (ff[0], ff_chips, wide_shift(ff_chips, 1))
    middle, ff_zero, mix_one, ff_one = settle(middle, ff_zero, mix_one, ff_one)
    mix_chips = over_chips(mix_one)
    ff_one = others_at_once(ff_one, me)
    q3, gate_up, q4, h_next, stats_two = ahead_ff(0, ff_zero, middle, cols)
    saved.append((h, q1, proj, conv, gated, q2, middle, stats_one, cols, kspec, q3, gate_up, q4, stats_two))
    h, mix_chips, ff_one = settle(h_next, mix_chips, ff_one)
    mix_one = (mix[1], mix_chips, wide_shift(mix_chips, 1))
    h, mix_one, ff_one, parts = settle(h, mix_one, ff_one, parts)
    ff_chips = over_chips(ff_one)
    near, far = narrow_shift(parts[1], 1), narrow_shift(parts[3], 3)
    q1, proj, conv, gated, q2, middle, stats_one, cols, kspec = ahead_mix(1, mix_one, h)
    middle, ff_chips, near, far = settle(middle, ff_chips, near, far)
    ff_one = (ff[1], ff_chips, wide_shift(ff_chips, 1))
    middle, ff_one, across = settle(middle, ff_one, parts[2])
    across = narrow_shift(across, 2)
    cotangent_here = [parts[0], near, across, far]
    q3, gate_up, q4, h_last, stats_two = ahead_ff(1, ff_one, middle, cols)
    saved.append((h, q1, proj, conv, gated, q2, middle, stats_one, cols, kspec, q3, gate_up, q4, stats_two))
    weights_mix, weights_ff = (mix_zero, mix_one), (ff_zero, ff_one)

    sizes = [weight.shape[2] // 128 for weight in factors]

    def finish(layer, group, earlier):
        shapes = [(LAYERS, size, 128) for size in sizes] + [(LAYERS, BLOCK_W, 128)]
        specs = [pl.BlockSpec((None, *shape[1:]), lambda _: (layer, 0, 0)) for shape in shapes]
        if layer:
            rest = [(208, 256)]
        else:
            rest = [(LAYERS, BLOCK_W)] * 3 + [(LAYERS, 3, 384), (LAYERS, BLOCK_W), (1, BLOCK_W)]
            rest += [(LAYERS, 5, 128), (LAYERS, 128), (LAYERS, 128, 128)]
        specs += [pl.BlockSpec(shape, lambda _, n=len(shape): (0,) * n) for shape in rest]
        inputs = [SCALARS] + [ANY] * (2 + len(earlier))
        if earlier:
            inputs[-1] = pl.BlockSpec(earlier[-1].shape, lambda _: (0, 0))
        return pl.pallas_call(
            functools.partial(finish_kernel, layer),
            grid=(1,),
            out_shape=[shaped(F32, *shape) for shape in shapes + rest],
            in_specs=inputs,
            out_specs=specs,
            scratch_shapes=[
                pltpu.VMEM((FF_ROWS, 384), BF16),
                pltpu.VMEM((384, 384), BF16),
                pltpu.VMEM((IN_GRAD_ROWS, 384), BF16),
                pltpu.VMEM((2, 768, 128), F32),
                pltpu.SemaphoreType.DMA((24,)),
            ],
            input_output_aliases={3 + at: at for at in range(9)} if earlier else {},
            compiler_params=pltpu.CompilerParams(vmem_limit_bytes=56 << 20),
            cost_estimate=pl.CostEstimate(flops=4 * 10**9, bytes_accessed=1 << 20, transcendentals=0),
        )(idx, *group, *earlier)

    def collect(table, dtype):
        return call(place_parts_kernel, shaped(dtype, BLOCK_W, BLOCKS * span), [], [WHOLE], WHOLE, 2)(table)

    def to_blocks(table):
        return lax.all_to_all(table, "narrow", split_axis=0, concat_axis=0, tiled=True)

    def back_ff(layer, g_top, deps):
        last = layer == LAYERS - 1
        h, q1, proj, conv, gated, q2, middle, stats_one, cols, kspec, q3, gate_up, q4, stats_two = saved[layer]
        return call(
            functools.partial(bwd_ff_kernel, last),
            [shaped(F32, D, span), *[shaped(BF16, 4, BLOCKS, FF_ROWS // 8, 384)] * 2, shaped(F32, BLOCKS, 16, BLOCK_W)],
            [
                ff_scratch,
                pltpu.VMEM((BLOCKS, FF_ROWS, 384), BF16),
                pltpu.VMEM((D, span), BF16),
                pltpu.VMEM((BLOCKS, 192, span), BF16),
                pltpu.VMEM((BLOCKS, 192, span), BF16),
                pltpu.VMEM((2 * FF_BLOCK, span), BF16),
                pltpu.VMEM((D, span), F32),
                sent,
            ],
            table_specs + [WHOLE] * (BLOCKS if last else 1) + [WHOLE] * 6,
            [WHOLE, ANY, ANY, WHOLE],
            27,
            deps,
        )(idx, *weights_ff[layer], *(g_top if last else [g_top]), q4, gate_up, q3, middle, stats_two, cols)

    def back_conv(layer, g_mid, small_ff, deps):
        h, q1, proj, conv, gated, q2, middle, stats_one, cols, kspec, q3, gate_up, q4, stats_two = saved[layer]
        return call(
            functools.partial(bwd_conv_kernel, seqs, penalty),
            [shaped(BF16, BLOCKS, 384, span), *[shaped(BF16, 4, BLOCKS, 48, 384)] * 2],
            [
                mix_scratch,
                pltpu.VMEM((BLOCKS, 384, 384), BF16),
                pltpu.VMEM((BLOCKS, 192, span), BF16),
                pltpu.VMEM((BLOCK_W, span), F32),
                pltpu.VMEM((BLOCK_W, span), F32),
                sent,
            ],
            table_specs + [WHOLE] * 15,
            [WHOLE, ANY, ANY],
            23,
            deps,
        )(
            idx,
            *weights_mix[layer],
            g_mid,
            q2,
            gated,
            conv,
            proj,
            pad,
            cols,
            kspec,
            ahead_low,
            back_low,
            small_ff,
            hidden[layer],
            filter_two[layer],
            features,
            back_full,
        )

    def back_in(layer, gv, g_mid, deps):
        first = layer == 0
        h, q1, proj, conv, gated, q2, middle, stats_one, cols, kspec, q3, gate_up, q4, stats_two = saved[layer]
        return call(
            functools.partial(bwd_in_kernel, first),
            [
                shaped(BF16, BLOCKS, BLOCK_W, span) if first else shaped(F32, D, span),
                *[shaped(BF16, 4, BLOCKS, IN_GRAD_ROWS // 8, 384)] * 2,
            ],
            [
                mix_scratch,
                pltpu.VMEM((BLOCKS, IN_GRAD_ROWS, 384), BF16),
                pltpu.VMEM((BLOCKS, 384, span), BF16),
                pltpu.VMEM((D, span), F32),
                pltpu.VMEM((BLOCKS, 16, BLOCK_W), F32),
                sent,
            ]
            + ([pltpu.VMEM((D, span), F32)] if first else []),
            table_specs + [WHOLE] * (7 if first else 6),
            [WHOLE, ANY, ANY],
            12,
            deps,
        )(idx, *weights_mix[layer], gv, g_mid, q1, h, stats_one, cols, *([chosen] if first else []))

    def spread(piece):
        chips = over_chips(piece)
        return chips, wide_shift(chips, 1)

    def each_after(arrays, *deps):
        return [after(x, *deps) for x in arrays]

    h_last, cotangent_here = settle(h_last, cotangent_here)
    mixed_parts = to_blocks(h_last)
    g_mid, near, far, small_ff = back_ff(1, cotangent_here, ())
    g_mid, near, far, mixed_parts = settle(g_mid, near, far, mixed_parts)
    mixed_out = collect(mixed_parts, BF16)
    ff_one = reduce_core(near, far)
    gv, near, far = back_conv(1, g_mid, small_ff, (mixed_out,))
    gv, near, far, ff_one = settle(gv, near, far, ff_one)
    conv_one = reduce_core(near, far)
    ff_parts = [ff_one[0], wide_shift(ff_one[1], 2), wide_shift(ff_one[2], 4)]
    g_top, near, far = back_in(1, gv, g_mid, ())
    g_top, near, far, conv_one, ff_parts, last = settle(g_top, near, far, conv_one, ff_parts, ff_one[3])
    near, far = settle(near, reduce_core(near, far))
    mix_parts, g_top = settle(join_rows(conv_one, far), g_top)
    ff_parts = ff_parts + [wide_shift(last, 6)]
    mix_parts = move_chips(mix_parts)
    g_mid, near, far, small_ff = back_ff(0, g_top, ())
    g_mid, near, far, mix_parts, ff_parts = settle(g_mid, near, far, mix_parts, ff_parts)
    all_one, ff_zero = settle(join_rows(add_chips(ff_parts), add_chips(mix_parts)), reduce_core(near, far))
    all_parts = blocks_at_once(all_one, me)
    ff_parts = move_chips(ff_zero)
    gv, near, far = back_conv(0, g_mid, small_ff, ff_zero)
    gv, near, far, all_parts, ff_parts = settle(gv, near, far, all_parts, ff_parts)
    one_chips = over_chips(added(all_parts))
    ff_parts = blocks_at_once(add_chips(ff_parts), me)
    conv_zero = reduce_core(near, far)
    g_top, near, far = back_in(0, gv, g_mid, ())
    g_top, near, far, one_chips, ff_parts, conv_zero = settle(g_top, near, far, one_chips, ff_parts, conv_zero)

    token_grads = to_blocks(g_top)
    in_zero = reduce_core(near, far)
    one_group = (one_chips, wide_shift(one_chips, 1))
    in_zero, one_group, ff_zero = settle(in_zero, one_group, added(ff_parts))
    mix_parts = move_chips(join_rows(conv_zero, in_zero))
    flat = finish(1, one_group, [])
    flat, mix_parts = settle(flat, mix_parts)
    zero_chips = over_chips(jnp.concatenate([ff_zero, reduce_blocks(add_chips(mix_parts))], axis=0))
    zero_chips, token_grads = settle(zero_chips, token_grads)
    zero_group = (zero_chips, wide_shift(zero_chips, 1))
    grad_tokens = collect(token_grads, F32)
    flat = finish(0, zero_group, flat)
    grads = [table.reshape(LAYERS, 1, table.shape[1] * 128) for table in flat[:8]]
    three, g_gain_one, g_gain_two, g_skip, g_taps, g_decay, g_mask, g_one, g_bias, g_two = flat[8:]
    return (
        mixed_out,
        grad_tokens,
        g_mask[0],
        g_gain_one,
        grads[0],
        grads[1],
        g_taps[:, :, None],
        g_skip,
        g_decay,
        g_one,
        g_bias,
        g_two,
        three,
        grads[2],
        grads[3],
        g_gain_two,
        grads[4],
        grads[5],
        grads[6],
        grads[7],
    )


def solution(mesh):
    placed = (
        P("narrow", "wide"),
        P("wide"),
        P("wide", None),
        P("narrow", "wide"),
        P("narrow"),
        P(None, "narrow"),
        P(None, "narrow", None),
        P(None, "narrow", None),
        P(None, None, "narrow", None),
        P(None, "narrow"),
        P(None, "narrow"),
        P(),
        P(),
        P(),
        P(None, "narrow", None),
        P(None, "narrow", None),
        P(None, "narrow", None),
        P(None, "narrow"),
        P(None, "narrow", None),
        P(None, "narrow", None),
        P(None, "narrow", None),
        P(None, "narrow", None),
    )
    return jax.shard_map(
        local,
        mesh=mesh,
        in_specs=placed,
        out_specs=(
            P("narrow", "wide"),
            P("narrow", "wide"),
            P("narrow"),
            P(None, "narrow"),
            P(None, "narrow", None),
            P(None, "narrow", None),
            P(None, None, "narrow", None),
            P(None, "narrow"),
            P(None, "narrow"),
            P(),
            P(),
            P(),
            P(None, "narrow", None),
            P(None, "narrow", None),
            P(None, "narrow", None),
            P(None, "narrow"),
            P(None, "narrow", None),
            P(None, "narrow", None),
            P(None, "narrow", None),
            P(None, "narrow", None),
        ),
        check_vma=False,
    )
```

```python
import math
import functools
import numpy as np
import jax
import jax.numpy as jnp
from jax import lax
from jax.experimental import pallas as pl
from jax.experimental.pallas import tpu as pltpu
from jax.sharding import PartitionSpec as P

F32 = jnp.float32
BF16 = jnp.bfloat16
D = 768
LENGTH = 128
LAYERS = 2
BLOCK_W = 192
FF_BLOCK = 768
BLOCKS = 4
EPSILON = 1e-05
HIGHEST = lax.Precision.HIGHEST
GAIN_ONE, GAIN_TWO, SKIP, TAP_X, TAP_G, MASK, DECAY = 0, 1, 2, 3, 6, 9, 10
IN_ONE, IN_TWO, OUT_ROWS, PARAM_ROWS = 0, 192, 576, 768
UP_ONE, UP_TWO, DOWN_ONE = 0, 192, 960
MIX_ROWS, FF_USED, FF_ROWS, IN_GRAD_ROWS = 1024, 1344, 1408, 640
HIDDEN_ONE, HIDDEN_TWO, SLOPE_ONE, SLOPE_TWO = 0, 1, 2, 3
PIECE_ROWS = {"ff": 176, "conv": 48, "in": 80}


def nn(a, b):
    return lax.dot_general(a, b, (((1,), (0,)), ((), ())), preferred_element_type=F32)


def nt(a, b):
    return lax.dot_general(a, b, (((1,), (1,)), ((), ())), preferred_element_type=F32)


def tn(a, b):
    return lax.dot_general(a, b, (((0,), (0,)), ((), ())), preferred_element_type=F32)


def spectrum_tables():
    time = np.arange(2 * LENGTH)
    freq = np.arange(LENGTH)
    angle = 2.0 * np.pi * np.outer(time, freq) / (2 * LENGTH)
    ahead = np.concatenate([np.cos(angle), -np.sin(angle)], axis=1)
    ahead[:, LENGTH] = np.cos(np.pi * time)
    scale = np.full((2 * LENGTH,), 2.0 / (2 * LENGTH))
    scale[0] = scale[LENGTH] = 1.0 / (2 * LENGTH)
    return ahead.astype(np.float32), (ahead * scale[None, :]).T.astype(np.float32)


def lanes_of(shape):
    return lax.broadcasted_iota(jnp.int32, shape, 1)


def column(cols, rows, at, lanes=LENGTH):
    one = jnp.broadcast_to(cols[rows, at : at + 1], (BLOCK_W, LENGTH))
    return one if lanes == LENGTH else jnp.concatenate([one] * (lanes // LENGTH), axis=1)


def later(v, lane):
    return jnp.where(lane == 0, 0.0, pltpu.roll(v, 1, 1))


def earlier(v, lane):
    return jnp.where(lane == LENGTH - 1, 0.0, pltpu.roll(v, LENGTH - 1, 1))


def norm_rows(parts):
    total = sum(jnp.sum(p, axis=0, keepdims=True) for p in parts)
    squares = sum(jnp.sum(p * p, axis=0, keepdims=True) for p in parts)
    mean = total / D
    inv = lax.rsqrt(squares / D - mean * mean + EPSILON)
    return mean, inv


def block(ref, b, width=BLOCK_W):
    return ref[pl.ds(b * width, width), :]


def fwd_mix_kernel(first, seqs, *refs):
    idx, own, rel_a, rel_b, *refs = refs
    if first:
        *parts, chosen_ref = refs[: BLOCKS + 1]
        refs = refs[BLOCKS + 1 :]
    else:
        h_ref, *refs = refs
    pad, hidden, ahead_full, ahead, back, *refs = refs
    if first:
        h_ref, *refs = refs
    q1, proj, conv, gated, q2, middle, stats, cols, kspec, table, normed, xs, gs, sem = refs
    at = distances(idx)
    fetched = fetch_table(idx, own, rel_a, rel_b, table.buffer, sem)
    w = table.buffer
    if first:
        fetched()
        make_params(w, at, hidden, ahead_full, cols, kspec)
        keep = chosen_ref[0:1, :]
        for k, part in enumerate(parts):
            rows = pl.ds(pl.multiple_of(block_of(idx, k) * BLOCK_W, BLOCK_W), BLOCK_W)
            h_ref.buffer[rows, :] = part[...].astype(F32) * (1.0 - keep) + keep * column(cols, rows, MASK, seqs * LENGTH)
        h_ref.start()
        h_ref = h_ref.buffer
    mean, inv = norm_rows([block(h_ref, b) for b in range(BLOCKS)])
    if not first:
        fetched()
        make_params(w, at, hidden, ahead_full, cols, kspec)
    table.start()
    stats[0:1, :] = mean
    stats[1:2, :] = inv
    for b in range(BLOCKS):
        rows = pl.ds(b * BLOCK_W, BLOCK_W)
        normed[rows, :] = ((h_ref[rows, :] - mean) * inv * column(cols, rows, GAIN_ONE, seqs * LENGTH)).astype(BF16)
    for b in range(BLOCKS):
        inner = tn(w[at[b], IN_ONE : IN_ONE + 192, :], block(normed, b)).astype(BF16)
        for c in range(BLOCKS):
            q1.buffer[c, 96 * b : 96 * b + 96, :] = inner[96 * c : 96 * c + 96]
    q1.start()
    lane = lanes_of((BLOCK_W, LENGTH))
    row_lane = lanes_of((BLOCK_W, LENGTH))
    for c in range(BLOCKS):
        rows = pl.ds(c * BLOCK_W, BLOCK_W)
        value = tn(w[at[c], IN_TWO : IN_TWO + 384, :], q1.buffer[c]) * pad[0:1, :]
        proj.buffer[c] = value.astype(BF16)
        taps = [[column(cols, rows, tap + n) for n in range(3)] for tap in (TAP_X, TAP_G)]
        skip = column(cols, rows, SKIP)
        for s in range(seqs):
            here = slice(s * LENGTH, (s + 1) * LENGTH)
            for part, tap, out in ((0, taps[0], xs), (192, taps[1], gs)):
                v = value[part : part + 192, here]
                out[:, here] = (
                    tap[0] * later(v, lane)
                    + tap[1] * v
                    + tap[2] * earlier(v, lane)
                )
        signal = jnp.concatenate([xs[:, s * LENGTH : (s + 1) * LENGTH] for s in range(seqs)], axis=0)
        spec = nn(signal.astype(BF16), ahead[...])
        k_re = kspec[rows, 0:LENGTH]
        k_im = kspec[rows, LENGTH : 2 * LENGTH]
        k_off = jnp.where(row_lane == 0, 0.0, k_im)
        k_im = jnp.where(row_lane == 0, k_im, k_re)
        made = []
        for s in range(seqs):
            re = spec[s * 192 : s * 192 + 192, 0:LENGTH]
            im = spec[s * 192 : s * 192 + 192, LENGTH : 2 * LENGTH]
            made.append(
                jnp.concatenate([re * k_re - im * k_off, re * k_off + im * k_im], axis=1).astype(BF16)
            )
        y = nn(jnp.concatenate(made, axis=0), back[...])
        for s in range(seqs):
            here = slice(s * LENGTH, (s + 1) * LENGTH)
            value = y[s * 192 : s * 192 + 192] + skip * xs[:, here]
            conv.buffer[rows, here] = value.astype(BF16)
            gated.buffer[rows, here] = (value * gs[:, here]).astype(BF16)
    for part in (proj, conv, gated):
        part.start()
    for b in range(BLOCKS):
        inner = tn(w[at[b], OUT_ROWS : OUT_ROWS + 192, 0:192], block(gated.buffer, b)).astype(BF16)
        for c in range(BLOCKS):
            q2[c, 48 * b : 48 * b + 48, :] = inner[48 * c : 48 * c + 48]
    for c in range(BLOCKS):
        rows = pl.ds(c * BLOCK_W, BLOCK_W)
        middle[rows, :] = h_ref[rows, :] + tn(w[at[c], OUT_ROWS : OUT_ROWS + 192, 192:384], q2[c])


def gelu_parts(v):
    inner = math.sqrt(2.0 / math.pi) * (v + 0.044715 * (v * v * v))
    return jnp.tanh(inner)


def fwd_ff_kernel(last, idx, own, rel_a, rel_b, middle, cols, q3, gate_up, q4, h_next, stats, table, normed, act, sem):
    at = distances(idx)
    fetched = fetch_table(idx, own, rel_a, rel_b, table.buffer, sem)
    w = table.buffer
    mean, inv = norm_rows([block(middle, b) for b in range(BLOCKS)])
    stats[0:1, :] = mean
    stats[1:2, :] = inv
    for b in range(BLOCKS):
        rows = pl.ds(b * BLOCK_W, BLOCK_W)
        normed[rows, :] = ((middle[rows, :] - mean) * inv * column(cols, rows, GAIN_TWO, middle.shape[1])).astype(BF16)
    fetched()
    table.start()
    for b in range(BLOCKS):
        inner = tn(w[at[b], UP_ONE : UP_ONE + 192, 0:192], block(normed, b)).astype(BF16)
        for c in range(BLOCKS):
            q3.buffer[c, 48 * b : 48 * b + 48, :] = inner[48 * c : 48 * c + 48]
    q3.start()
    for c in range(BLOCKS):
        for half in range(2):
            ups = []
            for piece in (half, half + 2):
                ups.append(tn(w[at[c], UP_TWO + 192 * piece : UP_TWO + 192 * piece + 192, :], q3.buffer[c]))
            gate, up = ups
            gate_up.buffer[c, 384 * half : 384 * half + 384, :] = gate.astype(BF16)
            gate_up.buffer[c, 768 + 384 * half : 768 + 384 * half + 384, :] = up.astype(BF16)
            act[384 * half : 384 * half + 384, :] = (
                0.5 * gate * (1.0 + gelu_parts(gate)) * up
            ).astype(BF16)
        gate_up.start(c)
        inner = (
            tn(w[at[c], DOWN_ONE : DOWN_ONE + 384, 0:192], act[0:384, :])
            + tn(w[at[c], DOWN_ONE : DOWN_ONE + 384, 192:384], act[384:768, :])
        ).astype(BF16)
        for to in range(BLOCKS):
            q4[to, 48 * c : 48 * c + 48, :] = inner[48 * to : 48 * to + 48]
    for c in range(BLOCKS):
        rows = pl.ds(c * BLOCK_W, BLOCK_W)
        value = middle[rows, :] + tn(w[at[c], UP_ONE : UP_ONE + 192, 192:384], q4[c])
        if last:
            h_next[c] = value.astype(BF16)
        else:
            h_next[rows, :] = value


def bwd_ff_kernel(last, idx, table, *refs):
    parts = refs[: BLOCKS if last else 1]
    q4, gate_up, q3, middle, stats, cols, g_mid, g_near, g_far, small, g_w, g_low, gi4, gi3, g_gu, g_n, sem = refs[len(parts) :]
    at = distances(idx)
    for part in parts:
        part.start()
    q4.start()
    table.start((slice(None), slice(UP_ONE, UP_ONE + 192)))
    gate_up.start(0)
    table.start((slice(None), slice(DOWN_ONE, FF_USED)))
    table.start((slice(None), slice(UP_TWO, DOWN_ONE)))
    q3.start()
    for b in range(1, BLOCKS):
        gate_up.start(b)
    for part in (middle, cols):
        part.start()
    w = table.buffer
    mean = stats[0:1, :]
    inv = stats[1:2, :]
    if last:
        for k, part in enumerate(parts):
            g_low[pl.ds(pl.multiple_of(block_of(idx, k) * BLOCK_W, BLOCK_W), BLOCK_W), :] = part.wait()[...]
        g_top = g_low
    else:
        g_top = parts[0].wait()
        for c in range(BLOCKS):
            g_low[c * 192 : c * 192 + 192, :] = block(g_top, c).astype(BF16)
    for b in range(BLOCKS):
        g_w[at[b], FF_USED:FF_ROWS, :] = jnp.zeros((FF_ROWS - FF_USED, 384), BF16)
    table.wait(0)
    q4 = q4.wait()
    for c in range(BLOCKS):
        gt = block(g_low, c)
        g_w[at[c], UP_ONE : UP_ONE + 192, 192:384] = nt(q4[c], gt).astype(BF16)
        gq = nn(w[at[c], UP_ONE : UP_ONE + 192, 192:384], gt).astype(BF16)
        for b in range(BLOCKS):
            gi4[b, 48 * c : 48 * c + 48, :] = gq[48 * b : 48 * b + 48]
    rate = math.sqrt(2.0 / math.pi)
    table.wait(1)
    for b in range(BLOCKS):
        gate_up.wait(b)
        if b == 0:
            table.wait()
            q3.wait()
        for half in range(2):
            span = slice(192 * half, 192 * half + 192)
            gate = gate_up.buffer[b, 384 * half : 384 * half + 384, :].astype(F32)
            up = gate_up.buffer[b, 768 + 384 * half : 768 + 384 * half + 384, :].astype(F32)
            ga = nn(w[at[b], DOWN_ONE : DOWN_ONE + 384, span], gi4[b])
            square = gate * gate
            t = jnp.tanh(rate * gate * (1.0 + 0.044715 * square))
            rise = 0.5 * (1.0 + t)
            gelu = gate * rise
            slope = rise + 0.5 * gelu_slope(gate, square, t, rate)
            act = (gelu * up).astype(BF16)
            g_w[at[b], DOWN_ONE : DOWN_ONE + 384, span] = nt(act, gi4[b]).astype(BF16)
            g_gu[384 * half : 384 * half + 384, :] = (ga * up * slope).astype(BF16)
            g_gu[768 + 384 * half : 768 + 384 * half + 384, :] = (ga * gelu).astype(BF16)
        gq = None
        for piece in range(4):
            rows = slice(UP_TWO + 192 * piece, UP_TWO + 192 * piece + 192)
            gg = g_gu[384 * piece : 384 * piece + 384, :]
            g_w[at[b], rows, :] = nt(q3.buffer[b], gg).astype(BF16)
            term = nn(w[at[b], rows, :], gg)
            gq = term if gq is None else gq + term
        gq = gq.astype(BF16)
        for to in range(BLOCKS):
            gi3[to, 48 * b : 48 * b + 48, :] = gq[48 * to : 48 * to + 48]
    finish = send_early(g_w, (g_near, g_far), idx, sem, UP_ONE + 192)
    norm_back(
        at, middle.wait(), mean, inv, cols.wait(), GAIN_TWO, w, slice(UP_ONE, UP_ONE + 192), slice(0, 192), gi3, g_n, g_w, small, 1, g_top, g_mid
    )
    finish()


def gelu_slope(gate, square, t, rate):
    return gate * (1.0 - t * t) * (rate * (1.0 + 3.0 * 0.044715 * square))


def row_sums(place, values):
    lanes = values.shape[1]
    part = values[:, 0:LENGTH]
    for at in range(LENGTH, lanes, LENGTH):
        part = part + values[:, at : at + LENGTH]
    high = part.astype(BF16)
    low = (part - high.astype(F32)).astype(BF16)
    pick = (lax.broadcasted_iota(jnp.int32, (16, LENGTH), 0) == place).astype(F32).astype(BF16)
    return nt(pick, high) + nt(pick, low)


def norm_back(at, h, mean, inv, cols, gain_at, w, w_rows, w_lanes, gi, g_n, g_w, small, place, g_in, g_out):
    plain = cross = 0.0
    for b in range(BLOCKS):
        rows = pl.ds(b * 192, 192)
        gain = column(cols, rows, gain_at, h.shape[1])
        xh = (h[rows, :] - mean) * inv
        gn = nn(w[at[b], w_rows, w_lanes], gi[b])
        g_w[at[b], w_rows, w_lanes] = nt((xh * gain).astype(BF16), gi[b]).astype(BF16)
        gx = gn * xh
        small[b] = row_sums(place, gx)
        g_n[rows, :] = gn * gain
        plain = plain + jnp.sum(gn * gain, axis=0, keepdims=True)
        cross = cross + jnp.sum(gx * gain, axis=0, keepdims=True)
    plain = plain / D
    cross = cross / D
    for b in range(BLOCKS):
        rows = pl.ds(b * 192, 192)
        xh = (h[rows, :] - mean) * inv
        value = g_in[rows, :].astype(F32) + inv * (g_n[rows, :] - plain - xh * cross)
        if isinstance(g_out, Move):
            g_out.buffer[rows, :] = value
            g_out.start((rows, slice(None)))
        else:
            g_out[rows, :] = value


def bwd_conv_kernel(
    seqs, penalty, idx, table, g_mid, q2, gated, conv, proj, pad, cols, kspec, ahead, back, small_ff,
    filt, weight_two, features, back_full, gv, g_near, g_far, g_w, gi2, gcs, xs, sem
):
    at = distances(idx)
    table.start((slice(None), slice(OUT_ROWS, PARAM_ROWS + BLOCK_W)))
    for part in (q2, g_mid, gated, proj, conv, kspec):
        part.start()
    w, q2, g_mid = table.wait(), q2.wait(), g_mid.wait()
    for c in range(BLOCKS):
        gt = block(g_mid, c).astype(BF16)
        g_w[at[c], 0:192, 192:384] = nt(q2[c], gt).astype(BF16)
        gq = nn(w[at[c], OUT_ROWS : OUT_ROWS + 192, 192:384], gt).astype(BF16)
        for b in range(BLOCKS):
            gi2[b, 48 * c : 48 * c + 48, :] = gq[48 * b : 48 * b + 48]
    lane = lanes_of((BLOCK_W, LENGTH))
    first_lane = lane == 0
    for part in (gated, proj, conv):
        part.wait()
    kspec = kspec.wait()
    for b in range(BLOCKS):
        rows = pl.ds(b * 192, 192)
        g_gated = nn(w[at[b], OUT_ROWS : OUT_ROWS + 192, 0:192], gi2[b])
        g_w[at[b], 0:192, 0:192] = nt(block(gated.buffer, b), gi2[b]).astype(BF16)
        tap_x = [column(cols, rows, TAP_X + n) for n in range(3)]
        tap_g = [column(cols, rows, TAP_G + n) for n in range(3)]
        skip = column(cols, rows, SKIP)
        sums = [0.0] * 7
        for s in range(seqs):
            here = slice(s * LENGTH, (s + 1) * LENGTH)
            v = proj.buffer[b, 0:192, here].astype(F32)
            xs[:, here] = (
                tap_x[0] * later(v, lane)
                + tap_x[1] * v
                + tap_x[2] * earlier(v, lane)
            )
            v = proj.buffer[b, 192:384, here].astype(F32)
            after, before = later(v, lane), earlier(v, lane)
            gate = (
                tap_g[0] * after
                + tap_g[1] * v
                + tap_g[2] * before
            )
            gg = g_gated[:, here]
            gcs[:, here] = gg * gate
            z = gg * conv.buffer[rows, here].astype(F32)
            sums[4] = sums[4] + z * after
            sums[5] = sums[5] + z * v
            sums[6] = sums[6] + z * before
            gv.buffer[b, 192:384, here] = (
                (
                    tap_g[0] * earlier(z, lane)
                    + tap_g[1] * z
                    + tap_g[2] * later(z, lane)
                )
                * pad[0:1, here]
            ).astype(BF16)
            sums[0] = sums[0] + gcs[:, here] * xs[:, here]
        stacked = jnp.concatenate(
            [ref[:, s * LENGTH : (s + 1) * LENGTH] for ref in (xs, gcs) for s in range(seqs)], axis=0
        )
        spec = nn(stacked.astype(BF16), ahead[...])
        k_re = kspec[rows, 0:LENGTH]
        k_im = kspec[rows, LENGTH : 2 * LENGTH]
        k_off = jnp.where(first_lane, 0.0, k_im)
        k_im = jnp.where(first_lane, k_im, k_re)
        made = []
        p_re = p_im = p_off = 0.0
        for s in range(seqs):
            x_re = spec[s * 192 : s * 192 + 192, 0:LENGTH]
            x_im = spec[s * 192 : s * 192 + 192, LENGTH : 2 * LENGTH]
            start = (seqs + s) * 192
            g_re = spec[start : start + 192, 0:LENGTH]
            g_im = spec[start : start + 192, LENGTH : 2 * LENGTH]
            p_re = p_re + g_re * x_re
            p_im = p_im + g_im * x_im
            p_off = p_off + (g_im * x_re - g_re * x_im)
            made.append(
                jnp.concatenate([g_re * k_re + g_im * k_off, g_im * k_im - g_re * k_off], axis=1).astype(BF16)
            )
        g_table = exact(
            jnp.concatenate(
                [jnp.where(first_lane, p_re, p_re + p_im), jnp.where(first_lane, p_im, p_off)], axis=1
            ),
            back_full[...],
            1,
            0,
        )
        last, envelope, kernel = filter_values(w, at, b, cols, filt[HIDDEN_TWO])
        g_table = g_table + penalty * kernel
        g_decay = -(g_table * kernel * filter_lag())
        g_shape = g_table * envelope
        g_w[at[b], 192:384, 0:128] = exact(g_shape, filt[HIDDEN_TWO], 1, 0).astype(BF16)
        term = exact(g_shape, last, 0, 0)
        g_hidden = term if b == 0 else g_hidden + term
        y = nn(jnp.concatenate(made, axis=0), back[...])
        for s in range(seqs):
            here = slice(s * LENGTH, (s + 1) * LENGTH)
            z = y[s * 192 : s * 192 + 192] + skip * gcs[:, here]
            v = proj.buffer[b, 0:192, here].astype(F32)
            sums[1] = sums[1] + z * later(v, lane)
            sums[2] = sums[2] + z * v
            sums[3] = sums[3] + z * earlier(v, lane)
            gv.buffer[b, 0:192, here] = (
                (
                    tap_x[0] * earlier(z, lane)
                    + tap_x[1] * z
                    + tap_x[2] * later(z, lane)
                )
                * pad[0:1, here]
            ).astype(BF16)
        gv.start(b)
        totals = small_ff[b]
        for place, value in enumerate(sums + [g_decay]):
            totals = totals + row_sums(2 + place, value)
        totals = totals.astype(BF16)
        g_w[at[b], 192:208, 256:384] = totals[:, 0:128]
        g_w[at[b], 208:224, 256:320] = totals[:, 128:192]
        g_w[at[b], 208:224, 320:384] = jnp.zeros((16, 64), BF16)
        g_w[at[b], 224:384, 256:384] = jnp.zeros((160, 128), BF16)
    g_two = g_hidden * filt[SLOPE_TWO]
    g_one = exact(g_two, weight_two[...], 1, 1) * filt[SLOPE_ONE]
    g_weight_two = exact(filt[HIDDEN_ONE], g_two, 0, 0).astype(BF16)
    g_weight_one = exact(features[...], g_one, 0, 0)[0:16, :].astype(BF16)
    for b in range(BLOCKS):
        g_w[at[b], 192:320, 128:256] = g_weight_two
        g_w[at[b], 320:336, 128:256] = g_weight_one
        g_w[at[b], 336:384, 128:256] = jnp.zeros((48, 128), BF16)
    send_pieces(g_w, (g_near, g_far), idx, sem)


def bwd_in_kernel(first, *refs):
    refs = list(refs)
    idx, table, gv, g_mid, q1, h, stats, cols = refs[:8]
    refs = refs[8:]
    chosen = refs.pop(0) if first else None
    g_out, g_near, g_far, g_w, gi1, g_n, small, sem = refs[:8]
    g_h = refs[8] if first else g_out
    at = distances(idx)
    for c in range(BLOCKS):
        gv.start(c)
        q1.start(c)
        if c == 0:
            table.start((slice(None), slice(IN_ONE, OUT_ROWS)))
    for part in (h, g_mid):
        part.start()
    w = table.wait()
    mean = stats[0:1, :]
    inv = stats[1:2, :]
    for c in range(BLOCKS):
        gv.wait(c)
        q1.wait(c)
        g_w[at[c], IN_TWO : IN_TWO + 384, :] = nt(q1.buffer[c], gv.buffer[c]).astype(BF16)
        gq = nn(w[at[c], IN_TWO : IN_TWO + 384, :], gv.buffer[c]).astype(BF16)
        for b in range(BLOCKS):
            gi1[b, 96 * c : 96 * c + 96, :] = gq[96 * b : 96 * b + 96]
    norm_back(
        at, h.wait(), mean, inv, cols, GAIN_ONE, w, slice(IN_ONE, IN_ONE + 192), slice(0, 384), gi1, g_n, g_w, small, 0, g_mid.wait(), g_h
    )
    for b in range(BLOCKS):
        rows = pl.ds(b * 192, 192)
        totals = small[b]
        if first:
            value = g_h[rows, :]
            masked = value * chosen[0:1, :]
            totals = totals + row_sums(1, masked)
            g_out.buffer[b] = (value - masked).astype(BF16)
            g_out.start(b)
        g_w[at[b], 576:592, 0:192] = totals.astype(BF16)
        g_w[at[b], 576:592, 192:384] = jnp.zeros((16, 192), BF16)
        g_w[at[b], 592:640, :] = jnp.zeros((48, 384), BF16)
    send_pieces(g_w, (g_near, g_far), idx, sem)


def piece_rows(idx, core, chip, rows):
    return pl.ds(pl.multiple_of((idx[1] ^ (2 * chip + core)) * rows, 16), rows)


def block_of(idx, k):
    return (idx[0] - k) & (BLOCKS - 1)


def distances(idx):
    return [(idx[0] - b) & (BLOCKS - 1) for b in range(BLOCKS)]


def start_copies(pairs, sem):
    copies = [pltpu.make_async_copy(source, target, sem.at[at]) for at, (source, target) in enumerate(pairs)]
    for copy in copies:
        copy.start()

    def wait():
        for copy in copies:
            copy.wait()

    return wait


def run_copies(pairs, sem):
    start_copies(pairs, sem)()


def send_early(table, outs, idx, sem, done):
    rows = outs[0].shape[2]
    late = -(-done // rows)
    copies = []
    for core in range(2):
        for chip in range(4):
            at = idx[1] ^ (2 * chip + core)
            copy = pltpu.make_async_copy(
                table.at[:, piece_rows(idx, core, chip, rows), :], outs[core].at[chip], sem.at[len(copies)]
            )
            pl.when(at >= late)(copy.start)
            copies.append((at, copy))

    def finish():
        for at, copy in copies:
            pl.when(at < late)(copy.start)
        for _, copy in copies:
            copy.wait()

    return finish


def send_pieces(table, outs, idx, sem):
    rows = outs[0].shape[2]
    run_copies(
        [(table.at[:, piece_rows(idx, core, chip, rows), :], outs[core].at[chip]) for core in range(2) for chip in range(4)],
        sem,
    )


def fetch_table(idx, own, rel_a, rel_b, table, sem):
    rows = rel_a.shape[2]
    return start_copies(
        [(own, table.at[0])]
        + [
            (rel.at[chip], table.at[1:BLOCKS, piece_rows(idx, core, chip, rows), :])
            for core, rel in enumerate((rel_a, rel_b))
            for chip in range(4)
        ],
        sem,
    )


def exact(a, b, left, right):
    return lax.dot_general(
        a, b, (((left,), (right,)), ((), ())), precision=HIGHEST, preferred_element_type=F32
    )


def filter_lag():
    place = lanes_of((BLOCK_W, 2 * LENGTH))
    return jnp.where(place < LENGTH, place, 2 * LENGTH - place).astype(F32)


def filter_values(w, at, b, cols, hidden):
    packed = w[at[b], PARAM_ROWS : PARAM_ROWS + BLOCK_W, 0:256].astype(F32)
    last = packed[:, 0:128] + packed[:, 128:256]
    lag = filter_lag()
    envelope = jnp.exp(-lag * cols[b * BLOCK_W : (b + 1) * BLOCK_W, DECAY : DECAY + 1]) * (1.0 / math.sqrt(LENGTH))
    envelope = jnp.where(lag == LENGTH, 0.0, envelope)
    return last, envelope, exact(last, hidden, 1, 1) * envelope


def make_params(w, at, hidden, ahead_full, cols, kspec):
    for b in range(BLOCKS):
        rows = pl.ds(b * BLOCK_W, BLOCK_W)
        three = w[at[b], PARAM_ROWS : PARAM_ROWS + BLOCK_W, 256:384].astype(F32)
        cols[rows, :] = three + pltpu.roll(three, 128 - 16, 1) + pltpu.roll(three, 128 - 32, 1)
        kspec[rows, :] = exact(filter_values(w, at, b, cols, hidden[HIDDEN_TWO])[2], ahead_full[...], 1, 0)


def fold_back(lines, wide, count):
    low = lanes_of((count // 2, 128)) < 64
    one, two, three = (lines[pl.ds(j, count // 2, stride=3), :] for j in range(3))
    three = pltpu.roll(three, 64, 1)
    wide[0, pl.ds(0, count // 2, stride=2), :] = one
    wide[1, pl.ds(0, count // 2, stride=2), :] = two
    wide[0, pl.ds(1, count // 2, stride=2), :] = jnp.where(low, pltpu.roll(two, 64, 1), three)
    wide[1, pl.ds(1, count // 2, stride=2), :] = three


def fold_out(wide, out, count):
    low = lanes_of((count // 2, 128)) < 64
    half = count // 2
    even_a = wide[0, pl.ds(0, half, stride=2), :]
    even_b = wide[1, pl.ds(0, half, stride=2), :]
    odd_a = pltpu.roll(wide[0, pl.ds(1, half, stride=2), :], 64, 1)
    odd_b = pltpu.roll(wide[1, pl.ds(1, half, stride=2), :], 64, 1)
    out[pl.ds(0, half, stride=3), :] = even_a
    out[pl.ds(1, half, stride=3), :] = jnp.where(low, even_b, odd_a)
    out[pl.ds(2, half, stride=3), :] = jnp.where(low, odd_a, odd_b)


def spread_lines(flat, layer, count, lanes, lines):
    rows = flat.shape[1]
    lines[0:rows, :] = flat[layer].astype(F32)
    return [lines[pl.ds(j, count, stride=lanes), :] for j in range(lanes)]


def narrow_lines(flat, layer, count, lines, wide):
    rows = flat.shape[1]
    lines[0:rows, :] = flat[layer].astype(F32)
    fold_back(lines, wide, count)
    return jnp.concatenate([wide[0, 0:count, :], wide[1, 0:count, 0:64]], axis=1).astype(BF16)


def own_piece(idx, table, out):
    rows = out.shape[0]
    out[...] = table[pl.ds(pl.multiple_of(idx[1] * rows, 16), rows), :]


def pack_mix_kernel(
    idx, in_one, in_two, out_one, out_two, gain_one, gain_two, skip, taps, mask, decay, filter_three,
    table_a, table_b, piece_a, piece_b, lines, wide, cols,
):
    tables, pieces = (table_a, table_b), (piece_a, piece_b)
    eye = (
        lax.broadcasted_iota(jnp.int32, (16, 128), 0) == lax.broadcasted_iota(jnp.int32, (16, 128), 1)
    ).astype(F32)
    cols[...] = jnp.zeros((16, BLOCK_W), F32)
    for layer in range(LAYERS):
        table = tables[layer]
        for flat, start, count in ((in_one, IN_ONE, 192), (in_two, IN_TWO, 384)):
            for j, part in enumerate(spread_lines(flat, layer, count, 3, lines)):
                table[start : start + count, 128 * j : 128 * j + 128] = part.astype(BF16)
        table[OUT_ROWS : OUT_ROWS + 192, 0:192] = narrow_lines(out_one, layer, 192, lines, wide)
        table[OUT_ROWS : OUT_ROWS + 192, 192:384] = narrow_lines(out_two, layer, 192, lines, wide)
        last = filter_three[layer]
        high = last.astype(BF16)
        rows = slice(PARAM_ROWS, PARAM_ROWS + BLOCK_W)
        table[rows, 0:128] = high
        table[rows, 128:256] = (last - high.astype(F32)).astype(BF16)
        for at, source in ((GAIN_ONE, gain_one), (GAIN_TWO, gain_two), (SKIP, skip), (DECAY, decay)):
            cols[at : at + 1, :] = source[layer : layer + 1, :]
        cols[TAP_X : TAP_X + 3, :] = taps[layer, :, 0:BLOCK_W]
        cols[TAP_G : TAP_G + 3, :] = taps[layer, :, BLOCK_W : 2 * BLOCK_W]
        cols[MASK : MASK + 1, :] = mask[...]
        left = lax.dot_general(
            cols[...], eye, (((0,), (0,)), ((), ())), precision=HIGHEST, preferred_element_type=F32
        )
        terms = jnp.zeros((BLOCK_W, 128), F32)
        for at in range(3):
            part = left.astype(BF16).astype(F32)
            left = left - part
            terms = terms + (pltpu.roll(part, 16 * at, 1) if at else part)
        table[rows, 256:384] = terms.astype(BF16)
        table[PARAM_ROWS + BLOCK_W : MIX_ROWS, :] = jnp.zeros((MIX_ROWS - PARAM_ROWS - BLOCK_W, 384), BF16)
        own_piece(idx, table, pieces[layer])


def pack_ff_kernel(idx, up_one, up_two, down_one, down_two, table_a, table_b, piece_a, piece_b, lines, wide):
    tables, pieces = (table_a, table_b), (piece_a, piece_b)
    for layer in range(LAYERS):
        table = tables[layer]
        table[UP_ONE : UP_ONE + 192, 0:192] = narrow_lines(up_one, layer, 192, lines, wide)
        table[UP_ONE : UP_ONE + 192, 192:384] = narrow_lines(down_two, layer, 192, lines, wide)
        for j, part in enumerate(spread_lines(up_two, layer, 192, 12, lines)):
            at = UP_TWO + 192 * (j // 3)
            table[at : at + 192, 128 * (j % 3) : 128 * (j % 3) + 128] = part.astype(BF16)
        down = narrow_lines(down_one, layer, 768, lines, wide)
        table[DOWN_ONE : DOWN_ONE + 384, 0:192] = down[0:384]
        table[DOWN_ONE : DOWN_ONE + 384, 192:384] = down[384:768]
        table[FF_USED:FF_ROWS, :] = jnp.zeros((FF_ROWS - FF_USED, 384), BF16)
        own_piece(idx, table, pieces[layer])


def finish_kernel(layer, groups, idx, *refs):
    count = 2 * len(groups)
    pieces, refs = refs[:count], refs[count:]
    names = sum(groups, ())
    with_ff, with_mix = "ff" in names, "conv" in names
    outs = 4 * with_ff + 5 * with_mix
    if layer == 0:
        refs = refs[outs:]
        if with_mix:
            other, refs = refs[0], refs[1:]
    if with_ff:
        up_one, up_two, down_one, down_two = refs[:4]
        refs = refs[4:]
    if with_mix:
        in_one, in_two, out_one, out_two, three = refs[:5]
        refs = refs[5:]
    rest, (ff, conv, inp, wide, sem) = refs[:-5], refs[-5:]
    tables = {"ff": ff, "conv": conv, "in": inp}
    pairs = []
    for at, group in enumerate(groups):
        for core in range(2):
            rel = pieces[2 * at + core]
            first = 0
            for name in group:
                rows = PIECE_ROWS[name]
                for chip in range(4):
                    pairs.append(
                        (rel.at[chip, pl.ds(first, rows), :], tables[name].at[piece_rows(idx, core, chip, rows), :])
                    )
                first += rows
    run_copies(pairs, sem)

    def spread(out, values, lanes, first):
        count = values.shape[0]
        for j in range(3):
            out[pl.ds(first + j, count, stride=lanes), :] = values[:, 128 * j : 128 * j + 128].astype(F32)

    def narrow_of(out, values):
        count = values.shape[0]
        wide[0, 0:count, :] = values[:, 0:128].astype(F32)
        wide[1, 0:count, 0:64] = values[:, 128:192].astype(F32)
        fold_out(wide, out, count)

    if with_ff:
        for q in range(4):
            at = UP_TWO + 192 * q
            spread(up_two, ff[at : at + 192, :], 12, 3 * q)
        narrow_of(up_one, ff[UP_ONE : UP_ONE + 192, 0:192])
        narrow_of(down_two, ff[UP_ONE : UP_ONE + 192, 192:384])
        narrow_of(
            down_one,
            jnp.concatenate([ff[DOWN_ONE : DOWN_ONE + 384, 0:192], ff[DOWN_ONE : DOWN_ONE + 384, 192:384]], axis=0),
        )
    if not with_mix:
        return
    spread(in_one, inp[IN_ONE : IN_ONE + 192, :], 3, 0)
    spread(in_two, inp[IN_TWO : IN_TWO + 384, :], 3, 0)
    narrow_of(out_one, conv[0:192, 0:192])
    narrow_of(out_two, conv[0:192, 192:384])
    three[...] = conv[192:384, 0:128].astype(F32)
    if layer > 0:
        rest[0][0:192, :] = conv[192:384, 128:384].astype(F32)
        rest[0][192:208, :] = inp[576:592, 0:256].astype(F32)
        return
    g_gain_one, g_gain_two, g_skip, g_taps, g_decay, g_mask, g_one, g_bias, g_two = rest
    for at in range(LAYERS):
        if at:
            shared, small, last = other[0:192, 0:128], other[0:32, 128:256], other[192:208, 0:192]
        else:
            shared = conv[192:384, 128:256].astype(F32)
            small = conv[192:224, 256:384].astype(F32)
            last = inp[576:592, 0:192].astype(F32)
        small = jnp.concatenate([small[0:16], small[16:32, 0:64]], axis=1)
        here = slice(at, at + 1)
        g_gain_one[here, :] = last[0:1]
        g_gain_two[here, :] = small[1:2]
        g_skip[here, :] = small[2:3]
        both = jnp.concatenate([small[3:6], small[6:9]], axis=1)
        for tap in range(3):
            g_taps[at, tap, :, :] = both[tap : tap + 1]
        g_decay[here, :] = small[9:10]
        g_two[at] = shared[0:128]
        for row in range(5):
            g_one[row, here, :] = shared[128 + row : 129 + row]
        g_bias[here, :] = shared[133:134]
        if at == 0:
            g_mask[...] = last[1:2]


ANY = pl.BlockSpec(memory_space=pl.ANY)
SCALARS = pl.BlockSpec(memory_space=pltpu.SMEM)
WHOLE = pl.BlockSpec(memory_space=pltpu.VMEM)


def shaped(dtype, *shape):
    return jax.ShapeDtypeStruct(shape, dtype)


EARLY = "early"
LATE = "late"


class Move:
    def __init__(self, buffer, operand, sem, inward):
        self.buffer, self.operand, self.sem, self.inward = buffer, operand, sem, inward
        self.open = []

    def start(self, part=None):
        here = self.buffer if part is None else self.buffer.at[part]
        there = self.operand if part is None else self.operand.at[part]
        pair = (there, here) if self.inward else (here, there)
        copy = pltpu.make_async_copy(*pair, self.sem.at[len(self.open)])
        copy.start()
        self.open.append(copy)

    def wait(self, at=None):
        for n, copy in enumerate(self.open):
            if copy is not None and (at is None or n == at):
                copy.wait()
                self.open[n] = None
        return self.buffer


def call(kernel, outs, scratch, in_specs, out_specs, micros, deps=()):
    outs = list(outs) if isinstance(outs, (list, tuple)) else [outs]
    out_specs = list(out_specs) if isinstance(out_specs, (list, tuple)) else [out_specs]
    ins, own = len(in_specs), len(scratch)
    early = [at for at, spec in enumerate(in_specs) if spec is EARLY]
    late = [at for at, spec in enumerate(out_specs) if spec is LATE]

    def body(*refs):
        inputs = list(refs[:ins])
        refs = refs[ins + len(deps) :]
        results = list(refs[: len(outs)])
        mine, refs = refs[len(outs) : len(outs) + own], refs[len(outs) + own :]
        for j, at in enumerate(early):
            inputs[at] = Move(refs[j], inputs[at], refs[-1].at[j], True)
        for j, at in enumerate(late):
            results[at] = Move(refs[len(early) + j], results[at], refs[-1].at[len(early) + j], False)
        kernel(*inputs, *results, *mine)
        for at in late:
            results[at].wait()

    def run(*arrays):
        buffers = [pltpu.VMEM(arrays[at].shape, arrays[at].dtype) for at in early]
        buffers += [pltpu.VMEM(outs[at].shape, outs[at].dtype) for at in late]
        if buffers:
            buffers.append(pltpu.SemaphoreType.DMA((len(buffers), BLOCKS)))
        made = pl.pallas_call(
            body,
            out_shape=outs,
            in_specs=[ANY if spec is EARLY else spec for spec in in_specs] + [ANY] * len(deps),
            out_specs=[ANY if spec is LATE else spec for spec in out_specs],
            scratch_shapes=list(scratch) + buffers,
            compiler_params=pltpu.CompilerParams(vmem_limit_bytes=58 << 20),
            cost_estimate=pl.CostEstimate(flops=int(micros * 1e9), bytes_accessed=1 << 20, transcendentals=0),
        )(*arrays, *deps)
        return made if len(outs) > 1 else made[0]

    return run


def place_parts_kernel(table, out):
    span = table.shape[2]
    for b in range(BLOCKS):
        out[:, b * span : (b + 1) * span] = table[b].astype(out.dtype)


def wide_shift(x, mask):
    return lax.ppermute(x, "wide", [(i, i ^ mask) for i in range(lax.axis_size("wide"))])


def narrow_shift(x, by):
    narrow = lax.axis_size("narrow")
    return lax.ppermute(x, "narrow", [(i, (i + by) % narrow) for i in range(narrow)])


def added(parts):
    return sum(p.astype(F32) for p in parts).astype(parts[0].dtype)


def after(x, *deps):
    return lax.optimization_barrier((x, deps))[0]


def settle(*trees):
    return lax.optimization_barrier(trees)


def exchange(parts):
    return [parts[0]] + [narrow_shift(parts[k], k) for k in range(1, BLOCKS)]


def over_blocks(piece):
    return jnp.stack([narrow_shift(piece, k) for k in range(1, BLOCKS)])


def others_at_once(pieces, me):
    moved = lax.all_to_all(pieces, "narrow", split_axis=0, concat_axis=0, tiled=True)
    return jnp.stack([lax.dynamic_index_in_dim(moved, (me - k) % BLOCKS, 0, keepdims=False) for k in range(1, BLOCKS)])


def over_chips(x):
    return jnp.stack([x] + [wide_shift(x, 2 * m) for m in range(1, 4)])


def reduce_core(near, far):
    moved = wide_shift(far, 1)
    return [added([near[m], moved[m]]) for m in range(4)]


def move_chips(half):
    return [half[0]] + [wide_shift(half[m], 2 * m) for m in range(1, 4)]


def add_chips(parts):
    total = [added([part[k] for part in parts]) for k in range(BLOCKS)]
    groups = lax.axis_size("wide") // 8
    if groups > 1:
        total = [added([t] + [wide_shift(t, 8 * g) for g in range(1, groups)]) for t in total]
    return total


def reduce_blocks(total):
    return added([total[0]] + [narrow_shift(total[k], -k) for k in range(1, BLOCKS)])


def blocks_at_once(total, me):
    table = jnp.stack(total)
    table = jnp.stack([lax.dynamic_index_in_dim(table, (me - b) % BLOCKS, 0, keepdims=False) for b in range(BLOCKS)])
    moved = lax.all_to_all(table, "narrow", split_axis=0, concat_axis=0, tiled=True)
    return [moved[b] for b in range(BLOCKS)]


def join_rows(*tables):
    return [jnp.concatenate(parts, axis=-2) for parts in zip(*tables)]


def filter_features():
    place = np.arange(2 * LENGTH)
    relative = np.where(place < LENGTH, place, place - 2 * LENGTH) / LENGTH
    table = np.zeros((2 * LENGTH, 128))
    for at, value in enumerate(
        (
            relative,
            np.cos(np.pi * relative),
            np.sin(np.pi * relative),
            np.cos(37.0 * np.pi * relative),
            np.sin(37.0 * np.pi * relative),
            np.ones_like(relative),
        )
    ):
        table[:, at] = value
    return jnp.asarray(table.astype(np.float32))


def filter_hidden(features, weight_one, bias_one, weight_two):
    one = jnp.dot(features[:, :5], weight_one, precision=HIGHEST) + bias_one
    hidden_one = jnp.sin(one)
    two = jnp.dot(hidden_one, weight_two, precision=HIGHEST)
    return jnp.stack([hidden_one, jnp.sin(two), jnp.cos(one), jnp.cos(two)])


def local(
    tokens,
    lengths,
    masked,
    cotangent,
    mask_vector,
    gain_one,
    in_first,
    in_second,
    short_taps,
    skip_gain,
    decay_rates,
    filter_one,
    filter_bias,
    filter_two,
    filter_three,
    out_first,
    out_second,
    gain_two,
    up_first,
    up_second,
    down_first,
    down_second,
):
    wide_count = lax.axis_size("wide")
    me = lax.axis_index("narrow")
    place = lax.axis_index("wide") & 7
    idx = jnp.stack([me, place]).astype(jnp.int32)
    seqs = lengths.shape[0] // BLOCKS
    span = seqs * LENGTH
    all_tokens = tokens.shape[1] * wide_count

    def token_parts(table):
        return [lax.dynamic_slice_in_dim(table, ((me + k) % BLOCKS) * span, span, 1) for k in range(BLOCKS)]

    def flat_lines(weight):
        return weight.reshape(LAYERS, weight.shape[2] // 128, 128)

    factors = [in_first, in_second, out_first, out_second, up_first, up_second, down_first, down_second]
    lines = [flat_lines(weight) for weight in factors]
    tokens_here = exchange(token_parts(tokens))

    def pack(kernel, rows, arrays, deps=(), scratch=()):
        return call(
            kernel,
            [shaped(BF16, rows, 384)] * LAYERS + [shaped(BF16, rows // 8, 384)] * LAYERS,
            [pltpu.VMEM((2304, 128), F32), pltpu.VMEM((2, 768, 128), F32)] + list(scratch),
            [SCALARS] + [WHOLE] * len(arrays),
            [WHOLE] * (2 * LAYERS),
            3,
            deps,
        )(idx, *arrays)

    per_feature = [gain_one, gain_two, skip_gain, short_taps[:, :, 0], mask_vector[None], decay_rates, filter_three]
    *mix, mix_zero, mix_one = pack(
        pack_mix_kernel, MIX_ROWS, lines[:4] + per_feature, scratch=[pltpu.VMEM((16, BLOCK_W), F32)]
    )
    ahead, back = spectrum_tables()
    ahead_low = jnp.asarray(ahead[:LENGTH]).astype(BF16)
    back_low = jnp.asarray(back[:, :LENGTH]).astype(BF16)
    ahead_full = jnp.asarray(ahead)
    features = filter_features()
    back_full = jnp.asarray(back)
    hidden = [
        filter_hidden(features, filter_one[layer], filter_bias[layer], filter_two[layer]) for layer in range(LAYERS)
    ]
    own_lengths = lax.dynamic_slice_in_dim(lengths, me * seqs, seqs, 0)
    own_masked = lax.dynamic_slice_in_dim(masked, me * seqs, seqs, 0)
    positions = jnp.arange(LENGTH, dtype=jnp.int32)
    pad = (positions[None, :] < own_lengths[:, None]).astype(F32).reshape(1, span)
    pad = jnp.broadcast_to(pad, (8, span))
    chosen = jnp.broadcast_to(own_masked.astype(F32).reshape(1, span), (8, span))

    parts = token_parts(tokens)
    near, across = narrow_shift(parts[1], 1), narrow_shift(parts[2], 2)

    mix_zero = others_at_once(jnp.stack([mix_zero] * BLOCKS), me)
    *ff, ff_zero, ff_one = pack(pack_ff_kernel, FF_ROWS, lines[4:], (near, across))
    mix_zero, ff_zero, hidden, near, across, far, pad, chosen = settle(
        mix_zero, ff_zero, hidden, near, across, parts[3], pad, chosen
    )
    far = narrow_shift(far, 3)
    mix_chips = over_chips(mix_zero)
    ff_zero = others_at_once(jnp.stack([ff_zero] * BLOCKS), me)
    one = jnp.stack([jnp.concatenate([mix_one, ff_one], axis=0)] * BLOCKS)
    mix_chips, ff_zero, one, far = settle(mix_chips, ff_zero, one, far)
    mix_zero = (mix[0], mix_chips, wide_shift(mix_chips, 1))
    tokens_here = [parts[0], near, across, far]

    penalty = 4.0 * math.sqrt(all_tokens) / (wide_count * BLOCKS)
    mix_table = shaped(BF16, BLOCKS, MIX_ROWS, 384)
    ff_table = shaped(BF16, BLOCKS, FF_ROWS, 384)
    fetched = pltpu.SemaphoreType.DMA((9,))
    sent = pltpu.SemaphoreType.DMA((8,))
    table_specs = [SCALARS, ANY, ANY, ANY]

    def ahead_mix(layer, table, h, deps=()):
        first = layer == 0
        return call(
            functools.partial(fwd_mix_kernel, first, seqs),
            ([shaped(F32, D, span)] if first else [])
            + [
                shaped(BF16, BLOCKS, 384, span),
                shaped(BF16, BLOCKS, 384, span),
                shaped(BF16, D, span),
                shaped(BF16, D, span),
                shaped(BF16, BLOCKS, 192, span),
                shaped(F32, D, span),
                shaped(F32, 8, span),
                shaped(F32, D, 128),
                shaped(F32, D, 256),
                mix_table,
            ],
            [
                pltpu.VMEM((D, span), BF16),
                pltpu.VMEM((BLOCK_W, span), F32),
                pltpu.VMEM((BLOCK_W, span), F32),
                fetched,
            ],
            table_specs + [WHOLE] * (BLOCKS + 1 if first else 1) + [WHOLE] * 5,
            ([LATE] if first else []) + [LATE] * 4 + [WHOLE] * 5 + [LATE],
            18,
            deps,
        )(idx, *table, *([*h, chosen] if first else [h]), pad, hidden[layer], ahead_full, ahead_low, back_low)

    def ahead_ff(layer, table, middle, cols, deps=()):
        last = layer == LAYERS - 1
        return call(
            functools.partial(fwd_ff_kernel, last),
            [
                shaped(BF16, BLOCKS, 192, span),
                shaped(BF16, BLOCKS, 1536, span),
                shaped(BF16, BLOCKS, 192, span),
                shaped(BF16, BLOCKS, BLOCK_W, span) if last else shaped(F32, D, span),
                shaped(F32, 8, span),
                ff_table,
            ],
            [pltpu.VMEM((D, span), BF16), pltpu.VMEM((FF_BLOCK, span), BF16), fetched],
            table_specs + [WHOLE] * 2,
            [LATE] * 2 + [WHOLE] * 3 + [LATE],
            15,
            deps,
        )(idx, *table, middle, cols)

    saved = []
    mix_zero, tokens_here, ff_zero, one = settle(mix_zero, tokens_here, ff_zero, one)
    ff_chips = over_chips(ff_zero)
    one = others_at_once(one, me)
    h, q1, proj, conv, gated, q2, middle, stats_one, cols, kspec, mix_w = ahead_mix(0, mix_zero, tokens_here)
    parts = token_parts(cotangent)
    middle, ff_chips, one, parts = settle(middle, ff_chips, one, parts)
    ff_zero = (ff[0], ff_chips, wide_shift(ff_chips, 1))
    middle, ff_zero, one, parts = settle(middle, ff_zero, one, parts)
    rows = MIX_ROWS // 8
    mix_chips = over_chips(one[:, :rows])
    near, far = narrow_shift(parts[1], 1), narrow_shift(parts[3], 3)
    q3, gate_up, q4, h_next, stats_two, ff_w = ahead_ff(0, ff_zero, middle, cols)
    saved.append((h, q1, proj, conv, gated, q2, middle, stats_one, cols, kspec, q3, gate_up, q4, stats_two, mix_w, ff_w))
    h, mix_chips, ff_one, near, far, across = settle(h_next, mix_chips, one[:, rows:], near, far, parts[2])
    mix_one = (mix[1], mix_chips, wide_shift(mix_chips, 1))
    h, mix_one, ff_one, across = settle(h, mix_one, ff_one, across)
    ff_chips = over_chips(ff_one)
    across = narrow_shift(across, 2)
    cotangent_here = [parts[0], near, across, far]
    q1, proj, conv, gated, q2, middle, stats_one, cols, kspec, mix_w = ahead_mix(1, mix_one, h)
    middle, ff_chips, cotangent_here = settle(middle, ff_chips, cotangent_here)
    ff_one = (ff[1], ff_chips, wide_shift(ff_chips, 1))
    middle, ff_one = settle(middle, ff_one)
    q3, gate_up, q4, h_last, stats_two, ff_w = ahead_ff(1, ff_one, middle, cols)
    saved.append((h, q1, proj, conv, gated, q2, middle, stats_one, cols, kspec, q3, gate_up, q4, stats_two, mix_w, ff_w))

    sizes = [weight.shape[2] // 128 for weight in factors]

    def finish(layer, names, groups, earlier):
        with_ff, with_mix = "ff" in sum(names, ()), "conv" in sum(names, ())
        shapes = [(LAYERS, size, 128) for size in (sizes[4:] if with_ff else []) + (sizes[:4] if with_mix else [])]
        shapes += [(LAYERS, BLOCK_W, 128)] if with_mix else []
        specs = [pl.BlockSpec((None, *shape[1:]), lambda _: (layer, 0, 0)) for shape in shapes]
        rest = []
        if with_mix and layer:
            rest = [(208, 256)]
        elif with_mix:
            rest = [(LAYERS, BLOCK_W)] * 3 + [(LAYERS, 3, 1, 384), (LAYERS, BLOCK_W), (1, BLOCK_W)]
            rest += [(5, LAYERS, 128), (LAYERS, 128), (LAYERS, 128, 128)]
        specs += [pl.BlockSpec(shape, lambda _, n=len(shape): (0,) * n) for shape in rest]
        arrays = [part for group in groups for part in group]
        inputs = [SCALARS] + [ANY] * (len(arrays) + len(earlier))
        if earlier and with_mix:
            inputs[-1] = pl.BlockSpec(earlier[-1].shape, lambda _: (0, 0))
        return pl.pallas_call(
            functools.partial(finish_kernel, layer, names),
            grid=(1,),
            out_shape=[shaped(F32, *shape) for shape in shapes + rest],
            in_specs=inputs,
            out_specs=specs,
            scratch_shapes=[
                pltpu.VMEM((FF_ROWS, 384), BF16),
                pltpu.VMEM((384, 384), BF16),
                pltpu.VMEM((IN_GRAD_ROWS, 384), BF16),
                pltpu.VMEM((2, 768, 128), F32),
                pltpu.SemaphoreType.DMA((24,)),
            ],
            input_output_aliases={1 + len(arrays) + at: at for at in range(len(shapes))} if earlier else {},
            compiler_params=pltpu.CompilerParams(vmem_limit_bytes=56 << 20),
            cost_estimate=pl.CostEstimate(flops=4 * 10**9, bytes_accessed=1 << 20, transcendentals=0),
        )(idx, *arrays, *earlier)

    def collect(table, dtype):
        return call(place_parts_kernel, shaped(dtype, BLOCK_W, BLOCKS * span), [], [WHOLE], WHOLE, 2)(table)

    def to_blocks(table):
        return lax.all_to_all(table, "narrow", split_axis=0, concat_axis=0, tiled=True)

    def back_ff(layer, g_top, deps):
        last = layer == LAYERS - 1
        h, q1, proj, conv, gated, q2, middle, stats_one, cols, kspec, q3, gate_up, q4, stats_two, mix_w, ff_w = saved[layer]
        return call(
            functools.partial(bwd_ff_kernel, last),
            [shaped(F32, D, span), *[shaped(BF16, 4, BLOCKS, FF_ROWS // 8, 384)] * 2, shaped(F32, BLOCKS, 16, BLOCK_W)],
            [
                pltpu.VMEM((BLOCKS, FF_ROWS, 384), BF16),
                pltpu.VMEM((D, span), BF16),
                pltpu.VMEM((BLOCKS, 192, span), BF16),
                pltpu.VMEM((BLOCKS, 192, span), BF16),
                pltpu.VMEM((2 * FF_BLOCK, span), BF16),
                pltpu.VMEM((D, span), F32),
                sent,
            ],
            [SCALARS, EARLY] + [EARLY] * (BLOCKS if last else 1) + [EARLY] * 4 + [WHOLE, EARLY],
            [LATE, ANY, ANY, WHOLE],
            27,
            deps,
        )(idx, ff_w, *(g_top if last else [g_top]), q4, gate_up, q3, middle, stats_two, cols)

    def back_conv(layer, g_mid, small_ff, deps):
        h, q1, proj, conv, gated, q2, middle, stats_one, cols, kspec, q3, gate_up, q4, stats_two, mix_w, ff_w = saved[layer]
        return call(
            functools.partial(bwd_conv_kernel, seqs, penalty),
            [shaped(BF16, BLOCKS, 384, span), *[shaped(BF16, 4, BLOCKS, 48, 384)] * 2],
            [
                pltpu.VMEM((BLOCKS, 384, 384), BF16),
                pltpu.VMEM((BLOCKS, 192, span), BF16),
                pltpu.VMEM((BLOCK_W, span), F32),
                pltpu.VMEM((BLOCK_W, span), F32),
                sent,
            ],
            [SCALARS, EARLY] + [EARLY] * 5 + [WHOLE] * 2 + [EARLY] + [WHOLE] * 7,
            [LATE, ANY, ANY],
            23,
            deps,
        )(
            idx,
            mix_w,
            g_mid,
            q2,
            gated,
            conv,
            proj,
            pad,
            cols,
            kspec,
            ahead_low,
            back_low,
            small_ff,
            hidden[layer],
            filter_two[layer],
            features,
            back_full,
        )

    def back_in(layer, gv, g_mid, deps):
        first = layer == 0
        h, q1, proj, conv, gated, q2, middle, stats_one, cols, kspec, q3, gate_up, q4, stats_two, mix_w, ff_w = saved[layer]
        return call(
            functools.partial(bwd_in_kernel, first),
            [
                shaped(BF16, BLOCKS, BLOCK_W, span) if first else shaped(F32, D, span),
                *[shaped(BF16, 4, BLOCKS, IN_GRAD_ROWS // 8, 384)] * 2,
            ],
            [
                pltpu.VMEM((BLOCKS, IN_GRAD_ROWS, 384), BF16),
                pltpu.VMEM((BLOCKS, 384, span), BF16),
                pltpu.VMEM((D, span), F32),
                pltpu.VMEM((BLOCKS, 16, BLOCK_W), F32),
                sent,
            ]
            + ([pltpu.VMEM((D, span), F32)] if first else []),
            [SCALARS] + [EARLY] * 5 + [WHOLE] * (3 if first else 2),
            [LATE, ANY, ANY],
            12,
            deps,
        )(idx, mix_w, gv, g_mid, q1, h, stats_one, cols, *([chosen] if first else []))

    def spread(piece):
        chips = over_chips(piece)
        return chips, wide_shift(chips, 1)

    def each_after(arrays, *deps):
        return [after(x, *deps) for x in arrays]

    h_last, cotangent_here = settle(h_last, cotangent_here)
    mixed_parts = to_blocks(h_last)
    g_mid, near, far, small_ff = back_ff(1, cotangent_here, ())
    g_mid, near, far, mixed_parts = settle(g_mid, near, far, mixed_parts)
    mixed_out = collect(mixed_parts, BF16)
    ff_one = reduce_core(near, far)
    gv, near, far = back_conv(1, g_mid, small_ff, (mixed_out,))
    gv, near, far, ff_one = settle(gv, near, far, ff_one)
    conv_one = reduce_core(near, far)
    ff_parts = [ff_one[0], wide_shift(ff_one[1], 2), wide_shift(ff_one[2], 4)]
    g_top, near, far = back_in(1, gv, g_mid, ())
    g_top, near, far, conv_one, ff_parts, last = settle(g_top, near, far, conv_one, ff_parts, ff_one[3])
    near, far = settle(near, reduce_core(near, far))
    mix_parts, g_top = settle(join_rows(conv_one, far), g_top)
    ff_parts = ff_parts + [wide_shift(last, 6)]
    mix_parts = move_chips(mix_parts)
    g_mid, near, far, small_ff = back_ff(0, g_top, ())
    g_mid, near, far, mix_parts, ff_parts = settle(g_mid, near, far, mix_parts, ff_parts)
    all_one, ff_zero = settle(join_rows(add_chips(ff_parts), add_chips(mix_parts)), reduce_core(near, far))
    all_parts = blocks_at_once(all_one, me)
    ff_parts = move_chips(ff_zero)
    gv, near, far = back_conv(0, g_mid, small_ff, ff_zero)
    gv, near, far, all_parts, ff_parts = settle(gv, near, far, all_parts, ff_parts)
    all_one = added(all_parts)
    one_chips = [all_one] + [wide_shift(all_one, 2 * m) for m in range(1, 4)]
    ff_parts = blocks_at_once(add_chips(ff_parts), me)
    conv_zero = reduce_core(near, far)
    g_top, near, far = back_in(0, gv, g_mid, ())
    ff_zero = added(ff_parts)
    g_top, near, far, one_chips, ff_zero, conv_zero = settle(g_top, near, far, one_chips, ff_zero, conv_zero)

    token_grads = to_blocks(g_top)
    in_zero = reduce_core(near, far)
    in_zero, conv_zero, one_chips = settle(in_zero, conv_zero, one_chips)
    mix_parts = move_chips(join_rows(conv_zero, in_zero))
    one_chips = jnp.stack(one_chips)
    one_group = (one_chips, wide_shift(one_chips, 1))
    *flat, table_one = finish(1, (("ff", "conv", "in"),), (one_group,), [])
    ff_chips = over_chips(after(ff_zero, table_one))
    mix_parts, flat, ff_chips = settle(mix_parts, flat, ff_chips)
    mix_zero = reduce_blocks(add_chips(mix_parts))
    ff_group = (ff_chips, wide_shift(ff_chips, 1))
    grad_tokens = collect(token_grads, F32)
    mix_zero, ff_group, grad_tokens = settle(mix_zero, ff_group, grad_tokens)
    flat_ff = finish(0, (("ff",),), (ff_group,), flat[:4])
    mix_chips = over_chips(mix_zero)
    mix_chips, flat_ff = settle(mix_chips, flat_ff)
    mix_group = (mix_chips, wide_shift(mix_chips, 1))
    flat_mix = finish(0, (("conv", "in"),), (mix_group,), [*flat[4:], table_one])
    flat = [*flat_mix[:4], *flat_ff, *flat_mix[4:]]
    grads = [table.reshape(LAYERS, 1, table.shape[1] * 128) for table in flat[:8]]
    three, g_gain_one, g_gain_two, g_skip, g_taps, g_decay, g_mask, g_one, g_bias, g_two = flat[8:]
    return (
        mixed_out,
        grad_tokens,
        g_mask[0],
        g_gain_one,
        grads[0],
        grads[1],
        g_taps,
        g_skip,
        g_decay,
        g_one.transpose(1, 0, 2),
        g_bias,
        g_two,
        three,
        grads[2],
        grads[3],
        g_gain_two,
        grads[4],
        grads[5],
        grads[6],
        grads[7],
    )


def solution(mesh):
    placed = (
        P("narrow", "wide"),
        P("wide"),
        P("wide", None),
        P("narrow", "wide"),
        P("narrow"),
        P(None, "narrow"),
        P(None, "narrow", None),
        P(None, "narrow", None),
        P(None, None, "narrow", None),
        P(None, "narrow"),
        P(None, "narrow"),
        P(),
        P(),
        P(),
        P(None, "narrow", None),
        P(None, "narrow", None),
        P(None, "narrow", None),
        P(None, "narrow"),
        P(None, "narrow", None),
        P(None, "narrow", None),
        P(None, "narrow", None),
        P(None, "narrow", None),
    )
    return jax.shard_map(
        local,
        mesh=mesh,
        in_specs=placed,
        out_specs=(
            P("narrow", "wide"),
            P("narrow", "wide"),
            P("narrow"),
            P(None, "narrow"),
            P(None, "narrow", None),
            P(None, "narrow", None),
            P(None, None, "narrow", None),
            P(None, "narrow"),
            P(None, "narrow"),
            P(),
            P(),
            P(),
            P(None, "narrow", None),
            P(None, "narrow", None),
            P(None, "narrow", None),
            P(None, "narrow"),
            P(None, "narrow", None),
            P(None, "narrow", None),
            P(None, "narrow", None),
            P(None, "narrow", None),
        ),
        check_vma=False,
    )
```

```python
import math
import functools
import numpy as np
import jax
import jax.numpy as jnp
from jax import lax
from jax.experimental import pallas as pl
from jax.experimental.pallas import tpu as pltpu
from jax.sharding import PartitionSpec as P

F32 = jnp.float32
BF16 = jnp.bfloat16
D = 768
LENGTH = 128
LAYERS = 2
BLOCK_W = 192
FF_BLOCK = 768
BLOCKS = 4
EPSILON = 1e-05
HIGHEST = lax.Precision.HIGHEST
GAIN_ONE, GAIN_TWO, SKIP, TAP_X, TAP_G, MASK, DECAY = 0, 1, 2, 3, 6, 9, 10
IN_ONE, IN_TWO, OUT_ROWS, PARAM_ROWS = 0, 192, 576, 768
UP_ONE, UP_TWO, DOWN_ONE = 0, 192, 960
MIX_ROWS, FF_USED, FF_ROWS, IN_GRAD_ROWS = 1024, 1344, 1408, 640
HIDDEN_ONE, HIDDEN_TWO, SLOPE_ONE, SLOPE_TWO = 0, 1, 2, 3
PIECE_ROWS = {"ff": 176, "conv": 48, "in": 80}


def nn(a, b):
    return lax.dot_general(a, b, (((1,), (0,)), ((), ())), preferred_element_type=F32)


def nt(a, b):
    return lax.dot_general(a, b, (((1,), (1,)), ((), ())), preferred_element_type=F32)


def tn(a, b):
    return lax.dot_general(a, b, (((0,), (0,)), ((), ())), preferred_element_type=F32)


def spectrum_tables():
    time = np.arange(2 * LENGTH)
    freq = np.arange(LENGTH)
    angle = 2.0 * np.pi * np.outer(time, freq) / (2 * LENGTH)
    ahead = np.concatenate([np.cos(angle), -np.sin(angle)], axis=1)
    ahead[:, LENGTH] = np.cos(np.pi * time)
    scale = np.full((2 * LENGTH,), 2.0 / (2 * LENGTH))
    scale[0] = scale[LENGTH] = 1.0 / (2 * LENGTH)
    return ahead.astype(np.float32), (ahead * scale[None, :]).T.astype(np.float32)


def lanes_of(shape):
    return lax.broadcasted_iota(jnp.int32, shape, 1)


def column(cols, rows, at, lanes=LENGTH):
    one = jnp.broadcast_to(cols[rows, at : at + 1], (BLOCK_W, LENGTH))
    return one if lanes == LENGTH else jnp.concatenate([one] * (lanes // LENGTH), axis=1)


def later(v, lane):
    return jnp.where(lane == 0, 0.0, pltpu.roll(v, 1, 1))


def earlier(v, lane):
    return jnp.where(lane == LENGTH - 1, 0.0, pltpu.roll(v, LENGTH - 1, 1))


def norm_rows(parts):
    total = sum(jnp.sum(p, axis=0, keepdims=True) for p in parts)
    squares = sum(jnp.sum(p * p, axis=0, keepdims=True) for p in parts)
    mean = total / D
    inv = lax.rsqrt(squares / D - mean * mean + EPSILON)
    return mean, inv


def block(ref, b, width=BLOCK_W):
    return ref[pl.ds(b * width, width), :]


def fwd_mix_kernel(first, seqs, *refs):
    idx, own, rel_a, rel_b, *refs = refs
    if first:
        *parts, chosen_ref = refs[: BLOCKS + 1]
        refs = refs[BLOCKS + 1 :]
    else:
        h_ref, *refs = refs
    pad, hidden, ahead_full, ahead, back, *refs = refs
    if first:
        h_ref, *refs = refs
    q1, proj, conv, gated, q2, middle, stats, cols, kspec, table, normed, xs, gs, sem = refs
    at = distances(idx)
    if not first:
        h_ref.start()
    fetched = fetch_table(idx, own, rel_a, rel_b, table.buffer, sem)
    w = table.buffer
    if first:
        fetched()
        make_params(w, at, hidden, ahead_full, cols, kspec)
        keep = chosen_ref[0:1, :]
        for k, part in enumerate(parts):
            rows = pl.ds(pl.multiple_of(block_of(idx, k) * BLOCK_W, BLOCK_W), BLOCK_W)
            h_ref.buffer[rows, :] = part[...].astype(F32) * (1.0 - keep) + keep * column(cols, rows, MASK, seqs * LENGTH)
        h_ref.start()
        h_ref = h_ref.buffer
    else:
        h_ref = h_ref.wait()
    mean, inv = norm_rows([block(h_ref, b) for b in range(BLOCKS)])
    if not first:
        fetched()
        make_params(w, at, hidden, ahead_full, cols, kspec)
    table.start()
    stats[0:1, :] = mean
    stats[1:2, :] = inv
    for b in range(BLOCKS):
        rows = pl.ds(b * BLOCK_W, BLOCK_W)
        normed[rows, :] = ((h_ref[rows, :] - mean) * inv * column(cols, rows, GAIN_ONE, seqs * LENGTH)).astype(BF16)
    for b in range(BLOCKS):
        inner = tn(w[at[b], IN_ONE : IN_ONE + 192, :], block(normed, b)).astype(BF16)
        for c in range(BLOCKS):
            q1.buffer[c, 96 * b : 96 * b + 96, :] = inner[96 * c : 96 * c + 96]
    q1.start()
    lane = lanes_of((BLOCK_W, LENGTH))
    row_lane = lanes_of((BLOCK_W, LENGTH))
    for c in range(BLOCKS):
        rows = pl.ds(c * BLOCK_W, BLOCK_W)
        value = tn(w[at[c], IN_TWO : IN_TWO + 384, :], q1.buffer[c]) * pad[0:1, :]
        proj.buffer[c] = value.astype(BF16)
        taps = [[column(cols, rows, tap + n) for n in range(3)] for tap in (TAP_X, TAP_G)]
        skip = column(cols, rows, SKIP)
        for s in range(seqs):
            here = slice(s * LENGTH, (s + 1) * LENGTH)
            for part, tap, out in ((0, taps[0], xs), (192, taps[1], gs)):
                v = value[part : part + 192, here]
                out[:, here] = (
                    tap[0] * later(v, lane)
                    + tap[1] * v
                    + tap[2] * earlier(v, lane)
                )
        signal = jnp.concatenate([xs[:, s * LENGTH : (s + 1) * LENGTH] for s in range(seqs)], axis=0)
        spec = nn(signal.astype(BF16), ahead[...])
        k_re = kspec[rows, 0:LENGTH]
        k_im = kspec[rows, LENGTH : 2 * LENGTH]
        k_off = jnp.where(row_lane == 0, 0.0, k_im)
        k_im = jnp.where(row_lane == 0, k_im, k_re)
        made = []
        for s in range(seqs):
            re = spec[s * 192 : s * 192 + 192, 0:LENGTH]
            im = spec[s * 192 : s * 192 + 192, LENGTH : 2 * LENGTH]
            made.append(
                jnp.concatenate([re * k_re - im * k_off, re * k_off + im * k_im], axis=1).astype(BF16)
            )
        y = nn(jnp.concatenate(made, axis=0), back[...])
        for s in range(seqs):
            here = slice(s * LENGTH, (s + 1) * LENGTH)
            value = y[s * 192 : s * 192 + 192] + skip * xs[:, here]
            conv.buffer[rows, here] = value.astype(BF16)
            gated.buffer[rows, here] = (value * gs[:, here]).astype(BF16)
    for part in (proj, conv, gated):
        part.start()
    for b in range(BLOCKS):
        inner = tn(w[at[b], OUT_ROWS : OUT_ROWS + 192, 0:192], block(gated.buffer, b)).astype(BF16)
        for c in range(BLOCKS):
            q2.buffer[c, 48 * b : 48 * b + 48, :] = inner[48 * c : 48 * c + 48]
    q2.start()
    for c in range(BLOCKS):
        rows = pl.ds(c * BLOCK_W, BLOCK_W)
        middle.buffer[rows, :] = h_ref[rows, :] + tn(w[at[c], OUT_ROWS : OUT_ROWS + 192, 192:384], q2.buffer[c])
        middle.start((rows, slice(None)))


def gelu_parts(v):
    inner = math.sqrt(2.0 / math.pi) * (v + 0.044715 * (v * v * v))
    return jnp.tanh(inner)


def fwd_ff_kernel(last, idx, own, rel_a, rel_b, middle, cols, q3, gate_up, q4, h_next, stats, table, normed, act, sem):
    at = distances(idx)
    middle.start()
    cols.start()
    fetched = fetch_table(idx, own, rel_a, rel_b, table.buffer, sem)
    w = table.buffer
    middle, cols = middle.wait(), cols.wait()
    mean, inv = norm_rows([block(middle, b) for b in range(BLOCKS)])
    stats[0:1, :] = mean
    stats[1:2, :] = inv
    for b in range(BLOCKS):
        rows = pl.ds(b * BLOCK_W, BLOCK_W)
        normed[rows, :] = ((middle[rows, :] - mean) * inv * column(cols, rows, GAIN_TWO, middle.shape[1])).astype(BF16)
    fetched()
    table.start()
    for b in range(BLOCKS):
        inner = tn(w[at[b], UP_ONE : UP_ONE + 192, 0:192], block(normed, b)).astype(BF16)
        for c in range(BLOCKS):
            q3.buffer[c, 48 * b : 48 * b + 48, :] = inner[48 * c : 48 * c + 48]
    q3.start()
    for c in range(BLOCKS):
        for half in range(2):
            ups = []
            for piece in (half, half + 2):
                ups.append(tn(w[at[c], UP_TWO + 192 * piece : UP_TWO + 192 * piece + 192, :], q3.buffer[c]))
            gate, up = ups
            gate_up.buffer[c, 384 * half : 384 * half + 384, :] = gate.astype(BF16)
            gate_up.buffer[c, 768 + 384 * half : 768 + 384 * half + 384, :] = up.astype(BF16)
            act[384 * half : 384 * half + 384, :] = (
                0.5 * gate * (1.0 + gelu_parts(gate)) * up
            ).astype(BF16)
        gate_up.start(c)
        inner = (
            tn(w[at[c], DOWN_ONE : DOWN_ONE + 384, 0:192], act[0:384, :])
            + tn(w[at[c], DOWN_ONE : DOWN_ONE + 384, 192:384], act[384:768, :])
        ).astype(BF16)
        for to in range(BLOCKS):
            q4.buffer[to, 48 * c : 48 * c + 48, :] = inner[48 * to : 48 * to + 48]
    q4.start()
    for c in range(BLOCKS):
        rows = pl.ds(c * BLOCK_W, BLOCK_W)
        value = middle[rows, :] + tn(w[at[c], UP_ONE : UP_ONE + 192, 192:384], q4.buffer[c])
        if last:
            h_next.buffer[c] = value.astype(BF16)
            h_next.start(c)
        else:
            h_next.buffer[rows, :] = value
            h_next.start((rows, slice(None)))


def bwd_ff_kernel(last, idx, table, *refs):
    parts = refs[: BLOCKS if last else 1]
    q4, gate_up, q3, middle, stats, cols, g_mid, g_near, g_far, small, g_w, g_low, gi4, gi3, g_gu, g_n, sem = refs[len(parts) :]
    at = distances(idx)
    for part in parts:
        part.start()
    q4.start()
    table.start((slice(None), slice(UP_ONE, UP_ONE + 192)))
    gate_up.start(0)
    table.start((slice(None), slice(DOWN_ONE, FF_USED)))
    table.start((slice(None), slice(UP_TWO, DOWN_ONE)))
    q3.start()
    for b in range(1, BLOCKS):
        gate_up.start(b)
    for part in (middle, cols):
        part.start()
    w = table.buffer
    mean = stats[0:1, :]
    inv = stats[1:2, :]
    if last:
        for k, part in enumerate(parts):
            g_low[pl.ds(pl.multiple_of(block_of(idx, k) * BLOCK_W, BLOCK_W), BLOCK_W), :] = part.wait()[...]
        g_top = g_low
    else:
        g_top = parts[0].wait()
        for c in range(BLOCKS):
            g_low[c * 192 : c * 192 + 192, :] = block(g_top, c).astype(BF16)
    for b in range(BLOCKS):
        g_w[at[b], FF_USED:FF_ROWS, :] = jnp.zeros((FF_ROWS - FF_USED, 384), BF16)
    table.wait(0)
    q4 = q4.wait()
    for c in range(BLOCKS):
        gt = block(g_low, c)
        g_w[at[c], UP_ONE : UP_ONE + 192, 192:384] = nt(q4[c], gt).astype(BF16)
        gq = nn(w[at[c], UP_ONE : UP_ONE + 192, 192:384], gt).astype(BF16)
        for b in range(BLOCKS):
            gi4[b, 48 * c : 48 * c + 48, :] = gq[48 * b : 48 * b + 48]
    rate = math.sqrt(2.0 / math.pi)
    table.wait(1)
    for b in range(BLOCKS):
        gate_up.wait(b)
        if b == 0:
            table.wait()
            q3.wait()
        for half in range(2):
            span = slice(192 * half, 192 * half + 192)
            gate = gate_up.buffer[b, 384 * half : 384 * half + 384, :].astype(F32)
            up = gate_up.buffer[b, 768 + 384 * half : 768 + 384 * half + 384, :].astype(F32)
            ga = nn(w[at[b], DOWN_ONE : DOWN_ONE + 384, span], gi4[b])
            square = gate * gate
            t = jnp.tanh(rate * gate * (1.0 + 0.044715 * square))
            rise = 0.5 * (1.0 + t)
            gelu = gate * rise
            slope = rise + 0.5 * gelu_slope(gate, square, t, rate)
            act = (gelu * up).astype(BF16)
            g_w[at[b], DOWN_ONE : DOWN_ONE + 384, span] = nt(act, gi4[b]).astype(BF16)
            g_gu[384 * half : 384 * half + 384, :] = (ga * up * slope).astype(BF16)
            g_gu[768 + 384 * half : 768 + 384 * half + 384, :] = (ga * gelu).astype(BF16)
        gq = None
        for piece in range(4):
            rows = slice(UP_TWO + 192 * piece, UP_TWO + 192 * piece + 192)
            gg = g_gu[384 * piece : 384 * piece + 384, :]
            g_w[at[b], rows, :] = nt(q3.buffer[b], gg).astype(BF16)
            term = nn(w[at[b], rows, :], gg)
            gq = term if gq is None else gq + term
        gq = gq.astype(BF16)
        for to in range(BLOCKS):
            gi3[to, 48 * b : 48 * b + 48, :] = gq[48 * to : 48 * to + 48]
    finish = send_early(g_w, (g_near, g_far), idx, sem, UP_ONE + 192)
    norm_back(
        at, middle.wait(), mean, inv, cols.wait(), GAIN_TWO, w, slice(UP_ONE, UP_ONE + 192), slice(0, 192), gi3, g_n, g_w, small, 1, g_top, g_mid
    )
    finish()


def gelu_slope(gate, square, t, rate):
    return gate * (1.0 - t * t) * (rate * (1.0 + 3.0 * 0.044715 * square))


def row_sums(place, values):
    lanes = values.shape[1]
    part = values[:, 0:LENGTH]
    for at in range(LENGTH, lanes, LENGTH):
        part = part + values[:, at : at + LENGTH]
    high = part.astype(BF16)
    low = (part - high.astype(F32)).astype(BF16)
    pick = (lax.broadcasted_iota(jnp.int32, (16, LENGTH), 0) == place).astype(F32).astype(BF16)
    return nt(pick, high) + nt(pick, low)


def norm_back(at, h, mean, inv, cols, gain_at, w, w_rows, w_lanes, gi, g_n, g_w, small, place, g_in, g_out):
    plain = cross = 0.0
    for b in range(BLOCKS):
        rows = pl.ds(b * 192, 192)
        gain = column(cols, rows, gain_at, h.shape[1])
        xh = (h[rows, :] - mean) * inv
        gn = nn(w[at[b], w_rows, w_lanes], gi[b])
        g_w[at[b], w_rows, w_lanes] = nt((xh * gain).astype(BF16), gi[b]).astype(BF16)
        gx = gn * xh
        small[b] = row_sums(place, gx)
        g_n[rows, :] = gn * gain
        plain = plain + jnp.sum(gn * gain, axis=0, keepdims=True)
        cross = cross + jnp.sum(gx * gain, axis=0, keepdims=True)
    plain = plain / D
    cross = cross / D
    for b in range(BLOCKS):
        rows = pl.ds(b * 192, 192)
        xh = (h[rows, :] - mean) * inv
        value = g_in[rows, :].astype(F32) + inv * (g_n[rows, :] - plain - xh * cross)
        if isinstance(g_out, Move):
            g_out.buffer[rows, :] = value
            g_out.start((rows, slice(None)))
        else:
            g_out[rows, :] = value


def bwd_conv_kernel(
    seqs, penalty, idx, table, g_mid, q2, gated, conv, proj, pad, cols, kspec, ahead, back, small_ff,
    filt, weight_two, features, back_full, gv, g_near, g_far, g_w, gi2, gcs, xs, sem
):
    at = distances(idx)
    table.start((slice(None), slice(OUT_ROWS, PARAM_ROWS + BLOCK_W)))
    for part in (q2, g_mid, gated, proj, conv, kspec):
        part.start()
    w, q2, g_mid = table.wait(), q2.wait(), g_mid.wait()
    for c in range(BLOCKS):
        gt = block(g_mid, c).astype(BF16)
        g_w[at[c], 0:192, 192:384] = nt(q2[c], gt).astype(BF16)
        gq = nn(w[at[c], OUT_ROWS : OUT_ROWS + 192, 192:384], gt).astype(BF16)
        for b in range(BLOCKS):
            gi2[b, 48 * c : 48 * c + 48, :] = gq[48 * b : 48 * b + 48]
    lane = lanes_of((BLOCK_W, LENGTH))
    first_lane = lane == 0
    for part in (gated, proj, conv):
        part.wait()
    kspec = kspec.wait()
    for b in range(BLOCKS):
        rows = pl.ds(b * 192, 192)
        g_gated = nn(w[at[b], OUT_ROWS : OUT_ROWS + 192, 0:192], gi2[b])
        g_w[at[b], 0:192, 0:192] = nt(block(gated.buffer, b), gi2[b]).astype(BF16)
        tap_x = [column(cols, rows, TAP_X + n) for n in range(3)]
        tap_g = [column(cols, rows, TAP_G + n) for n in range(3)]
        skip = column(cols, rows, SKIP)
        sums = [0.0] * 7
        for s in range(seqs):
            here = slice(s * LENGTH, (s + 1) * LENGTH)
            v = proj.buffer[b, 0:192, here].astype(F32)
            xs[:, here] = (
                tap_x[0] * later(v, lane)
                + tap_x[1] * v
                + tap_x[2] * earlier(v, lane)
            )
            v = proj.buffer[b, 192:384, here].astype(F32)
            after, before = later(v, lane), earlier(v, lane)
            gate = (
                tap_g[0] * after
                + tap_g[1] * v
                + tap_g[2] * before
            )
            gg = g_gated[:, here]
            gcs[:, here] = gg * gate
            z = gg * conv.buffer[rows, here].astype(F32)
            sums[4] = sums[4] + z * after
            sums[5] = sums[5] + z * v
            sums[6] = sums[6] + z * before
            gv.buffer[b, 192:384, here] = (
                (
                    tap_g[0] * earlier(z, lane)
                    + tap_g[1] * z
                    + tap_g[2] * later(z, lane)
                )
                * pad[0:1, here]
            ).astype(BF16)
            sums[0] = sums[0] + gcs[:, here] * xs[:, here]
        stacked = jnp.concatenate(
            [ref[:, s * LENGTH : (s + 1) * LENGTH] for ref in (xs, gcs) for s in range(seqs)], axis=0
        )
        spec = nn(stacked.astype(BF16), ahead[...])
        k_re = kspec[rows, 0:LENGTH]
        k_im = kspec[rows, LENGTH : 2 * LENGTH]
        k_off = jnp.where(first_lane, 0.0, k_im)
        k_im = jnp.where(first_lane, k_im, k_re)
        made = []
        p_re = p_im = p_off = 0.0
        for s in range(seqs):
            x_re = spec[s * 192 : s * 192 + 192, 0:LENGTH]
            x_im = spec[s * 192 : s * 192 + 192, LENGTH : 2 * LENGTH]
            start = (seqs + s) * 192
            g_re = spec[start : start + 192, 0:LENGTH]
            g_im = spec[start : start + 192, LENGTH : 2 * LENGTH]
            p_re = p_re + g_re * x_re
            p_im = p_im + g_im * x_im
            p_off = p_off + (g_im * x_re - g_re * x_im)
            made.append(
                jnp.concatenate([g_re * k_re + g_im * k_off, g_im * k_im - g_re * k_off], axis=1).astype(BF16)
            )
        g_table = exact(
            jnp.concatenate(
                [jnp.where(first_lane, p_re, p_re + p_im), jnp.where(first_lane, p_im, p_off)], axis=1
            ),
            back_full[...],
            1,
            0,
        )
        last, envelope, kernel = filter_values(w, at, b, cols, filt[HIDDEN_TWO])
        g_table = g_table + penalty * kernel
        g_decay = -(g_table * kernel * filter_lag())
        g_shape = g_table * envelope
        g_w[at[b], 192:384, 0:128] = exact(g_shape, filt[HIDDEN_TWO], 1, 0).astype(BF16)
        term = exact(g_shape, last, 0, 0)
        g_hidden = term if b == 0 else g_hidden + term
        y = nn(jnp.concatenate(made, axis=0), back[...])
        for s in range(seqs):
            here = slice(s * LENGTH, (s + 1) * LENGTH)
            z = y[s * 192 : s * 192 + 192] + skip * gcs[:, here]
            v = proj.buffer[b, 0:192, here].astype(F32)
            sums[1] = sums[1] + z * later(v, lane)
            sums[2] = sums[2] + z * v
            sums[3] = sums[3] + z * earlier(v, lane)
            gv.buffer[b, 0:192, here] = (
                (
                    tap_x[0] * earlier(z, lane)
                    + tap_x[1] * z
                    + tap_x[2] * later(z, lane)
                )
                * pad[0:1, here]
            ).astype(BF16)
        gv.start(b)
        totals = small_ff[b]
        for place, value in enumerate(sums + [g_decay]):
            totals = totals + row_sums(2 + place, value)
        totals = totals.astype(BF16)
        g_w[at[b], 192:208, 256:384] = totals[:, 0:128]
        g_w[at[b], 208:224, 256:320] = totals[:, 128:192]
        g_w[at[b], 208:224, 320:384] = jnp.zeros((16, 64), BF16)
        g_w[at[b], 224:384, 256:384] = jnp.zeros((160, 128), BF16)
    g_two = g_hidden * filt[SLOPE_TWO]
    g_one = exact(g_two, weight_two[...], 1, 1) * filt[SLOPE_ONE]
    g_weight_two = exact(filt[HIDDEN_ONE], g_two, 0, 0).astype(BF16)
    g_weight_one = exact(features[...], g_one, 0, 0)[0:16, :].astype(BF16)
    for b in range(BLOCKS):
        g_w[at[b], 192:320, 128:256] = g_weight_two
        g_w[at[b], 320:336, 128:256] = g_weight_one
        g_w[at[b], 336:384, 128:256] = jnp.zeros((48, 128), BF16)
    send_pieces(g_w, (g_near, g_far), idx, sem)


def bwd_in_kernel(first, *refs):
    refs = list(refs)
    idx, table, gv, g_mid, q1, h, stats, cols = refs[:8]
    refs = refs[8:]
    chosen = refs.pop(0) if first else None
    g_out, g_near, g_far, g_w, gi1, g_n, small, sem = refs[:8]
    g_h = refs[8] if first else g_out
    at = distances(idx)
    for c in range(BLOCKS):
        gv.start(c)
        q1.start(c)
        if c == 0:
            table.start((slice(None), slice(IN_ONE, OUT_ROWS)))
    for part in (h, g_mid):
        part.start()
    w = table.wait()
    mean = stats[0:1, :]
    inv = stats[1:2, :]
    for c in range(BLOCKS):
        gv.wait(c)
        q1.wait(c)
        g_w[at[c], IN_TWO : IN_TWO + 384, :] = nt(q1.buffer[c], gv.buffer[c]).astype(BF16)
        gq = nn(w[at[c], IN_TWO : IN_TWO + 384, :], gv.buffer[c]).astype(BF16)
        for b in range(BLOCKS):
            gi1[b, 96 * c : 96 * c + 96, :] = gq[96 * b : 96 * b + 96]
    norm_back(
        at, h.wait(), mean, inv, cols, GAIN_ONE, w, slice(IN_ONE, IN_ONE + 192), slice(0, 384), gi1, g_n, g_w, small, 0, g_mid.wait(), g_h
    )
    for b in range(BLOCKS):
        rows = pl.ds(b * 192, 192)
        totals = small[b]
        if first:
            value = g_h[rows, :]
            masked = value * chosen[0:1, :]
            totals = totals + row_sums(1, masked)
            ahead_by = (b - idx[0]) & (BLOCKS - 1)
            g_out.buffer[ahead_by] = (value - masked).astype(BF16)
            g_out.start(ahead_by)
        g_w[at[b], 576:592, 0:192] = totals.astype(BF16)
        g_w[at[b], 576:592, 192:384] = jnp.zeros((16, 192), BF16)
        g_w[at[b], 592:640, :] = jnp.zeros((48, 384), BF16)
    send_pieces(g_w, (g_near, g_far), idx, sem)


def piece_rows(idx, core, chip, rows):
    return pl.ds(pl.multiple_of((idx[1] ^ (2 * chip + core)) * rows, 16), rows)


def block_of(idx, k):
    return (idx[0] - k) & (BLOCKS - 1)


def distances(idx):
    return [(idx[0] - b) & (BLOCKS - 1) for b in range(BLOCKS)]


def start_copies(pairs, sem):
    copies = [pltpu.make_async_copy(source, target, sem.at[at]) for at, (source, target) in enumerate(pairs)]
    for copy in copies:
        copy.start()

    def wait():
        for copy in copies:
            copy.wait()

    return wait


def run_copies(pairs, sem):
    start_copies(pairs, sem)()


def send_early(table, outs, idx, sem, done):
    rows = outs[0].shape[2]
    late = -(-done // rows)
    copies = []
    for core in range(2):
        for chip in range(4):
            at = idx[1] ^ (2 * chip + core)
            copy = pltpu.make_async_copy(
                table.at[:, piece_rows(idx, core, chip, rows), :], outs[core].at[chip], sem.at[len(copies)]
            )
            pl.when(at >= late)(copy.start)
            copies.append((at, copy))

    def finish():
        for at, copy in copies:
            pl.when(at < late)(copy.start)
        for _, copy in copies:
            copy.wait()

    return finish


def send_pieces(table, outs, idx, sem):
    rows = outs[0].shape[2]
    run_copies(
        [(table.at[:, piece_rows(idx, core, chip, rows), :], outs[core].at[chip]) for core in range(2) for chip in range(4)],
        sem,
    )


def fetch_table(idx, own, rel_a, rel_b, table, sem):
    rows = rel_a.shape[2]
    return start_copies(
        [(own, table.at[0])]
        + [
            (rel.at[chip], table.at[1:BLOCKS, piece_rows(idx, core, chip, rows), :])
            for core, rel in enumerate((rel_a, rel_b))
            for chip in range(4)
        ],
        sem,
    )


def exact(a, b, left, right):
    return lax.dot_general(
        a, b, (((left,), (right,)), ((), ())), precision=HIGHEST, preferred_element_type=F32
    )


def filter_lag():
    place = lanes_of((BLOCK_W, 2 * LENGTH))
    return jnp.where(place < LENGTH, place, 2 * LENGTH - place).astype(F32)


def filter_values(w, at, b, cols, hidden):
    packed = w[at[b], PARAM_ROWS : PARAM_ROWS + BLOCK_W, 0:256].astype(F32)
    last = packed[:, 0:128] + packed[:, 128:256]
    lag = filter_lag()
    envelope = jnp.exp(-lag * cols[b * BLOCK_W : (b + 1) * BLOCK_W, DECAY : DECAY + 1]) * (1.0 / math.sqrt(LENGTH))
    envelope = jnp.where(lag == LENGTH, 0.0, envelope)
    return last, envelope, exact(last, hidden, 1, 1) * envelope


def make_params(w, at, hidden, ahead_full, cols, kspec):
    for b in range(BLOCKS):
        rows = pl.ds(b * BLOCK_W, BLOCK_W)
        three = w[at[b], PARAM_ROWS : PARAM_ROWS + BLOCK_W, 256:384].astype(F32)
        cols[rows, :] = three + pltpu.roll(three, 128 - 16, 1) + pltpu.roll(three, 128 - 32, 1)
        kspec[rows, :] = exact(filter_values(w, at, b, cols, hidden[HIDDEN_TWO])[2], ahead_full[...], 1, 0)


def fold_back(lines, wide, count):
    low = lanes_of((count // 2, 128)) < 64
    one, two, three = (lines[pl.ds(j, count // 2, stride=3), :] for j in range(3))
    three = pltpu.roll(three, 64, 1)
    wide[0, pl.ds(0, count // 2, stride=2), :] = one
    wide[1, pl.ds(0, count // 2, stride=2), :] = two
    wide[0, pl.ds(1, count // 2, stride=2), :] = jnp.where(low, pltpu.roll(two, 64, 1), three)
    wide[1, pl.ds(1, count // 2, stride=2), :] = three


def fold_out(wide, out, count):
    low = lanes_of((count // 2, 128)) < 64
    half = count // 2
    even_a = wide[0, pl.ds(0, half, stride=2), :]
    even_b = wide[1, pl.ds(0, half, stride=2), :]
    odd_a = pltpu.roll(wide[0, pl.ds(1, half, stride=2), :], 64, 1)
    odd_b = pltpu.roll(wide[1, pl.ds(1, half, stride=2), :], 64, 1)
    out[pl.ds(0, half, stride=3), :] = even_a
    out[pl.ds(1, half, stride=3), :] = jnp.where(low, even_b, odd_a)
    out[pl.ds(2, half, stride=3), :] = jnp.where(low, odd_a, odd_b)


def spread_lines(flat, layer, count, lanes, lines):
    rows = flat.shape[1]
    lines[0:rows, :] = flat[layer].astype(F32)
    return [lines[pl.ds(j, count, stride=lanes), :] for j in range(lanes)]


def narrow_lines(flat, layer, count, lines, wide):
    rows = flat.shape[1]
    lines[0:rows, :] = flat[layer].astype(F32)
    fold_back(lines, wide, count)
    return jnp.concatenate([wide[0, 0:count, :], wide[1, 0:count, 0:64]], axis=1).astype(BF16)


def own_piece(idx, table, out):
    rows = out.shape[0]
    out[...] = table[pl.ds(pl.multiple_of(idx[1] * rows, 16), rows), :]


def pack_mix_kernel(
    idx, in_one, in_two, out_one, out_two, gain_one, gain_two, skip, taps, mask, decay, filter_three,
    table_a, table_b, piece_a, piece_b, lines, wide, cols,
):
    tables, pieces = (table_a, table_b), (piece_a, piece_b)
    eye = (
        lax.broadcasted_iota(jnp.int32, (16, 128), 0) == lax.broadcasted_iota(jnp.int32, (16, 128), 1)
    ).astype(F32)
    cols[...] = jnp.zeros((16, BLOCK_W), F32)
    for layer in range(LAYERS):
        table = tables[layer]
        for flat, start, count in ((in_one, IN_ONE, 192), (in_two, IN_TWO, 384)):
            for j, part in enumerate(spread_lines(flat, layer, count, 3, lines)):
                table[start : start + count, 128 * j : 128 * j + 128] = part.astype(BF16)
        table[OUT_ROWS : OUT_ROWS + 192, 0:192] = narrow_lines(out_one, layer, 192, lines, wide)
        table[OUT_ROWS : OUT_ROWS + 192, 192:384] = narrow_lines(out_two, layer, 192, lines, wide)
        last = filter_three[layer]
        high = last.astype(BF16)
        rows = slice(PARAM_ROWS, PARAM_ROWS + BLOCK_W)
        table[rows, 0:128] = high
        table[rows, 128:256] = (last - high.astype(F32)).astype(BF16)
        for at, source in ((GAIN_ONE, gain_one), (GAIN_TWO, gain_two), (SKIP, skip), (DECAY, decay)):
            cols[at : at + 1, :] = source[layer : layer + 1, :]
        cols[TAP_X : TAP_X + 3, :] = taps[layer, :, 0:BLOCK_W]
        cols[TAP_G : TAP_G + 3, :] = taps[layer, :, BLOCK_W : 2 * BLOCK_W]
        cols[MASK : MASK + 1, :] = mask[...]
        left = lax.dot_general(
            cols[...], eye, (((0,), (0,)), ((), ())), precision=HIGHEST, preferred_element_type=F32
        )
        terms = jnp.zeros((BLOCK_W, 128), F32)
        for at in range(3):
            part = left.astype(BF16).astype(F32)
            left = left - part
            terms = terms + (pltpu.roll(part, 16 * at, 1) if at else part)
        table[rows, 256:384] = terms.astype(BF16)
        table[PARAM_ROWS + BLOCK_W : MIX_ROWS, :] = jnp.zeros((MIX_ROWS - PARAM_ROWS - BLOCK_W, 384), BF16)
        own_piece(idx, table, pieces[layer])


def pack_ff_kernel(idx, up_one, up_two, down_one, down_two, table_a, table_b, piece_a, piece_b, lines, wide):
    tables, pieces = (table_a, table_b), (piece_a, piece_b)
    for layer in range(LAYERS):
        table = tables[layer]
        table[UP_ONE : UP_ONE + 192, 0:192] = narrow_lines(up_one, layer, 192, lines, wide)
        table[UP_ONE : UP_ONE + 192, 192:384] = narrow_lines(down_two, layer, 192, lines, wide)
        for j, part in enumerate(spread_lines(up_two, layer, 192, 12, lines)):
            at = UP_TWO + 192 * (j // 3)
            table[at : at + 192, 128 * (j % 3) : 128 * (j % 3) + 128] = part.astype(BF16)
        down = narrow_lines(down_one, layer, 768, lines, wide)
        table[DOWN_ONE : DOWN_ONE + 384, 0:192] = down[0:384]
        table[DOWN_ONE : DOWN_ONE + 384, 192:384] = down[384:768]
        table[FF_USED:FF_ROWS, :] = jnp.zeros((FF_ROWS - FF_USED, 384), BF16)
        own_piece(idx, table, pieces[layer])


def finish_kernel(layer, groups, idx, *refs):
    count = 2 * len(groups)
    pieces, refs = refs[:count], refs[count:]
    names = sum(groups, ())
    with_ff, with_mix = "ff" in names, "conv" in names
    outs = 4 * with_ff + 5 * with_mix
    if layer == 0:
        refs = refs[outs:]
        if with_mix:
            other, refs = refs[0], refs[1:]
    if with_ff:
        up_one, up_two, down_one, down_two = refs[:4]
        refs = refs[4:]
    if with_mix:
        in_one, in_two, out_one, out_two, three = refs[:5]
        refs = refs[5:]
    rest, (ff, conv, inp, wide, sem) = refs[:-5], refs[-5:]
    tables = {"ff": ff, "conv": conv, "in": inp}
    pairs = []
    for at, group in enumerate(groups):
        for core in range(2):
            rel = pieces[2 * at + core]
            first = 0
            for name in group:
                rows = PIECE_ROWS[name]
                for chip in range(4):
                    pairs.append(
                        (rel.at[chip, pl.ds(first, rows), :], tables[name].at[piece_rows(idx, core, chip, rows), :])
                    )
                first += rows
    run_copies(pairs, sem)

    def spread(out, values, lanes, first):
        count = values.shape[0]
        for j in range(3):
            out[pl.ds(first + j, count, stride=lanes), :] = values[:, 128 * j : 128 * j + 128].astype(F32)

    def narrow_of(out, values):
        count = values.shape[0]
        wide[0, 0:count, :] = values[:, 0:128].astype(F32)
        wide[1, 0:count, 0:64] = values[:, 128:192].astype(F32)
        fold_out(wide, out, count)

    if with_ff:
        for q in range(4):
            at = UP_TWO + 192 * q
            spread(up_two, ff[at : at + 192, :], 12, 3 * q)
        narrow_of(up_one, ff[UP_ONE : UP_ONE + 192, 0:192])
        narrow_of(down_two, ff[UP_ONE : UP_ONE + 192, 192:384])
        narrow_of(
            down_one,
            jnp.concatenate([ff[DOWN_ONE : DOWN_ONE + 384, 0:192], ff[DOWN_ONE : DOWN_ONE + 384, 192:384]], axis=0),
        )
    if not with_mix:
        return
    spread(in_one, inp[IN_ONE : IN_ONE + 192, :], 3, 0)
    spread(in_two, inp[IN_TWO : IN_TWO + 384, :], 3, 0)
    narrow_of(out_one, conv[0:192, 0:192])
    narrow_of(out_two, conv[0:192, 192:384])
    three[...] = conv[192:384, 0:128].astype(F32)
    if layer > 0:
        rest[0][0:192, :] = conv[192:384, 128:384].astype(F32)
        rest[0][192:208, :] = inp[576:592, 0:256].astype(F32)
        return
    g_gain_one, g_gain_two, g_skip, g_taps, g_decay, g_mask, g_one, g_bias, g_two = rest
    for at in range(LAYERS):
        if at:
            shared, small, last = other[0:192, 0:128], other[0:32, 128:256], other[192:208, 0:192]
        else:
            shared = conv[192:384, 128:256].astype(F32)
            small = conv[192:224, 256:384].astype(F32)
            last = inp[576:592, 0:192].astype(F32)
        small = jnp.concatenate([small[0:16], small[16:32, 0:64]], axis=1)
        here = slice(at, at + 1)
        g_gain_one[here, :] = last[0:1]
        g_gain_two[here, :] = small[1:2]
        g_skip[here, :] = small[2:3]
        both = jnp.concatenate([small[3:6], small[6:9]], axis=1)
        for tap in range(3):
            g_taps[at, tap, :, :] = both[tap : tap + 1]
        g_decay[here, :] = small[9:10]
        g_two[at] = shared[0:128]
        for row in range(5):
            g_one[row, here, :] = shared[128 + row : 129 + row]
        g_bias[here, :] = shared[133:134]
        if at == 0:
            g_mask[...] = last[1:2]


ANY = pl.BlockSpec(memory_space=pl.ANY)
SCALARS = pl.BlockSpec(memory_space=pltpu.SMEM)
WHOLE = pl.BlockSpec(memory_space=pltpu.VMEM)


def shaped(dtype, *shape):
    return jax.ShapeDtypeStruct(shape, dtype)


EARLY = "early"
LATE = "late"


class Move:
    def __init__(self, buffer, operand, sem, inward):
        self.buffer, self.operand, self.sem, self.inward = buffer, operand, sem, inward
        self.open = []

    def start(self, part=None):
        here = self.buffer if part is None else self.buffer.at[part]
        there = self.operand if part is None else self.operand.at[part]
        pair = (there, here) if self.inward else (here, there)
        copy = pltpu.make_async_copy(*pair, self.sem.at[len(self.open)])
        copy.start()
        self.open.append(copy)

    def wait(self, at=None):
        for n, copy in enumerate(self.open):
            if copy is not None and (at is None or n == at):
                copy.wait()
                self.open[n] = None
        return self.buffer


def call(kernel, outs, scratch, in_specs, out_specs, micros, deps=()):
    outs = list(outs) if isinstance(outs, (list, tuple)) else [outs]
    out_specs = list(out_specs) if isinstance(out_specs, (list, tuple)) else [out_specs]
    ins, own = len(in_specs), len(scratch)
    early = [at for at, spec in enumerate(in_specs) if spec is EARLY]
    late = [at for at, spec in enumerate(out_specs) if spec is LATE]

    def body(*refs):
        inputs = list(refs[:ins])
        refs = refs[ins + len(deps) :]
        results = list(refs[: len(outs)])
        mine, refs = refs[len(outs) : len(outs) + own], refs[len(outs) + own :]
        for j, at in enumerate(early):
            inputs[at] = Move(refs[j], inputs[at], refs[-1].at[j], True)
        for j, at in enumerate(late):
            results[at] = Move(refs[len(early) + j], results[at], refs[-1].at[len(early) + j], False)
        kernel(*inputs, *results, *mine)
        for at in late:
            results[at].wait()

    def run(*arrays):
        buffers = [pltpu.VMEM(arrays[at].shape, arrays[at].dtype) for at in early]
        buffers += [pltpu.VMEM(outs[at].shape, outs[at].dtype) for at in late]
        if buffers:
            buffers.append(pltpu.SemaphoreType.DMA((len(buffers), BLOCKS)))
        made = pl.pallas_call(
            body,
            out_shape=outs,
            in_specs=[ANY if spec is EARLY else spec for spec in in_specs] + [ANY] * len(deps),
            out_specs=[ANY if spec is LATE else spec for spec in out_specs],
            scratch_shapes=list(scratch) + buffers,
            compiler_params=pltpu.CompilerParams(vmem_limit_bytes=58 << 20),
            cost_estimate=pl.CostEstimate(flops=int(micros * 1e9), bytes_accessed=1 << 20, transcendentals=0),
        )(*arrays, *deps)
        return made if len(outs) > 1 else made[0]

    return run


def place_distances_kernel(idx, *refs):
    parts, out = refs[:BLOCKS], refs[BLOCKS]
    span = parts[0].shape[1]
    for k, part in enumerate(parts):
        out[:, pl.ds(pl.multiple_of(block_of(idx, k) * span, 128), span)] = part[...].astype(out.dtype)


def place_parts_kernel(table, out):
    span = table.shape[2]
    for b in range(BLOCKS):
        out[:, b * span : (b + 1) * span] = table[b].astype(out.dtype)


def wide_shift(x, mask):
    return lax.ppermute(x, "wide", [(i, i ^ mask) for i in range(lax.axis_size("wide"))])


def narrow_shift(x, by):
    narrow = lax.axis_size("narrow")
    return lax.ppermute(x, "narrow", [(i, (i + by) % narrow) for i in range(narrow)])


def added(parts):
    return sum(p.astype(F32) for p in parts).astype(parts[0].dtype)


def after(x, *deps):
    return lax.optimization_barrier((x, deps))[0]


def settle(*trees):
    return lax.optimization_barrier(trees)


def exchange(parts):
    return [parts[0]] + [narrow_shift(parts[k], k) for k in range(1, BLOCKS)]


def over_blocks(piece):
    return jnp.stack([narrow_shift(piece, k) for k in range(1, BLOCKS)])


def others_at_once(pieces, me):
    moved = lax.all_to_all(pieces, "narrow", split_axis=0, concat_axis=0, tiled=True)
    return jnp.stack([lax.dynamic_index_in_dim(moved, (me - k) % BLOCKS, 0, keepdims=False) for k in range(1, BLOCKS)])


def over_chips(x):
    return jnp.stack([x] + [wide_shift(x, 2 * m) for m in range(1, 4)])


def reduce_core(near, far):
    moved = wide_shift(far, 1)
    return [added([near[m], moved[m]]) for m in range(4)]


def move_chips(half):
    return [half[0]] + [wide_shift(half[m], 2 * m) for m in range(1, 4)]


def add_chips(parts):
    total = [added([part[k] for part in parts]) for k in range(BLOCKS)]
    groups = lax.axis_size("wide") // 8
    if groups > 1:
        total = [added([t] + [wide_shift(t, 8 * g) for g in range(1, groups)]) for t in total]
    return total


def reduce_blocks(total):
    return added([total[0]] + [narrow_shift(total[k], -k) for k in range(1, BLOCKS)])


def in_order(total, me):
    table = jnp.stack(total)
    return jnp.stack([lax.dynamic_index_in_dim(table, (me - b) % BLOCKS, 0, keepdims=False) for b in range(BLOCKS)])


def blocks_at_once(table):
    moved = lax.all_to_all(table, "narrow", split_axis=0, concat_axis=0, tiled=True)
    return [moved[b] for b in range(BLOCKS)]


def join_rows(*tables):
    return [jnp.concatenate(parts, axis=-2) for parts in zip(*tables)]


def filter_features():
    place = np.arange(2 * LENGTH)
    relative = np.where(place < LENGTH, place, place - 2 * LENGTH) / LENGTH
    table = np.zeros((2 * LENGTH, 128))
    for at, value in enumerate(
        (
            relative,
            np.cos(np.pi * relative),
            np.sin(np.pi * relative),
            np.cos(37.0 * np.pi * relative),
            np.sin(37.0 * np.pi * relative),
            np.ones_like(relative),
        )
    ):
        table[:, at] = value
    return jnp.asarray(table.astype(np.float32))


def filter_hidden(features, weight_one, bias_one, weight_two):
    one = jnp.dot(features[:, :5], weight_one, precision=HIGHEST) + bias_one
    hidden_one = jnp.sin(one)
    two = jnp.dot(hidden_one, weight_two, precision=HIGHEST)
    return jnp.stack([hidden_one, jnp.sin(two), jnp.cos(one), jnp.cos(two)])


def local(
    tokens,
    lengths,
    masked,
    cotangent,
    mask_vector,
    gain_one,
    in_first,
    in_second,
    short_taps,
    skip_gain,
    decay_rates,
    filter_one,
    filter_bias,
    filter_two,
    filter_three,
    out_first,
    out_second,
    gain_two,
    up_first,
    up_second,
    down_first,
    down_second,
):
    wide_count = lax.axis_size("wide")
    me = lax.axis_index("narrow")
    place = lax.axis_index("wide") & 7
    idx = jnp.stack([me, place]).astype(jnp.int32)
    seqs = lengths.shape[0] // BLOCKS
    span = seqs * LENGTH
    all_tokens = tokens.shape[1] * wide_count

    def token_parts(table):
        return [lax.dynamic_slice_in_dim(table, ((me + k) % BLOCKS) * span, span, 1) for k in range(BLOCKS)]

    def flat_lines(weight):
        return weight.reshape(LAYERS, weight.shape[2] // 128, 128)

    factors = [in_first, in_second, out_first, out_second, up_first, up_second, down_first, down_second]
    lines = [flat_lines(weight) for weight in factors]
    tokens_here = exchange(token_parts(tokens))

    def pack(kernel, rows, arrays, deps=(), scratch=()):
        return call(
            kernel,
            [shaped(BF16, rows, 384)] * LAYERS + [shaped(BF16, rows // 8, 384)] * LAYERS,
            [pltpu.VMEM((2304, 128), F32), pltpu.VMEM((2, 768, 128), F32)] + list(scratch),
            [SCALARS] + [WHOLE] * len(arrays),
            [WHOLE] * (2 * LAYERS),
            3,
            deps,
        )(idx, *arrays)

    per_feature = [gain_one, gain_two, skip_gain, short_taps[:, :, 0], mask_vector[None], decay_rates, filter_three]
    *mix, mix_zero, mix_one = pack(
        pack_mix_kernel, MIX_ROWS, lines[:4] + per_feature, scratch=[pltpu.VMEM((16, BLOCK_W), F32)]
    )
    ahead, back = spectrum_tables()
    ahead_low = jnp.asarray(ahead[:LENGTH]).astype(BF16)
    back_low = jnp.asarray(back[:, :LENGTH]).astype(BF16)
    ahead_full = jnp.asarray(ahead)
    features = filter_features()
    back_full = jnp.asarray(back)
    hidden = [
        filter_hidden(features, filter_one[layer], filter_bias[layer], filter_two[layer]) for layer in range(LAYERS)
    ]
    own_lengths = lax.dynamic_slice_in_dim(lengths, me * seqs, seqs, 0)
    own_masked = lax.dynamic_slice_in_dim(masked, me * seqs, seqs, 0)
    positions = jnp.arange(LENGTH, dtype=jnp.int32)
    pad = (positions[None, :] < own_lengths[:, None]).astype(F32).reshape(1, span)
    pad = jnp.broadcast_to(pad, (8, span))
    chosen = jnp.broadcast_to(own_masked.astype(F32).reshape(1, span), (8, span))

    parts = token_parts(tokens)
    near, across = narrow_shift(parts[1], 1), narrow_shift(parts[2], 2)

    mix_zero = others_at_once(jnp.stack([mix_zero] * BLOCKS), me)
    *ff, ff_zero, ff_one = pack(pack_ff_kernel, FF_ROWS, lines[4:], (near, across))
    mix_zero, ff_zero, hidden, near, across, far, pad, chosen = settle(
        mix_zero, ff_zero, hidden, near, across, parts[3], pad, chosen
    )
    far = narrow_shift(far, 3)
    mix_chips = over_chips(mix_zero)
    ff_zero = others_at_once(jnp.stack([ff_zero] * BLOCKS), me)
    one = jnp.stack([jnp.concatenate([mix_one, ff_one], axis=0)] * BLOCKS)
    mix_chips, ff_zero, one, far = settle(mix_chips, ff_zero, one, far)
    mix_zero = (mix[0], mix_chips, wide_shift(mix_chips, 1))
    tokens_here = [parts[0], near, across, far]

    penalty = 4.0 * math.sqrt(all_tokens) / (wide_count * BLOCKS)
    mix_table = shaped(BF16, BLOCKS, MIX_ROWS, 384)
    ff_table = shaped(BF16, BLOCKS, FF_ROWS, 384)
    fetched = pltpu.SemaphoreType.DMA((9,))
    sent = pltpu.SemaphoreType.DMA((8,))
    table_specs = [SCALARS, ANY, ANY, ANY]

    def ahead_mix(layer, table, h, deps=()):
        first = layer == 0
        return call(
            functools.partial(fwd_mix_kernel, first, seqs),
            ([shaped(F32, D, span)] if first else [])
            + [
                shaped(BF16, BLOCKS, 384, span),
                shaped(BF16, BLOCKS, 384, span),
                shaped(BF16, D, span),
                shaped(BF16, D, span),
                shaped(BF16, BLOCKS, 192, span),
                shaped(F32, D, span),
                shaped(F32, 8, span),
                shaped(F32, D, 128),
                shaped(F32, D, 256),
                mix_table,
            ],
            [
                pltpu.VMEM((D, span), BF16),
                pltpu.VMEM((BLOCK_W, span), F32),
                pltpu.VMEM((BLOCK_W, span), F32),
                fetched,
            ],
            table_specs + ([WHOLE] * (BLOCKS + 1) if first else [EARLY]) + [WHOLE] * 5,
            ([LATE] if first else []) + [LATE] * 6 + [WHOLE] * 3 + [LATE],
            18,
            deps,
        )(idx, *table, *([*h, chosen] if first else [h]), pad, hidden[layer], ahead_full, ahead_low, back_low)

    def ahead_ff(layer, table, middle, cols, deps=()):
        last = layer == LAYERS - 1
        return call(
            functools.partial(fwd_ff_kernel, last),
            [
                shaped(BF16, BLOCKS, 192, span),
                shaped(BF16, BLOCKS, 1536, span),
                shaped(BF16, BLOCKS, 192, span),
                shaped(BF16, BLOCKS, BLOCK_W, span) if last else shaped(F32, D, span),
                shaped(F32, 8, span),
                ff_table,
            ],
            [pltpu.VMEM((D, span), BF16), pltpu.VMEM((FF_BLOCK, span), BF16), fetched],
            table_specs + [EARLY] * 2,
            [LATE] * 4 + [WHOLE] + [LATE],
            15,
            deps,
        )(idx, *table, middle, cols)

    saved = []
    mix_zero, tokens_here, ff_zero, one = settle(mix_zero, tokens_here, ff_zero, one)
    ff_chips = over_chips(ff_zero)
    one = others_at_once(one, me)
    h, q1, proj, conv, gated, q2, middle, stats_one, cols, kspec, mix_w = ahead_mix(0, mix_zero, tokens_here)
    parts = token_parts(cotangent)
    middle, ff_chips, parts = settle(middle, ff_chips, parts)
    ff_zero = (ff[0], ff_chips, wide_shift(ff_chips, 1))
    middle, ff_zero, one, parts = settle(middle, ff_zero, one, parts)
    rows = MIX_ROWS // 8
    mix_chips = over_chips(one[:, :rows])
    near, far = narrow_shift(parts[1], 1), narrow_shift(parts[3], 3)
    q3, gate_up, q4, h_next, stats_two, ff_w = ahead_ff(0, ff_zero, middle, cols)
    saved.append((h, q1, proj, conv, gated, q2, middle, stats_one, cols, kspec, q3, gate_up, q4, stats_two, mix_w, ff_w))
    h, mix_chips, ff_one, near, far, across = settle(h_next, mix_chips, one[:, rows:], near, far, parts[2])
    mix_one = (mix[1], mix_chips, wide_shift(mix_chips, 1))
    h, mix_one, ff_one, across = settle(h, mix_one, ff_one, across)
    ff_chips = over_chips(ff_one)
    across = narrow_shift(across, 2)
    cotangent_here = [parts[0], near, across, far]
    q1, proj, conv, gated, q2, middle, stats_one, cols, kspec, mix_w = ahead_mix(1, mix_one, h)
    middle, ff_chips, cotangent_here = settle(middle, ff_chips, cotangent_here)
    ff_one = (ff[1], ff_chips, wide_shift(ff_chips, 1))
    middle, ff_one = settle(middle, ff_one)
    q3, gate_up, q4, h_last, stats_two, ff_w = ahead_ff(1, ff_one, middle, cols)
    saved.append((h, q1, proj, conv, gated, q2, middle, stats_one, cols, kspec, q3, gate_up, q4, stats_two, mix_w, ff_w))

    sizes = [weight.shape[2] // 128 for weight in factors]

    def finish(layer, names, groups, earlier):
        with_ff, with_mix = "ff" in sum(names, ()), "conv" in sum(names, ())
        shapes = [(LAYERS, size, 128) for size in (sizes[4:] if with_ff else []) + (sizes[:4] if with_mix else [])]
        shapes += [(LAYERS, BLOCK_W, 128)] if with_mix else []
        specs = [pl.BlockSpec((None, *shape[1:]), lambda _: (layer, 0, 0)) for shape in shapes]
        rest = []
        if with_mix and layer:
            rest = [(208, 256)]
        elif with_mix:
            rest = [(LAYERS, BLOCK_W)] * 3 + [(LAYERS, 3, 1, 384), (LAYERS, BLOCK_W), (1, BLOCK_W)]
            rest += [(5, LAYERS, 128), (LAYERS, 128), (LAYERS, 128, 128)]
        specs += [pl.BlockSpec(shape, lambda _, n=len(shape): (0,) * n) for shape in rest]
        arrays = [part for group in groups for part in group]
        inputs = [SCALARS] + [ANY] * (len(arrays) + len(earlier))
        if earlier and with_mix:
            inputs[-1] = pl.BlockSpec(earlier[-1].shape, lambda _: (0, 0))
        return pl.pallas_call(
            functools.partial(finish_kernel, layer, names),
            grid=(1,),
            out_shape=[shaped(F32, *shape) for shape in shapes + rest],
            in_specs=inputs,
            out_specs=specs,
            scratch_shapes=[
                pltpu.VMEM((FF_ROWS, 384), BF16),
                pltpu.VMEM((384, 384), BF16),
                pltpu.VMEM((IN_GRAD_ROWS, 384), BF16),
                pltpu.VMEM((2, 768, 128), F32),
                pltpu.SemaphoreType.DMA((24,)),
            ],
            input_output_aliases={1 + len(arrays) + at: at for at in range(len(shapes))} if earlier else {},
            compiler_params=pltpu.CompilerParams(vmem_limit_bytes=56 << 20),
            cost_estimate=pl.CostEstimate(flops=4 * 10**9, bytes_accessed=1 << 20, transcendentals=0),
        )(idx, *arrays, *earlier)

    def collect(table, dtype):
        return call(place_parts_kernel, shaped(dtype, BLOCK_W, BLOCKS * span), [], [WHOLE], WHOLE, 2)(table)

    def to_blocks(table):
        return lax.all_to_all(table, "narrow", split_axis=0, concat_axis=0, tiled=True)

    def back_ff(layer, g_top, deps):
        last = layer == LAYERS - 1
        h, q1, proj, conv, gated, q2, middle, stats_one, cols, kspec, q3, gate_up, q4, stats_two, mix_w, ff_w = saved[layer]
        return call(
            functools.partial(bwd_ff_kernel, last),
            [shaped(F32, D, span), *[shaped(BF16, 4, BLOCKS, FF_ROWS // 8, 384)] * 2, shaped(F32, BLOCKS, 16, BLOCK_W)],
            [
                pltpu.VMEM((BLOCKS, FF_ROWS, 384), BF16),
                pltpu.VMEM((D, span), BF16),
                pltpu.VMEM((BLOCKS, 192, span), BF16),
                pltpu.VMEM((BLOCKS, 192, span), BF16),
                pltpu.VMEM((2 * FF_BLOCK, span), BF16),
                pltpu.VMEM((D, span), F32),
                sent,
            ],
            [SCALARS, EARLY] + [EARLY] * (BLOCKS if last else 1) + [EARLY] * 4 + [WHOLE, EARLY],
            [LATE, ANY, ANY, WHOLE],
            27,
            deps,
        )(idx, ff_w, *(g_top if last else [g_top]), q4, gate_up, q3, middle, stats_two, cols)

    def back_conv(layer, g_mid, small_ff, deps):
        h, q1, proj, conv, gated, q2, middle, stats_one, cols, kspec, q3, gate_up, q4, stats_two, mix_w, ff_w = saved[layer]
        return call(
            functools.partial(bwd_conv_kernel, seqs, penalty),
            [shaped(BF16, BLOCKS, 384, span), *[shaped(BF16, 4, BLOCKS, 48, 384)] * 2],
            [
                pltpu.VMEM((BLOCKS, 384, 384), BF16),
                pltpu.VMEM((BLOCKS, 192, span), BF16),
                pltpu.VMEM((BLOCK_W, span), F32),
                pltpu.VMEM((BLOCK_W, span), F32),
                sent,
            ],
            [SCALARS, EARLY] + [EARLY] * 5 + [WHOLE] * 2 + [EARLY] + [WHOLE] * 7,
            [LATE, ANY, ANY],
            23,
            deps,
        )(
            idx,
            mix_w,
            g_mid,
            q2,
            gated,
            conv,
            proj,
            pad,
            cols,
            kspec,
            ahead_low,
            back_low,
            small_ff,
            hidden[layer],
            filter_two[layer],
            features,
            back_full,
        )

    def back_in(layer, gv, g_mid, deps):
        first = layer == 0
        h, q1, proj, conv, gated, q2, middle, stats_one, cols, kspec, q3, gate_up, q4, stats_two, mix_w, ff_w = saved[layer]
        return call(
            functools.partial(bwd_in_kernel, first),
            [
                shaped(BF16, BLOCKS, BLOCK_W, span) if first else shaped(F32, D, span),
                *[shaped(BF16, 4, BLOCKS, IN_GRAD_ROWS // 8, 384)] * 2,
            ],
            [
                pltpu.VMEM((BLOCKS, IN_GRAD_ROWS, 384), BF16),
                pltpu.VMEM((BLOCKS, 384, span), BF16),
                pltpu.VMEM((D, span), F32),
                pltpu.VMEM((BLOCKS, 16, BLOCK_W), F32),
                sent,
            ]
            + ([pltpu.VMEM((D, span), F32)] if first else []),
            [SCALARS] + [EARLY] * 5 + [WHOLE] * (3 if first else 2),
            [LATE, ANY, ANY],
            12,
            deps,
        )(idx, mix_w, gv, g_mid, q1, h, stats_one, cols, *([chosen] if first else []))

    def spread(piece):
        chips = over_chips(piece)
        return chips, wide_shift(chips, 1)

    def each_after(arrays, *deps):
        return [after(x, *deps) for x in arrays]

    h_last, cotangent_here = settle(h_last, cotangent_here)
    mixed_parts = to_blocks(h_last)
    g_mid, near, far, small_ff = back_ff(1, cotangent_here, ())
    g_mid, near, far = settle(g_mid, near, far)
    ff_one = reduce_core(near, far)
    gv, near, far = back_conv(1, g_mid, small_ff, ())
    gv, near, far, ff_one = settle(gv, near, far, ff_one)
    conv_one = reduce_core(near, far)
    ff_parts = [ff_one[0], wide_shift(ff_one[1], 2), wide_shift(ff_one[2], 4)]
    g_top, near, far = back_in(1, gv, g_mid, ())
    g_top, near, far, conv_one, ff_parts, last, mixed_parts = settle(
        g_top, near, far, conv_one, ff_parts, ff_one[3], mixed_parts
    )
    mixed_out = collect(mixed_parts, BF16)
    near, far, mixed_out = settle(near, reduce_core(near, far), mixed_out)
    mix_parts, g_top = settle(join_rows(conv_one, far), g_top)
    ff_parts = ff_parts + [wide_shift(last, 6)]
    mix_parts = move_chips(mix_parts)
    g_mid, near, far, small_ff = back_ff(0, g_top, ())
    g_mid, near, far, mix_parts, ff_parts = settle(g_mid, near, far, mix_parts, ff_parts)
    all_one = in_order(join_rows(add_chips(ff_parts), add_chips(mix_parts)), me)
    all_one, ff_zero = settle(all_one, reduce_core(near, far))
    all_parts = blocks_at_once(all_one)
    ff_parts = move_chips(ff_zero)
    gv, near, far = back_conv(0, g_mid, small_ff, ff_zero)
    gv, near, far, all_parts, ff_parts = settle(gv, near, far, all_parts, ff_parts)
    all_one = added(all_parts)
    one_chips = [all_one] + [wide_shift(all_one, 2 * m) for m in range(1, 4)]
    ff_parts = blocks_at_once(in_order(add_chips(ff_parts), me))
    conv_zero = reduce_core(near, far)
    g_top, near, far = back_in(0, gv, g_mid, ())
    ff_zero = added(ff_parts)
    g_top, near, far, one_chips = settle(g_top, near, far, one_chips)
    token_near, across = narrow_shift(g_top[1], 1), narrow_shift(g_top[2], 2)
    in_zero, ff_zero, conv_zero, one_chips = settle(reduce_core(near, far), ff_zero, conv_zero, one_chips)

    mix_parts = move_chips(join_rows(conv_zero, in_zero))
    one_chips = jnp.stack(one_chips)
    one_group = (one_chips, wide_shift(one_chips, 1))
    *flat, table_one = finish(1, (("ff", "conv", "in"),), (one_group,), [])
    mix_parts, flat, ff_zero, token_near, across = settle(mix_parts, flat, ff_zero, token_near, across)
    mix_zero = reduce_blocks(add_chips(mix_parts))
    ff_chips = over_chips(ff_zero)
    mix_zero, ff_chips, token_far = settle(mix_zero, ff_chips, g_top[3])
    mix_chips = over_chips(mix_zero)
    ff_group = (ff_chips, wide_shift(ff_chips, 1))
    token_far = narrow_shift(token_far, 3)
    flat_ff = finish(0, (("ff",),), (ff_group,), flat[:4])
    mix_chips, flat_ff, token_far = settle(mix_chips, flat_ff, token_far)
    mix_group = (mix_chips, wide_shift(mix_chips, 1))
    flat_mix = finish(0, (("conv", "in"),), (mix_group,), [*flat[4:], table_one])
    flat = [*flat_mix[:4], *flat_ff, *flat_mix[4:]]
    grad_tokens = call(
        place_distances_kernel,
        shaped(F32, BLOCK_W, BLOCKS * span),
        [],
        [SCALARS] + [WHOLE] * BLOCKS,
        WHOLE,
        2,
    )(idx, g_top[0], token_near, across, token_far)
    grads = [table.reshape(LAYERS, 1, table.shape[1] * 128) for table in flat[:8]]
    three, g_gain_one, g_gain_two, g_skip, g_taps, g_decay, g_mask, g_one, g_bias, g_two = flat[8:]
    return (
        mixed_out,
        grad_tokens,
        g_mask[0],
        g_gain_one,
        grads[0],
        grads[1],
        g_taps,
        g_skip,
        g_decay,
        g_one.transpose(1, 0, 2),
        g_bias,
        g_two,
        three,
        grads[2],
        grads[3],
        g_gain_two,
        grads[4],
        grads[5],
        grads[6],
        grads[7],
    )


def solution(mesh):
    placed = (
        P("narrow", "wide"),
        P("wide"),
        P("wide", None),
        P("narrow", "wide"),
        P("narrow"),
        P(None, "narrow"),
        P(None, "narrow", None),
        P(None, "narrow", None),
        P(None, None, "narrow", None),
        P(None, "narrow"),
        P(None, "narrow"),
        P(),
        P(),
        P(),
        P(None, "narrow", None),
        P(None, "narrow", None),
        P(None, "narrow", None),
        P(None, "narrow"),
        P(None, "narrow", None),
        P(None, "narrow", None),
        P(None, "narrow", None),
        P(None, "narrow", None),
    )
    return jax.shard_map(
        local,
        mesh=mesh,
        in_specs=placed,
        out_specs=(
            P("narrow", "wide"),
            P("narrow", "wide"),
            P("narrow"),
            P(None, "narrow"),
            P(None, "narrow", None),
            P(None, "narrow", None),
            P(None, None, "narrow", None),
            P(None, "narrow"),
            P(None, "narrow"),
            P(),
            P(),
            P(),
            P(None, "narrow", None),
            P(None, "narrow", None),
            P(None, "narrow", None),
            P(None, "narrow"),
            P(None, "narrow", None),
            P(None, "narrow", None),
            P(None, "narrow", None),
            P(None, "narrow", None),
        ),
        check_vma=False,
    )
```

```python
import math
import functools
import numpy as np
import jax
import jax.numpy as jnp
from jax import lax
from jax.experimental import pallas as pl
from jax.experimental.pallas import tpu as pltpu
from jax.sharding import PartitionSpec as P

F32 = jnp.float32
BF16 = jnp.bfloat16
D = 768
LENGTH = 128
LAYERS = 2
BLOCK_W = 192
FF_BLOCK = 768
BLOCKS = 4
EPSILON = 1e-05
HIGHEST = lax.Precision.HIGHEST
GAIN_ONE, GAIN_TWO, SKIP, TAP_X, TAP_G, MASK, DECAY = 0, 1, 2, 3, 6, 9, 10
IN_ONE, IN_TWO, OUT_ROWS, PARAM_ROWS = 0, 192, 576, 768
UP_ONE, UP_TWO, DOWN_ONE = 0, 192, 960
MIX_ROWS, FF_USED, FF_ROWS, IN_GRAD_ROWS = 1024, 1344, 1408, 640
HIDDEN_ONE, HIDDEN_TWO, SLOPE_ONE, SLOPE_TWO = 0, 1, 2, 3
PIECE_ROWS = {"ff": 176, "conv": 48, "in": 80}


def nn(a, b):
    return lax.dot_general(a, b, (((1,), (0,)), ((), ())), preferred_element_type=F32)


def nt(a, b):
    return lax.dot_general(a, b, (((1,), (1,)), ((), ())), preferred_element_type=F32)


def tn(a, b):
    return lax.dot_general(a, b, (((0,), (0,)), ((), ())), preferred_element_type=F32)


def spectrum_tables():
    time = np.arange(2 * LENGTH)
    freq = np.arange(LENGTH)
    angle = 2.0 * np.pi * np.outer(time, freq) / (2 * LENGTH)
    ahead = np.concatenate([np.cos(angle), -np.sin(angle)], axis=1)
    ahead[:, LENGTH] = np.cos(np.pi * time)
    scale = np.full((2 * LENGTH,), 2.0 / (2 * LENGTH))
    scale[0] = scale[LENGTH] = 1.0 / (2 * LENGTH)
    return ahead.astype(np.float32), (ahead * scale[None, :]).T.astype(np.float32)


def lanes_of(shape):
    return lax.broadcasted_iota(jnp.int32, shape, 1)


def column(cols, rows, at, lanes=LENGTH):
    one = jnp.broadcast_to(cols[rows, at : at + 1], (BLOCK_W, LENGTH))
    return one if lanes == LENGTH else jnp.concatenate([one] * (lanes // LENGTH), axis=1)


def later(v, lane):
    return jnp.where(lane == 0, 0.0, pltpu.roll(v, 1, 1))


def earlier(v, lane):
    return jnp.where(lane == LENGTH - 1, 0.0, pltpu.roll(v, LENGTH - 1, 1))


def norm_rows(parts):
    total = sum(jnp.sum(p, axis=0, keepdims=True) for p in parts)
    squares = sum(jnp.sum(p * p, axis=0, keepdims=True) for p in parts)
    mean = total / D
    inv = lax.rsqrt(squares / D - mean * mean + EPSILON)
    return mean, inv


def block(ref, b, width=BLOCK_W):
    return ref[pl.ds(b * width, width), :]


def fwd_mix_kernel(first, seqs, *refs):
    idx, own, rel_a, rel_b, *refs = refs
    if first:
        *parts, chosen_ref = refs[: BLOCKS + 1]
        refs = refs[BLOCKS + 1 :]
    else:
        h_ref, *refs = refs
    pad, hidden, ahead_full, ahead, back, *refs = refs
    if first:
        h_ref, *refs = refs
    q1, proj, conv, gated, q2, middle, stats, cols, kspec, table, normed, xs, gs, sem = refs
    at = distances(idx)
    if not first:
        h_ref.start()
    fetched = fetch_table(idx, own, rel_a, rel_b, table.buffer, sem)
    w = table.buffer
    if first:
        fetched()
        make_params(w, at, hidden, ahead_full, cols, kspec)
        keep = chosen_ref[0:1, :]
        for k, part in enumerate(parts):
            rows = pl.ds(pl.multiple_of(block_of(idx, k) * BLOCK_W, BLOCK_W), BLOCK_W)
            h_ref.buffer[rows, :] = part[...].astype(F32) * (1.0 - keep) + keep * column(cols, rows, MASK, seqs * LENGTH)
        h_ref.start()
        h_ref = h_ref.buffer
    else:
        h_ref = h_ref.wait()
    mean, inv = norm_rows([block(h_ref, b) for b in range(BLOCKS)])
    if not first:
        fetched()
        make_params(w, at, hidden, ahead_full, cols, kspec)
    table.start()
    stats[0:1, :] = mean
    stats[1:2, :] = inv
    for b in range(BLOCKS):
        rows = pl.ds(b * BLOCK_W, BLOCK_W)
        normed[rows, :] = ((h_ref[rows, :] - mean) * inv * column(cols, rows, GAIN_ONE, seqs * LENGTH)).astype(BF16)
    for b in range(BLOCKS):
        inner = tn(w[at[b], IN_ONE : IN_ONE + 192, :], block(normed, b)).astype(BF16)
        for c in range(BLOCKS):
            q1.buffer[c, 96 * b : 96 * b + 96, :] = inner[96 * c : 96 * c + 96]
    q1.start()
    lane = lanes_of((BLOCK_W, LENGTH))
    row_lane = lanes_of((BLOCK_W, LENGTH))
    for c in range(BLOCKS):
        rows = pl.ds(c * BLOCK_W, BLOCK_W)
        value = tn(w[at[c], IN_TWO : IN_TWO + 384, :], q1.buffer[c]) * pad[0:1, :]
        proj.buffer[c] = value.astype(BF16)
        taps = [[column(cols, rows, tap + n) for n in range(3)] for tap in (TAP_X, TAP_G)]
        skip = column(cols, rows, SKIP)
        for s in range(seqs):
            here = slice(s * LENGTH, (s + 1) * LENGTH)
            for part, tap, out in ((0, taps[0], xs), (192, taps[1], gs)):
                v = value[part : part + 192, here]
                out[:, here] = (
                    tap[0] * later(v, lane)
                    + tap[1] * v
                    + tap[2] * earlier(v, lane)
                )
        signal = jnp.concatenate([xs[:, s * LENGTH : (s + 1) * LENGTH] for s in range(seqs)], axis=0)
        spec = nn(signal.astype(BF16), ahead[...])
        k_re = kspec[rows, 0:LENGTH]
        k_im = kspec[rows, LENGTH : 2 * LENGTH]
        k_off = jnp.where(row_lane == 0, 0.0, k_im)
        k_im = jnp.where(row_lane == 0, k_im, k_re)
        made = []
        for s in range(seqs):
            re = spec[s * 192 : s * 192 + 192, 0:LENGTH]
            im = spec[s * 192 : s * 192 + 192, LENGTH : 2 * LENGTH]
            made.append(
                jnp.concatenate([re * k_re - im * k_off, re * k_off + im * k_im], axis=1).astype(BF16)
            )
        y = nn(jnp.concatenate(made, axis=0), back[...])
        for s in range(seqs):
            here = slice(s * LENGTH, (s + 1) * LENGTH)
            value = y[s * 192 : s * 192 + 192] + skip * xs[:, here]
            conv.buffer[rows, here] = value.astype(BF16)
            gated.buffer[rows, here] = (value * gs[:, here]).astype(BF16)
    for part in (proj, conv, gated):
        part.start()
    for b in range(BLOCKS):
        inner = tn(w[at[b], OUT_ROWS : OUT_ROWS + 192, 0:192], block(gated.buffer, b)).astype(BF16)
        for c in range(BLOCKS):
            q2.buffer[c, 48 * b : 48 * b + 48, :] = inner[48 * c : 48 * c + 48]
    q2.start()
    for c in range(BLOCKS):
        rows = pl.ds(c * BLOCK_W, BLOCK_W)
        middle.buffer[rows, :] = h_ref[rows, :] + tn(w[at[c], OUT_ROWS : OUT_ROWS + 192, 192:384], q2.buffer[c])
        middle.start((rows, slice(None)))


def gelu_of(v):
    rate = math.sqrt(2.0 / math.pi)
    return v * (0.5 + 0.5 * jnp.tanh(v * (rate + 0.044715 * rate * (v * v))))


def fwd_ff_kernel(last, idx, own, rel_a, rel_b, middle, cols, q3, gate_up, q4, h_next, stats, table, normed, act, sem):
    at = distances(idx)
    middle.start()
    cols.start()
    fetched = fetch_table(idx, own, rel_a, rel_b, table.buffer, sem)
    w = table.buffer
    middle, cols = middle.wait(), cols.wait()
    mean, inv = norm_rows([block(middle, b) for b in range(BLOCKS)])
    stats[0:1, :] = mean
    stats[1:2, :] = inv
    for b in range(BLOCKS):
        rows = pl.ds(b * BLOCK_W, BLOCK_W)
        normed[rows, :] = ((middle[rows, :] - mean) * inv * column(cols, rows, GAIN_TWO, middle.shape[1])).astype(BF16)
    fetched()
    table.start()
    for b in range(BLOCKS):
        inner = tn(w[at[b], UP_ONE : UP_ONE + 192, 0:192], block(normed, b)).astype(BF16)
        for c in range(BLOCKS):
            q3.buffer[c, 48 * b : 48 * b + 48, :] = inner[48 * c : 48 * c + 48]
    q3.start()
    for c in range(BLOCKS):
        for half in range(2):
            ups = []
            for piece in (half, half + 2):
                ups.append(tn(w[at[c], UP_TWO + 192 * piece : UP_TWO + 192 * piece + 192, :], q3.buffer[c]))
            gate, up = ups[0], ups[1].astype(BF16)
            gate_up.buffer[c, 384 * half : 384 * half + 384, :] = gate.astype(BF16)
            gate_up.buffer[c, 768 + 384 * half : 768 + 384 * half + 384, :] = up
            act[384 * half : 384 * half + 384, :] = gelu_of(gate).astype(BF16) * up
        gate_up.start(c)
        inner = (
            tn(w[at[c], DOWN_ONE : DOWN_ONE + 384, 0:192], act[0:384, :])
            + tn(w[at[c], DOWN_ONE : DOWN_ONE + 384, 192:384], act[384:768, :])
        ).astype(BF16)
        for to in range(BLOCKS):
            q4.buffer[to, 48 * c : 48 * c + 48, :] = inner[48 * to : 48 * to + 48]
    q4.start()
    for c in range(BLOCKS):
        rows = pl.ds(c * BLOCK_W, BLOCK_W)
        value = middle[rows, :] + tn(w[at[c], UP_ONE : UP_ONE + 192, 192:384], q4.buffer[c])
        if last:
            h_next.buffer[c] = value.astype(BF16)
            h_next.start(c)
        else:
            h_next.buffer[rows, :] = value
            h_next.start((rows, slice(None)))


def bwd_ff_kernel(last, idx, table, *refs):
    parts = refs[: BLOCKS if last else 1]
    q4, gate_up, q3, middle, stats, cols, g_mid, g_near, g_far, small, g_w, g_low, gi4, gi3, g_gu, g_n, sem = refs[len(parts) :]
    at = distances(idx)
    for part in parts:
        part.start()
    q4.start()
    table.start((slice(None), slice(UP_ONE, UP_ONE + 192)))
    gate_up.start(0)
    table.start((slice(None), slice(DOWN_ONE, FF_USED)))
    table.start((slice(None), slice(UP_TWO, DOWN_ONE)))
    q3.start()
    for b in range(1, BLOCKS):
        gate_up.start(b)
    for part in (middle, cols):
        part.start()
    w = table.buffer
    mean = stats[0:1, :]
    inv = stats[1:2, :]
    if last:
        for k, part in enumerate(parts):
            g_low[pl.ds(pl.multiple_of(block_of(idx, k) * BLOCK_W, BLOCK_W), BLOCK_W), :] = part.wait()[...]
        g_top = g_low
    else:
        g_top = parts[0].wait()
        for c in range(BLOCKS):
            g_low[c * 192 : c * 192 + 192, :] = block(g_top, c).astype(BF16)
    for b in range(BLOCKS):
        g_w[at[b], FF_USED:FF_ROWS, :] = jnp.zeros((FF_ROWS - FF_USED, 384), BF16)
    table.wait(0)
    q4 = q4.wait()
    for c in range(BLOCKS):
        gt = block(g_low, c)
        g_w[at[c], UP_ONE : UP_ONE + 192, 192:384] = nt(q4[c], gt).astype(BF16)
        gq = nn(w[at[c], UP_ONE : UP_ONE + 192, 192:384], gt).astype(BF16)
        for b in range(BLOCKS):
            gi4[b, 48 * c : 48 * c + 48, :] = gq[48 * b : 48 * b + 48]
    rate = math.sqrt(2.0 / math.pi)
    table.wait(1)
    for b in range(BLOCKS):
        gate_up.wait(b)
        if b == 0:
            table.wait()
            q3.wait()
        for half in range(2):
            span = slice(192 * half, 192 * half + 192)
            gate = gate_up.buffer[b, 384 * half : 384 * half + 384, :].astype(F32)
            up = gate_up.buffer[b, 768 + 384 * half : 768 + 384 * half + 384, :]
            ga = nn(w[at[b], DOWN_ONE : DOWN_ONE + 384, span], gi4[b]).astype(BF16)
            square = gate * gate
            rise = 0.5 + 0.5 * jnp.tanh(gate * (rate + 0.044715 * rate * square))
            gelu = (gate * rise).astype(BF16)
            slope = rise * (1.0 + (1.0 - rise) * (gate * (2.0 * rate + 6.0 * 0.044715 * rate * square)))
            g_w[at[b], DOWN_ONE : DOWN_ONE + 384, span] = nt(gelu * up, gi4[b]).astype(BF16)
            g_gu[384 * half : 384 * half + 384, :] = ga * (up * slope.astype(BF16))
            g_gu[768 + 384 * half : 768 + 384 * half + 384, :] = ga * gelu
        gq = None
        for piece in range(4):
            rows = slice(UP_TWO + 192 * piece, UP_TWO + 192 * piece + 192)
            gg = g_gu[384 * piece : 384 * piece + 384, :]
            g_w[at[b], rows, :] = nt(q3.buffer[b], gg).astype(BF16)
            term = nn(w[at[b], rows, :], gg)
            gq = term if gq is None else gq + term
        gq = gq.astype(BF16)
        for to in range(BLOCKS):
            gi3[to, 48 * b : 48 * b + 48, :] = gq[48 * to : 48 * to + 48]
    finish = send_early(g_w, (g_near, g_far), idx, sem, UP_ONE + 192)
    norm_back(
        at, middle.wait(), mean, inv, cols.wait(), GAIN_TWO, w, slice(UP_ONE, UP_ONE + 192), slice(0, 192), gi3, g_n, g_w, small, 1, g_top, g_mid
    )
    finish()


def row_sums(place, values):
    lanes = values.shape[1]
    part = values[:, 0:LENGTH]
    for at in range(LENGTH, lanes, LENGTH):
        part = part + values[:, at : at + LENGTH]
    high = part.astype(BF16)
    low = (part - high.astype(F32)).astype(BF16)
    pick = (lax.broadcasted_iota(jnp.int32, (16, LENGTH), 0) == place).astype(F32).astype(BF16)
    return nt(pick, high) + nt(pick, low)


def norm_back(at, h, mean, inv, cols, gain_at, w, w_rows, w_lanes, gi, g_n, g_w, small, place, g_in, g_out):
    plain = cross = 0.0
    for b in range(BLOCKS):
        rows = pl.ds(b * 192, 192)
        gain = column(cols, rows, gain_at, h.shape[1])
        xh = (h[rows, :] - mean) * inv
        gn = nn(w[at[b], w_rows, w_lanes], gi[b])
        g_w[at[b], w_rows, w_lanes] = nt((xh * gain).astype(BF16), gi[b]).astype(BF16)
        gx = gn * xh
        small[b] = row_sums(place, gx)
        g_n[rows, :] = gn * gain
        plain = plain + jnp.sum(gn * gain, axis=0, keepdims=True)
        cross = cross + jnp.sum(gx * gain, axis=0, keepdims=True)
    plain = plain / D
    cross = cross / D
    for b in range(BLOCKS):
        rows = pl.ds(b * 192, 192)
        xh = (h[rows, :] - mean) * inv
        value = g_in[rows, :].astype(F32) + inv * (g_n[rows, :] - plain - xh * cross)
        if isinstance(g_out, Move):
            g_out.buffer[rows, :] = value
            g_out.start((rows, slice(None)))
        else:
            g_out[rows, :] = value


def bwd_conv_kernel(
    seqs, penalty, idx, table, g_mid, q2, gated, conv, proj, pad, cols, kspec, ahead, back, small_ff,
    filt, weight_two, features, back_full, gv, g_near, g_far, g_w, gi2, gcs, xs, sem
):
    at = distances(idx)
    table.start((slice(None), slice(OUT_ROWS, PARAM_ROWS + BLOCK_W)))
    for part in (q2, g_mid, gated, proj, conv, kspec):
        part.start()
    w, q2, g_mid = table.wait(), q2.wait(), g_mid.wait()
    for c in range(BLOCKS):
        gt = block(g_mid, c).astype(BF16)
        g_w[at[c], 0:192, 192:384] = nt(q2[c], gt).astype(BF16)
        gq = nn(w[at[c], OUT_ROWS : OUT_ROWS + 192, 192:384], gt).astype(BF16)
        for b in range(BLOCKS):
            gi2[b, 48 * c : 48 * c + 48, :] = gq[48 * b : 48 * b + 48]
    lane = lanes_of((BLOCK_W, LENGTH))
    first_lane = lane == 0
    for part in (gated, proj, conv):
        part.wait()
    kspec = kspec.wait()
    for b in range(BLOCKS):
        rows = pl.ds(b * 192, 192)
        g_gated = nn(w[at[b], OUT_ROWS : OUT_ROWS + 192, 0:192], gi2[b])
        g_w[at[b], 0:192, 0:192] = nt(block(gated.buffer, b), gi2[b]).astype(BF16)
        tap_x = [column(cols, rows, TAP_X + n) for n in range(3)]
        tap_g = [column(cols, rows, TAP_G + n) for n in range(3)]
        skip = column(cols, rows, SKIP)
        sums = [0.0] * 7
        for s in range(seqs):
            here = slice(s * LENGTH, (s + 1) * LENGTH)
            v = proj.buffer[b, 0:192, here].astype(F32)
            xs[:, here] = (
                tap_x[0] * later(v, lane)
                + tap_x[1] * v
                + tap_x[2] * earlier(v, lane)
            )
            v = proj.buffer[b, 192:384, here].astype(F32)
            after, before = later(v, lane), earlier(v, lane)
            gate = (
                tap_g[0] * after
                + tap_g[1] * v
                + tap_g[2] * before
            )
            gg = g_gated[:, here]
            gcs[:, here] = gg * gate
            z = gg * conv.buffer[rows, here].astype(F32)
            sums[4] = sums[4] + z * after
            sums[5] = sums[5] + z * v
            sums[6] = sums[6] + z * before
            gv.buffer[b, 192:384, here] = (
                (
                    tap_g[0] * earlier(z, lane)
                    + tap_g[1] * z
                    + tap_g[2] * later(z, lane)
                )
                * pad[0:1, here]
            ).astype(BF16)
            sums[0] = sums[0] + gcs[:, here] * xs[:, here]
        stacked = jnp.concatenate(
            [ref[:, s * LENGTH : (s + 1) * LENGTH] for ref in (xs, gcs) for s in range(seqs)], axis=0
        )
        spec = nn(stacked.astype(BF16), ahead[...])
        k_re = kspec[rows, 0:LENGTH]
        k_im = kspec[rows, LENGTH : 2 * LENGTH]
        k_off = jnp.where(first_lane, 0.0, k_im)
        k_im = jnp.where(first_lane, k_im, k_re)
        made = []
        p_re = p_im = p_off = 0.0
        for s in range(seqs):
            x_re = spec[s * 192 : s * 192 + 192, 0:LENGTH]
            x_im = spec[s * 192 : s * 192 + 192, LENGTH : 2 * LENGTH]
            start = (seqs + s) * 192
            g_re = spec[start : start + 192, 0:LENGTH]
            g_im = spec[start : start + 192, LENGTH : 2 * LENGTH]
            p_re = p_re + g_re * x_re
            p_im = p_im + g_im * x_im
            p_off = p_off + (g_im * x_re - g_re * x_im)
            made.append(
                jnp.concatenate([g_re * k_re + g_im * k_off, g_im * k_im - g_re * k_off], axis=1).astype(BF16)
            )
        g_table = exact(
            jnp.concatenate(
                [jnp.where(first_lane, p_re, p_re + p_im), jnp.where(first_lane, p_im, p_off)], axis=1
            ),
            back_full[...],
            1,
            0,
        )
        last, envelope, kernel = filter_values(w, at, b, cols, filt[HIDDEN_TWO])
        g_table = g_table + penalty * kernel
        g_decay = -(g_table * kernel * filter_lag())
        g_shape = g_table * envelope
        g_w[at[b], 192:384, 0:128] = exact(g_shape, filt[HIDDEN_TWO], 1, 0).astype(BF16)
        term = exact(g_shape, last, 0, 0)
        g_hidden = term if b == 0 else g_hidden + term
        y = nn(jnp.concatenate(made, axis=0), back[...])
        for s in range(seqs):
            here = slice(s * LENGTH, (s + 1) * LENGTH)
            z = y[s * 192 : s * 192 + 192] + skip * gcs[:, here]
            v = proj.buffer[b, 0:192, here].astype(F32)
            sums[1] = sums[1] + z * later(v, lane)
            sums[2] = sums[2] + z * v
            sums[3] = sums[3] + z * earlier(v, lane)
            gv.buffer[b, 0:192, here] = (
                (
                    tap_x[0] * earlier(z, lane)
                    + tap_x[1] * z
                    + tap_x[2] * later(z, lane)
                )
                * pad[0:1, here]
            ).astype(BF16)
        gv.start(b)
        totals = small_ff[b]
        for place, value in enumerate(sums + [g_decay]):
            totals = totals + row_sums(2 + place, value)
        totals = totals.astype(BF16)
        g_w[at[b], 192:208, 256:384] = totals[:, 0:128]
        g_w[at[b], 208:224, 256:320] = totals[:, 128:192]
        g_w[at[b], 208:224, 320:384] = jnp.zeros((16, 64), BF16)
        g_w[at[b], 224:384, 256:384] = jnp.zeros((160, 128), BF16)
    g_two = g_hidden * filt[SLOPE_TWO]
    g_one = exact(g_two, weight_two[...], 1, 1) * filt[SLOPE_ONE]
    g_weight_two = exact(filt[HIDDEN_ONE], g_two, 0, 0).astype(BF16)
    g_weight_one = exact(features[...], g_one, 0, 0)[0:16, :].astype(BF16)
    for b in range(BLOCKS):
        g_w[at[b], 192:320, 128:256] = g_weight_two
        g_w[at[b], 320:336, 128:256] = g_weight_one
        g_w[at[b], 336:384, 128:256] = jnp.zeros((48, 128), BF16)
    send_pieces(g_w, (g_near, g_far), idx, sem)


def bwd_in_kernel(first, *refs):
    refs = list(refs)
    idx, table, gv, g_mid, q1, h, stats, cols = refs[:8]
    refs = refs[8:]
    chosen = refs.pop(0) if first else None
    g_out, g_near, g_far, g_w, gi1, g_n, small, sem = refs[:8]
    g_h = refs[8] if first else g_out
    at = distances(idx)
    for c in range(BLOCKS):
        gv.start(c)
        q1.start(c)
        if c == 0:
            table.start((slice(None), slice(IN_ONE, OUT_ROWS)))
    for part in (h, g_mid):
        part.start()
    w = table.wait()
    mean = stats[0:1, :]
    inv = stats[1:2, :]
    for c in range(BLOCKS):
        gv.wait(c)
        q1.wait(c)
        g_w[at[c], IN_TWO : IN_TWO + 384, :] = nt(q1.buffer[c], gv.buffer[c]).astype(BF16)
        gq = nn(w[at[c], IN_TWO : IN_TWO + 384, :], gv.buffer[c]).astype(BF16)
        for b in range(BLOCKS):
            gi1[b, 96 * c : 96 * c + 96, :] = gq[96 * b : 96 * b + 96]
    norm_back(
        at, h.wait(), mean, inv, cols, GAIN_ONE, w, slice(IN_ONE, IN_ONE + 192), slice(0, 384), gi1, g_n, g_w, small, 0, g_mid.wait(), g_h
    )
    for b in range(BLOCKS):
        rows = pl.ds(b * 192, 192)
        totals = small[b]
        if first:
            value = g_h[rows, :]
            masked = value * chosen[0:1, :]
            totals = totals + row_sums(1, masked)
            ahead_by = (b - idx[0]) & (BLOCKS - 1)
            g_out.buffer[ahead_by] = (value - masked).astype(BF16)
            g_out.start(ahead_by)
        g_w[at[b], 576:592, 0:192] = totals.astype(BF16)
        g_w[at[b], 576:592, 192:384] = jnp.zeros((16, 192), BF16)
        g_w[at[b], 592:640, :] = jnp.zeros((48, 384), BF16)
    send_pieces(g_w, (g_near, g_far), idx, sem)


def piece_rows(idx, core, chip, rows):
    return pl.ds(pl.multiple_of((idx[1] ^ (2 * chip + core)) * rows, 16), rows)


def block_of(idx, k):
    return (idx[0] - k) & (BLOCKS - 1)


def distances(idx):
    return [(idx[0] - b) & (BLOCKS - 1) for b in range(BLOCKS)]


def start_copies(pairs, sem):
    copies = [pltpu.make_async_copy(source, target, sem.at[at]) for at, (source, target) in enumerate(pairs)]
    for copy in copies:
        copy.start()

    def wait():
        for copy in copies:
            copy.wait()

    return wait


def run_copies(pairs, sem):
    start_copies(pairs, sem)()


def send_early(table, outs, idx, sem, done):
    rows = outs[0].shape[2]
    late = -(-done // rows)
    copies = []
    for core in range(2):
        for chip in range(4):
            at = idx[1] ^ (2 * chip + core)
            copy = pltpu.make_async_copy(
                table.at[:, piece_rows(idx, core, chip, rows), :], outs[core].at[chip], sem.at[len(copies)]
            )
            pl.when(at >= late)(copy.start)
            copies.append((at, copy))

    def finish():
        for at, copy in copies:
            pl.when(at < late)(copy.start)
        for _, copy in copies:
            copy.wait()

    return finish


def send_pieces(table, outs, idx, sem):
    rows = outs[0].shape[2]
    run_copies(
        [(table.at[:, piece_rows(idx, core, chip, rows), :], outs[core].at[chip]) for core in range(2) for chip in range(4)],
        sem,
    )


def fetch_table(idx, own, rel_a, rel_b, table, sem):
    rows = rel_a.shape[2]
    return start_copies(
        [(own, table.at[0])]
        + [
            (rel.at[chip], table.at[1:BLOCKS, piece_rows(idx, core, chip, rows), :])
            for core, rel in enumerate((rel_a, rel_b))
            for chip in range(4)
        ],
        sem,
    )


def exact(a, b, left, right):
    return lax.dot_general(
        a, b, (((left,), (right,)), ((), ())), precision=HIGHEST, preferred_element_type=F32
    )


def filter_lag():
    place = lanes_of((BLOCK_W, 2 * LENGTH))
    return jnp.where(place < LENGTH, place, 2 * LENGTH - place).astype(F32)


def filter_values(w, at, b, cols, hidden):
    packed = w[at[b], PARAM_ROWS : PARAM_ROWS + BLOCK_W, 0:256].astype(F32)
    last = packed[:, 0:128] + packed[:, 128:256]
    lag = filter_lag()
    envelope = jnp.exp(-lag * cols[b * BLOCK_W : (b + 1) * BLOCK_W, DECAY : DECAY + 1]) * (1.0 / math.sqrt(LENGTH))
    envelope = jnp.where(lag == LENGTH, 0.0, envelope)
    return last, envelope, exact(last, hidden, 1, 1) * envelope


def make_params(w, at, hidden, ahead_full, cols, kspec):
    for b in range(BLOCKS):
        rows = pl.ds(b * BLOCK_W, BLOCK_W)
        three = w[at[b], PARAM_ROWS : PARAM_ROWS + BLOCK_W, 256:384].astype(F32)
        cols[rows, :] = three + pltpu.roll(three, 128 - 16, 1) + pltpu.roll(three, 128 - 32, 1)
        kspec[rows, :] = exact(filter_values(w, at, b, cols, hidden[HIDDEN_TWO])[2], ahead_full[...], 1, 0)


def fold_back(lines, wide, count):
    low = lanes_of((count // 2, 128)) < 64
    one, two, three = (lines[pl.ds(j, count // 2, stride=3), :] for j in range(3))
    three = pltpu.roll(three, 64, 1)
    wide[0, pl.ds(0, count // 2, stride=2), :] = one
    wide[1, pl.ds(0, count // 2, stride=2), :] = two
    wide[0, pl.ds(1, count // 2, stride=2), :] = jnp.where(low, pltpu.roll(two, 64, 1), three)
    wide[1, pl.ds(1, count // 2, stride=2), :] = three


def fold_out(wide, out, count):
    low = lanes_of((count // 2, 128)) < 64
    half = count // 2
    even_a = wide[0, pl.ds(0, half, stride=2), :]
    even_b = wide[1, pl.ds(0, half, stride=2), :]
    odd_a = pltpu.roll(wide[0, pl.ds(1, half, stride=2), :], 64, 1)
    odd_b = pltpu.roll(wide[1, pl.ds(1, half, stride=2), :], 64, 1)
    out[pl.ds(0, half, stride=3), :] = even_a
    out[pl.ds(1, half, stride=3), :] = jnp.where(low, even_b, odd_a)
    out[pl.ds(2, half, stride=3), :] = jnp.where(low, odd_a, odd_b)


def spread_lines(flat, layer, count, lanes, lines):
    rows = flat.shape[1]
    lines[0:rows, :] = flat[layer].astype(F32)
    return [lines[pl.ds(j, count, stride=lanes), :] for j in range(lanes)]


def narrow_lines(flat, layer, count, lines, wide):
    rows = flat.shape[1]
    lines[0:rows, :] = flat[layer].astype(F32)
    fold_back(lines, wide, count)
    return jnp.concatenate([wide[0, 0:count, :], wide[1, 0:count, 0:64]], axis=1).astype(BF16)


def own_piece(idx, table, out):
    rows = out.shape[0]
    out[...] = table[pl.ds(pl.multiple_of(idx[1] * rows, 16), rows), :]


def pack_mix_kernel(
    idx, in_one, in_two, out_one, out_two, gain_one, gain_two, skip, taps, mask, decay, filter_three,
    table_a, table_b, piece_a, piece_b, lines, wide, cols,
):
    tables, pieces = (table_a, table_b), (piece_a, piece_b)
    eye = (
        lax.broadcasted_iota(jnp.int32, (16, 128), 0) == lax.broadcasted_iota(jnp.int32, (16, 128), 1)
    ).astype(F32)
    cols[...] = jnp.zeros((16, BLOCK_W), F32)
    for layer in range(LAYERS):
        table = tables[layer]
        for flat, start, count in ((in_one, IN_ONE, 192), (in_two, IN_TWO, 384)):
            for j, part in enumerate(spread_lines(flat, layer, count, 3, lines)):
                table[start : start + count, 128 * j : 128 * j + 128] = part.astype(BF16)
        table[OUT_ROWS : OUT_ROWS + 192, 0:192] = narrow_lines(out_one, layer, 192, lines, wide)
        table[OUT_ROWS : OUT_ROWS + 192, 192:384] = narrow_lines(out_two, layer, 192, lines, wide)
        last = filter_three[layer]
        high = last.astype(BF16)
        rows = slice(PARAM_ROWS, PARAM_ROWS + BLOCK_W)
        table[rows, 0:128] = high
        table[rows, 128:256] = (last - high.astype(F32)).astype(BF16)
        for at, source in ((GAIN_ONE, gain_one), (GAIN_TWO, gain_two), (SKIP, skip), (DECAY, decay)):
            cols[at : at + 1, :] = source[layer : layer + 1, :]
        cols[TAP_X : TAP_X + 3, :] = taps[layer, :, 0:BLOCK_W]
        cols[TAP_G : TAP_G + 3, :] = taps[layer, :, BLOCK_W : 2 * BLOCK_W]
        cols[MASK : MASK + 1, :] = mask[...]
        left = lax.dot_general(
            cols[...], eye, (((0,), (0,)), ((), ())), precision=HIGHEST, preferred_element_type=F32
        )
        terms = jnp.zeros((BLOCK_W, 128), F32)
        for at in range(3):
            part = left.astype(BF16).astype(F32)
            left = left - part
            terms = terms + (pltpu.roll(part, 16 * at, 1) if at else part)
        table[rows, 256:384] = terms.astype(BF16)
        table[PARAM_ROWS + BLOCK_W : MIX_ROWS, :] = jnp.zeros((MIX_ROWS - PARAM_ROWS - BLOCK_W, 384), BF16)
        own_piece(idx, table, pieces[layer])


def pack_ff_kernel(idx, up_one, up_two, down_one, down_two, table_a, table_b, piece_a, piece_b, lines, wide):
    tables, pieces = (table_a, table_b), (piece_a, piece_b)
    for layer in range(LAYERS):
        table = tables[layer]
        table[UP_ONE : UP_ONE + 192, 0:192] = narrow_lines(up_one, layer, 192, lines, wide)
        table[UP_ONE : UP_ONE + 192, 192:384] = narrow_lines(down_two, layer, 192, lines, wide)
        for j, part in enumerate(spread_lines(up_two, layer, 192, 12, lines)):
            at = UP_TWO + 192 * (j // 3)
            table[at : at + 192, 128 * (j % 3) : 128 * (j % 3) + 128] = part.astype(BF16)
        down = narrow_lines(down_one, layer, 768, lines, wide)
        table[DOWN_ONE : DOWN_ONE + 384, 0:192] = down[0:384]
        table[DOWN_ONE : DOWN_ONE + 384, 192:384] = down[384:768]
        table[FF_USED:FF_ROWS, :] = jnp.zeros((FF_ROWS - FF_USED, 384), BF16)
        own_piece(idx, table, pieces[layer])


def finish_kernel(layer, groups, idx, *refs):
    count = 2 * len(groups)
    pieces, refs = refs[:count], refs[count:]
    names = sum(groups, ())
    with_ff, with_mix = "ff" in names, "conv" in names
    outs = 4 * with_ff + 5 * with_mix
    if layer == 0:
        refs = refs[outs:]
        if with_mix:
            other, refs = refs[0], refs[1:]
    if with_ff:
        up_one, up_two, down_one, down_two = refs[:4]
        refs = refs[4:]
    if with_mix:
        in_one, in_two, out_one, out_two, three = refs[:5]
        refs = refs[5:]
    rest, (ff, conv, inp, wide, sem) = refs[:-5], refs[-5:]
    tables = {"ff": ff, "conv": conv, "in": inp}
    pairs = []
    for at, group in enumerate(groups):
        for core in range(2):
            rel = pieces[2 * at + core]
            first = 0
            for name in group:
                rows = PIECE_ROWS[name]
                for chip in range(4):
                    pairs.append(
                        (rel.at[chip, pl.ds(first, rows), :], tables[name].at[piece_rows(idx, core, chip, rows), :])
                    )
                first += rows
    run_copies(pairs, sem)

    def spread(out, values, lanes, first):
        count = values.shape[0]
        for j in range(3):
            out[pl.ds(first + j, count, stride=lanes), :] = values[:, 128 * j : 128 * j + 128].astype(F32)

    def narrow_of(out, values):
        count = values.shape[0]
        wide[0, 0:count, :] = values[:, 0:128].astype(F32)
        wide[1, 0:count, 0:64] = values[:, 128:192].astype(F32)
        fold_out(wide, out, count)

    if with_ff:
        for q in range(4):
            at = UP_TWO + 192 * q
            spread(up_two, ff[at : at + 192, :], 12, 3 * q)
        narrow_of(up_one, ff[UP_ONE : UP_ONE + 192, 0:192])
        narrow_of(down_two, ff[UP_ONE : UP_ONE + 192, 192:384])
        narrow_of(
            down_one,
            jnp.concatenate([ff[DOWN_ONE : DOWN_ONE + 384, 0:192], ff[DOWN_ONE : DOWN_ONE + 384, 192:384]], axis=0),
        )
    if not with_mix:
        return
    spread(in_one, inp[IN_ONE : IN_ONE + 192, :], 3, 0)
    spread(in_two, inp[IN_TWO : IN_TWO + 384, :], 3, 0)
    narrow_of(out_one, conv[0:192, 0:192])
    narrow_of(out_two, conv[0:192, 192:384])
    three[...] = conv[192:384, 0:128].astype(F32)
    if layer > 0:
        rest[0][0:192, :] = conv[192:384, 128:384].astype(F32)
        rest[0][192:208, :] = inp[576:592, 0:256].astype(F32)
        return
    g_gain_one, g_gain_two, g_skip, g_taps, g_decay, g_mask, g_one, g_bias, g_two = rest
    for at in range(LAYERS):
        if at:
            shared, small, last = other[0:192, 0:128], other[0:32, 128:256], other[192:208, 0:192]
        else:
            shared = conv[192:384, 128:256].astype(F32)
            small = conv[192:224, 256:384].astype(F32)
            last = inp[576:592, 0:192].astype(F32)
        small = jnp.concatenate([small[0:16], small[16:32, 0:64]], axis=1)
        here = slice(at, at + 1)
        g_gain_one[here, :] = last[0:1]
        g_gain_two[here, :] = small[1:2]
        g_skip[here, :] = small[2:3]
        both = jnp.concatenate([small[3:6], small[6:9]], axis=1)
        for tap in range(3):
            g_taps[at, tap, :, :] = both[tap : tap + 1]
        g_decay[here, :] = small[9:10]
        g_two[at] = shared[0:128]
        for row in range(5):
            g_one[row, here, :] = shared[128 + row : 129 + row]
        g_bias[here, :] = shared[133:134]
        if at == 0:
            g_mask[...] = last[1:2]


ANY = pl.BlockSpec(memory_space=pl.ANY)
SCALARS = pl.BlockSpec(memory_space=pltpu.SMEM)
WHOLE = pl.BlockSpec(memory_space=pltpu.VMEM)


def shaped(dtype, *shape):
    return jax.ShapeDtypeStruct(shape, dtype)


EARLY = "early"
LATE = "late"


class Move:
    def __init__(self, buffer, operand, sem, inward):
        self.buffer, self.operand, self.sem, self.inward = buffer, operand, sem, inward
        self.open = []

    def start(self, part=None):
        here = self.buffer if part is None else self.buffer.at[part]
        there = self.operand if part is None else self.operand.at[part]
        pair = (there, here) if self.inward else (here, there)
        copy = pltpu.make_async_copy(*pair, self.sem.at[len(self.open)])
        copy.start()
        self.open.append(copy)

    def wait(self, at=None):
        for n, copy in enumerate(self.open):
            if copy is not None and (at is None or n == at):
                copy.wait()
                self.open[n] = None
        return self.buffer


def call(kernel, outs, scratch, in_specs, out_specs, micros, deps=()):
    outs = list(outs) if isinstance(outs, (list, tuple)) else [outs]
    out_specs = list(out_specs) if isinstance(out_specs, (list, tuple)) else [out_specs]
    ins, own = len(in_specs), len(scratch)
    early = [at for at, spec in enumerate(in_specs) if spec is EARLY]
    late = [at for at, spec in enumerate(out_specs) if spec is LATE]

    def body(*refs):
        inputs = list(refs[:ins])
        refs = refs[ins + len(deps) :]
        results = list(refs[: len(outs)])
        mine, refs = refs[len(outs) : len(outs) + own], refs[len(outs) + own :]
        for j, at in enumerate(early):
            inputs[at] = Move(refs[j], inputs[at], refs[-1].at[j], True)
        for j, at in enumerate(late):
            results[at] = Move(refs[len(early) + j], results[at], refs[-1].at[len(early) + j], False)
        kernel(*inputs, *results, *mine)
        for at in late:
            results[at].wait()

    def run(*arrays):
        buffers = [pltpu.VMEM(arrays[at].shape, arrays[at].dtype) for at in early]
        buffers += [pltpu.VMEM(outs[at].shape, outs[at].dtype) for at in late]
        if buffers:
            buffers.append(pltpu.SemaphoreType.DMA((len(buffers), BLOCKS)))
        made = pl.pallas_call(
            body,
            out_shape=outs,
            in_specs=[ANY if spec is EARLY else spec for spec in in_specs] + [ANY] * len(deps),
            out_specs=[ANY if spec is LATE else spec for spec in out_specs],
            scratch_shapes=list(scratch) + buffers,
            compiler_params=pltpu.CompilerParams(vmem_limit_bytes=54 << 20),
            cost_estimate=pl.CostEstimate(flops=int(micros * 1e9), bytes_accessed=1 << 20, transcendentals=0),
        )(*arrays, *deps)
        return made if len(outs) > 1 else made[0]

    return run


def place_distances_kernel(idx, *refs):
    parts, out = refs[:BLOCKS], refs[BLOCKS]
    span = parts[0].shape[1]
    for k, part in enumerate(parts):
        out[:, pl.ds(pl.multiple_of(block_of(idx, k) * span, 128), span)] = part[...].astype(out.dtype)


def place_parts_kernel(table, out):
    span = table.shape[2]
    for b in range(BLOCKS):
        out[:, b * span : (b + 1) * span] = table[b].astype(out.dtype)


def wide_shift(x, mask):
    return lax.ppermute(x, "wide", [(i, i ^ mask) for i in range(lax.axis_size("wide"))])


def narrow_shift(x, by):
    narrow = lax.axis_size("narrow")
    return lax.ppermute(x, "narrow", [(i, (i + by) % narrow) for i in range(narrow)])


def added(parts):
    return sum(p.astype(F32) for p in parts).astype(parts[0].dtype)


def after(x, *deps):
    return lax.optimization_barrier((x, deps))[0]


def settle(*trees):
    return lax.optimization_barrier(trees)


def exchange(parts):
    return [parts[0]] + [narrow_shift(parts[k], k) for k in range(1, BLOCKS)]


def over_blocks(piece):
    return jnp.stack([narrow_shift(piece, k) for k in range(1, BLOCKS)])


def others_at_once(pieces, me):
    moved = lax.all_to_all(pieces, "narrow", split_axis=0, concat_axis=0, tiled=True)
    return jnp.stack([lax.dynamic_index_in_dim(moved, (me - k) % BLOCKS, 0, keepdims=False) for k in range(1, BLOCKS)])


def over_chips(x):
    return jnp.stack([x] + [wide_shift(x, 2 * m) for m in range(1, 4)])


def reduce_core(near, far):
    moved = wide_shift(far, 1)
    return [added([near[m], moved[m]]) for m in range(4)]


def move_chips(half):
    return [half[0]] + [wide_shift(half[m], 2 * m) for m in range(1, 4)]


def add_chips(parts):
    total = [added([part[k] for part in parts]) for k in range(BLOCKS)]
    groups = lax.axis_size("wide") // 8
    if groups > 1:
        total = [added([t] + [wide_shift(t, 8 * g) for g in range(1, groups)]) for t in total]
    return total


def reduce_blocks(total):
    return added([total[0]] + [narrow_shift(total[k], -k) for k in range(1, BLOCKS)])


def in_order(total, me):
    table = jnp.stack(total)
    return jnp.stack([lax.dynamic_index_in_dim(table, (me - b) % BLOCKS, 0, keepdims=False) for b in range(BLOCKS)])


def blocks_at_once(table):
    moved = lax.all_to_all(table, "narrow", split_axis=0, concat_axis=0, tiled=True)
    return [moved[b] for b in range(BLOCKS)]


def join_rows(*tables):
    return [jnp.concatenate(parts, axis=-2) for parts in zip(*tables)]


def filter_features():
    place = np.arange(2 * LENGTH)
    relative = np.where(place < LENGTH, place, place - 2 * LENGTH) / LENGTH
    table = np.zeros((2 * LENGTH, 128))
    for at, value in enumerate(
        (
            relative,
            np.cos(np.pi * relative),
            np.sin(np.pi * relative),
            np.cos(37.0 * np.pi * relative),
            np.sin(37.0 * np.pi * relative),
            np.ones_like(relative),
        )
    ):
        table[:, at] = value
    return jnp.asarray(table.astype(np.float32))


def filter_hidden(features, weight_one, bias_one, weight_two):
    one = jnp.dot(features[:, :5], weight_one, precision=HIGHEST) + bias_one
    hidden_one = jnp.sin(one)
    two = jnp.dot(hidden_one, weight_two, precision=HIGHEST)
    return jnp.stack([hidden_one, jnp.sin(two), jnp.cos(one), jnp.cos(two)])


def local(
    tokens,
    lengths,
    masked,
    cotangent,
    mask_vector,
    gain_one,
    in_first,
    in_second,
    short_taps,
    skip_gain,
    decay_rates,
    filter_one,
    filter_bias,
    filter_two,
    filter_three,
    out_first,
    out_second,
    gain_two,
    up_first,
    up_second,
    down_first,
    down_second,
):
    wide_count = lax.axis_size("wide")
    me = lax.axis_index("narrow")
    place = lax.axis_index("wide") & 7
    idx = jnp.stack([me, place]).astype(jnp.int32)
    seqs = lengths.shape[0] // BLOCKS
    span = seqs * LENGTH
    all_tokens = tokens.shape[1] * wide_count

    def token_parts(table):
        return [lax.dynamic_slice_in_dim(table, ((me + k) % BLOCKS) * span, span, 1) for k in range(BLOCKS)]

    def flat_lines(weight):
        return weight.reshape(LAYERS, weight.shape[2] // 128, 128)

    factors = [in_first, in_second, out_first, out_second, up_first, up_second, down_first, down_second]
    lines = [flat_lines(weight) for weight in factors]
    tokens_here = exchange(token_parts(tokens))

    def pack(kernel, rows, arrays, deps=(), scratch=()):
        return call(
            kernel,
            [shaped(BF16, rows, 384)] * LAYERS + [shaped(BF16, rows // 8, 384)] * LAYERS,
            [pltpu.VMEM((2304, 128), F32), pltpu.VMEM((2, 768, 128), F32)] + list(scratch),
            [SCALARS] + [WHOLE] * len(arrays),
            [WHOLE] * (2 * LAYERS),
            3,
            deps,
        )(idx, *arrays)

    per_feature = [gain_one, gain_two, skip_gain, short_taps[:, :, 0], mask_vector[None], decay_rates, filter_three]
    *mix, mix_zero, mix_one = pack(
        pack_mix_kernel, MIX_ROWS, lines[:4] + per_feature, scratch=[pltpu.VMEM((16, BLOCK_W), F32)]
    )
    ahead, back = spectrum_tables()
    ahead_low = jnp.asarray(ahead[:LENGTH]).astype(BF16)
    back_low = jnp.asarray(back[:, :LENGTH]).astype(BF16)
    ahead_full = jnp.asarray(ahead)
    features = filter_features()
    back_full = jnp.asarray(back)
    hidden = [
        filter_hidden(features, filter_one[layer], filter_bias[layer], filter_two[layer]) for layer in range(LAYERS)
    ]
    own_lengths = lax.dynamic_slice_in_dim(lengths, me * seqs, seqs, 0)
    own_masked = lax.dynamic_slice_in_dim(masked, me * seqs, seqs, 0)
    positions = jnp.arange(LENGTH, dtype=jnp.int32)
    pad = (positions[None, :] < own_lengths[:, None]).astype(F32).reshape(1, span)
    pad = jnp.broadcast_to(pad, (8, span))
    chosen = jnp.broadcast_to(own_masked.astype(F32).reshape(1, span), (8, span))

    parts = token_parts(tokens)
    near, across = narrow_shift(parts[1], 1), narrow_shift(parts[2], 2)

    mix_zero = others_at_once(jnp.stack([mix_zero] * BLOCKS), me)
    *ff, ff_zero, ff_one = pack(pack_ff_kernel, FF_ROWS, lines[4:], (near, across))
    mix_zero, ff_zero, hidden, near, across, far, pad, chosen = settle(
        mix_zero, ff_zero, hidden, near, across, parts[3], pad, chosen
    )
    far = narrow_shift(far, 3)
    mix_chips = over_chips(mix_zero)
    ff_zero = others_at_once(jnp.stack([ff_zero] * BLOCKS), me)
    one = jnp.stack([jnp.concatenate([mix_one, ff_one], axis=0)] * BLOCKS)
    mix_chips, ff_zero, one, far = settle(mix_chips, ff_zero, one, far)
    mix_zero = (mix[0], mix_chips, wide_shift(mix_chips, 1))
    tokens_here = [parts[0], near, across, far]

    penalty = 4.0 * math.sqrt(all_tokens) / (wide_count * BLOCKS)
    mix_table = shaped(BF16, BLOCKS, MIX_ROWS, 384)
    ff_table = shaped(BF16, BLOCKS, FF_ROWS, 384)
    fetched = pltpu.SemaphoreType.DMA((9,))
    sent = pltpu.SemaphoreType.DMA((8,))
    table_specs = [SCALARS, ANY, ANY, ANY]

    def ahead_mix(layer, table, h, deps=()):
        first = layer == 0
        return call(
            functools.partial(fwd_mix_kernel, first, seqs),
            ([shaped(F32, D, span)] if first else [])
            + [
                shaped(BF16, BLOCKS, 384, span),
                shaped(BF16, BLOCKS, 384, span),
                shaped(BF16, D, span),
                shaped(BF16, D, span),
                shaped(BF16, BLOCKS, 192, span),
                shaped(F32, D, span),
                shaped(F32, 8, span),
                shaped(F32, D, 128),
                shaped(F32, D, 256),
                mix_table,
            ],
            [
                pltpu.VMEM((D, span), BF16),
                pltpu.VMEM((BLOCK_W, span), F32),
                pltpu.VMEM((BLOCK_W, span), F32),
                fetched,
            ],
            table_specs + ([WHOLE] * (BLOCKS + 1) if first else [EARLY]) + [WHOLE] * 5,
            ([LATE] if first else []) + [LATE] * 6 + [WHOLE] * 3 + [LATE],
            18,
            deps,
        )(idx, *table, *([*h, chosen] if first else [h]), pad, hidden[layer], ahead_full, ahead_low, back_low)

    def ahead_ff(layer, table, middle, cols, deps=()):
        last = layer == LAYERS - 1
        return call(
            functools.partial(fwd_ff_kernel, last),
            [
                shaped(BF16, BLOCKS, 192, span),
                shaped(BF16, BLOCKS, 1536, span),
                shaped(BF16, BLOCKS, 192, span),
                shaped(BF16, BLOCKS, BLOCK_W, span) if last else shaped(F32, D, span),
                shaped(F32, 8, span),
                ff_table,
            ],
            [pltpu.VMEM((D, span), BF16), pltpu.VMEM((FF_BLOCK, span), BF16), fetched],
            table_specs + [EARLY] * 2,
            [LATE] * 4 + [WHOLE] + [LATE],
            15,
            deps,
        )(idx, *table, middle, cols)

    saved = []
    mix_zero, tokens_here, ff_zero, one = settle(mix_zero, tokens_here, ff_zero, one)
    ff_chips = over_chips(ff_zero)
    one = others_at_once(one, me)
    h, q1, proj, conv, gated, q2, middle, stats_one, cols, kspec, mix_w = ahead_mix(0, mix_zero, tokens_here)
    parts = token_parts(cotangent)
    middle, ff_chips, parts = settle(middle, ff_chips, parts)
    ff_zero = (ff[0], ff_chips, wide_shift(ff_chips, 1))
    middle, ff_zero, one, parts = settle(middle, ff_zero, one, parts)
    rows = MIX_ROWS // 8
    mix_chips = over_chips(one[:, :rows])
    near, far = narrow_shift(parts[1], 1), narrow_shift(parts[3], 3)
    q3, gate_up, q4, h_next, stats_two, ff_w = ahead_ff(0, ff_zero, middle, cols)
    saved.append((h, q1, proj, conv, gated, q2, middle, stats_one, cols, kspec, q3, gate_up, q4, stats_two, mix_w, ff_w))
    h, mix_chips, ff_one, near, far, across = settle(h_next, mix_chips, one[:, rows:], near, far, parts[2])
    mix_one = (mix[1], mix_chips, wide_shift(mix_chips, 1))
    h, mix_one, ff_one, across = settle(h, mix_one, ff_one, across)
    ff_chips = over_chips(ff_one)
    across = narrow_shift(across, 2)
    cotangent_here = [parts[0], near, across, far]
    q1, proj, conv, gated, q2, middle, stats_one, cols, kspec, mix_w = ahead_mix(1, mix_one, h)
    middle, ff_chips, cotangent_here = settle(middle, ff_chips, cotangent_here)
    ff_one = (ff[1], ff_chips, wide_shift(ff_chips, 1))
    middle, ff_one = settle(middle, ff_one)
    q3, gate_up, q4, h_last, stats_two, ff_w = ahead_ff(1, ff_one, middle, cols)
    saved.append((h, q1, proj, conv, gated, q2, middle, stats_one, cols, kspec, q3, gate_up, q4, stats_two, mix_w, ff_w))

    sizes = [weight.shape[2] // 128 for weight in factors]

    def finish(layer, names, groups, earlier):
        with_ff, with_mix = "ff" in sum(names, ()), "conv" in sum(names, ())
        shapes = [(LAYERS, size, 128) for size in (sizes[4:] if with_ff else []) + (sizes[:4] if with_mix else [])]
        shapes += [(LAYERS, BLOCK_W, 128)] if with_mix else []
        specs = [pl.BlockSpec((None, *shape[1:]), lambda _: (layer, 0, 0)) for shape in shapes]
        rest = []
        if with_mix and layer:
            rest = [(208, 256)]
        elif with_mix:
            rest = [(LAYERS, BLOCK_W)] * 3 + [(LAYERS, 3, 1, 384), (LAYERS, BLOCK_W), (1, BLOCK_W)]
            rest += [(5, LAYERS, 128), (LAYERS, 128), (LAYERS, 128, 128)]
        specs += [pl.BlockSpec(shape, lambda _, n=len(shape): (0,) * n) for shape in rest]
        arrays = [part for group in groups for part in group]
        inputs = [SCALARS] + [ANY] * (len(arrays) + len(earlier))
        if earlier and with_mix:
            inputs[-1] = pl.BlockSpec(earlier[-1].shape, lambda _: (0, 0))
        return pl.pallas_call(
            functools.partial(finish_kernel, layer, names),
            grid=(1,),
            out_shape=[shaped(F32, *shape) for shape in shapes + rest],
            in_specs=inputs,
            out_specs=specs,
            scratch_shapes=[
                pltpu.VMEM((FF_ROWS, 384), BF16),
                pltpu.VMEM((384, 384), BF16),
                pltpu.VMEM((IN_GRAD_ROWS, 384), BF16),
                pltpu.VMEM((2, 768, 128), F32),
                pltpu.SemaphoreType.DMA((24,)),
            ],
            input_output_aliases={1 + len(arrays) + at: at for at in range(len(shapes))} if earlier else {},
            compiler_params=pltpu.CompilerParams(vmem_limit_bytes=56 << 20),
            cost_estimate=pl.CostEstimate(flops=4 * 10**9, bytes_accessed=1 << 20, transcendentals=0),
        )(idx, *arrays, *earlier)

    def collect(table, dtype):
        return call(place_parts_kernel, shaped(dtype, BLOCK_W, BLOCKS * span), [], [WHOLE], WHOLE, 2)(table)

    def to_blocks(table):
        return lax.all_to_all(table, "narrow", split_axis=0, concat_axis=0, tiled=True)

    def back_ff(layer, g_top, deps):
        last = layer == LAYERS - 1
        h, q1, proj, conv, gated, q2, middle, stats_one, cols, kspec, q3, gate_up, q4, stats_two, mix_w, ff_w = saved[layer]
        return call(
            functools.partial(bwd_ff_kernel, last),
            [shaped(F32, D, span), *[shaped(BF16, 4, BLOCKS, FF_ROWS // 8, 384)] * 2, shaped(F32, BLOCKS, 16, BLOCK_W)],
            [
                pltpu.VMEM((BLOCKS, FF_ROWS, 384), BF16),
                pltpu.VMEM((D, span), BF16),
                pltpu.VMEM((BLOCKS, 192, span), BF16),
                pltpu.VMEM((BLOCKS, 192, span), BF16),
                pltpu.VMEM((2 * FF_BLOCK, span), BF16),
                pltpu.VMEM((D, span), F32),
                sent,
            ],
            [SCALARS, EARLY] + [EARLY] * (BLOCKS if last else 1) + [EARLY] * 4 + [WHOLE, EARLY],
            [LATE, ANY, ANY, WHOLE],
            27,
            deps,
        )(idx, ff_w, *(g_top if last else [g_top]), q4, gate_up, q3, middle, stats_two, cols)

    def back_conv(layer, g_mid, small_ff, deps):
        h, q1, proj, conv, gated, q2, middle, stats_one, cols, kspec, q3, gate_up, q4, stats_two, mix_w, ff_w = saved[layer]
        return call(
            functools.partial(bwd_conv_kernel, seqs, penalty),
            [shaped(BF16, BLOCKS, 384, span), *[shaped(BF16, 4, BLOCKS, 48, 384)] * 2],
            [
                pltpu.VMEM((BLOCKS, 384, 384), BF16),
                pltpu.VMEM((BLOCKS, 192, span), BF16),
                pltpu.VMEM((BLOCK_W, span), F32),
                pltpu.VMEM((BLOCK_W, span), F32),
                sent,
            ],
            [SCALARS, EARLY] + [EARLY] * 5 + [WHOLE] * 2 + [EARLY] + [WHOLE] * 7,
            [LATE, ANY, ANY],
            23,
            deps,
        )(
            idx,
            mix_w,
            g_mid,
            q2,
            gated,
            conv,
            proj,
            pad,
            cols,
            kspec,
            ahead_low,
            back_low,
            small_ff,
            hidden[layer],
            filter_two[layer],
            features,
            back_full,
        )

    def back_in(layer, gv, g_mid, deps):
        first = layer == 0
        h, q1, proj, conv, gated, q2, middle, stats_one, cols, kspec, q3, gate_up, q4, stats_two, mix_w, ff_w = saved[layer]
        return call(
            functools.partial(bwd_in_kernel, first),
            [
                shaped(BF16, BLOCKS, BLOCK_W, span) if first else shaped(F32, D, span),
                *[shaped(BF16, 4, BLOCKS, IN_GRAD_ROWS // 8, 384)] * 2,
            ],
            [
                pltpu.VMEM((BLOCKS, IN_GRAD_ROWS, 384), BF16),
                pltpu.VMEM((BLOCKS, 384, span), BF16),
                pltpu.VMEM((D, span), F32),
                pltpu.VMEM((BLOCKS, 16, BLOCK_W), F32),
                sent,
            ]
            + ([pltpu.VMEM((D, span), F32)] if first else []),
            [SCALARS] + [EARLY] * 5 + [WHOLE] * (3 if first else 2),
            [LATE, ANY, ANY],
            12,
            deps,
        )(idx, mix_w, gv, g_mid, q1, h, stats_one, cols, *([chosen] if first else []))

    def spread(piece):
        chips = over_chips(piece)
        return chips, wide_shift(chips, 1)

    def each_after(arrays, *deps):
        return [after(x, *deps) for x in arrays]

    h_last, cotangent_here = settle(h_last, cotangent_here)
    mixed_parts = to_blocks(h_last)
    g_mid, near, far, small_ff = back_ff(1, cotangent_here, ())
    g_mid, near, far = settle(g_mid, near, far)
    ff_one = reduce_core(near, far)
    gv, near, far = back_conv(1, g_mid, small_ff, ())
    gv, near, far, ff_one = settle(gv, near, far, ff_one)
    conv_one = reduce_core(near, far)
    ff_parts = [ff_one[0], wide_shift(ff_one[1], 2), wide_shift(ff_one[2], 4)]
    g_top, near, far = back_in(1, gv, g_mid, ())
    g_top, near, far, conv_one, ff_parts, last, mixed_parts = settle(
        g_top, near, far, conv_one, ff_parts, ff_one[3], mixed_parts
    )
    mixed_out = collect(mixed_parts, BF16)
    near, far, mixed_out = settle(near, reduce_core(near, far), mixed_out)
    mix_parts, g_top = settle(join_rows(conv_one, far), g_top)
    ff_parts = ff_parts + [wide_shift(last, 6)]
    mix_parts = move_chips(mix_parts)
    g_mid, near, far, small_ff = back_ff(0, g_top, ())
    g_mid, near, far, mix_parts, ff_parts = settle(g_mid, near, far, mix_parts, ff_parts)
    all_one = in_order(join_rows(add_chips(ff_parts), add_chips(mix_parts)), me)
    all_one, ff_zero = settle(all_one, reduce_core(near, far))
    all_parts = blocks_at_once(all_one)
    ff_parts = move_chips(ff_zero)
    gv, near, far = back_conv(0, g_mid, small_ff, ff_zero)
    gv, near, far, all_parts, ff_parts = settle(gv, near, far, all_parts, ff_parts)
    all_one = added(all_parts)
    one_chips = [all_one] + [wide_shift(all_one, 2 * m) for m in range(1, 4)]
    ff_parts = blocks_at_once(in_order(add_chips(ff_parts), me))
    conv_zero = reduce_core(near, far)
    g_top, near, far = back_in(0, gv, g_mid, ())
    ff_zero = added(ff_parts)
    g_top, near, far, one_chips = settle(g_top, near, far, one_chips)
    token_near, across = narrow_shift(g_top[1], 1), narrow_shift(g_top[2], 2)
    in_zero, ff_zero, conv_zero, one_chips = settle(reduce_core(near, far), ff_zero, conv_zero, one_chips)

    mix_parts = move_chips(join_rows(conv_zero, in_zero))
    one_chips = jnp.stack(one_chips)
    one_group = (one_chips, wide_shift(one_chips, 1))
    *flat, table_one = finish(1, (("ff", "conv", "in"),), (one_group,), [])
    mix_parts, flat, ff_zero, token_near, across = settle(mix_parts, flat, ff_zero, token_near, across)
    mix_zero = reduce_blocks(add_chips(mix_parts))
    ff_chips = over_chips(ff_zero)
    mix_zero, ff_chips, token_far = settle(mix_zero, ff_chips, g_top[3])
    mix_chips = over_chips(mix_zero)
    ff_group = (ff_chips, wide_shift(ff_chips, 1))
    token_far = narrow_shift(token_far, 3)
    flat_ff = finish(0, (("ff",),), (ff_group,), flat[:4])
    mix_chips, flat_ff, token_far = settle(mix_chips, flat_ff, token_far)
    mix_group = (mix_chips, wide_shift(mix_chips, 1))
    flat_mix = finish(0, (("conv", "in"),), (mix_group,), [*flat[4:], table_one])
    flat = [*flat_mix[:4], *flat_ff, *flat_mix[4:]]
    grad_tokens = call(
        place_distances_kernel,
        shaped(F32, BLOCK_W, BLOCKS * span),
        [],
        [SCALARS] + [WHOLE] * BLOCKS,
        WHOLE,
        2,
    )(idx, g_top[0], token_near, across, token_far)
    grads = [table.reshape(LAYERS, 1, table.shape[1] * 128) for table in flat[:8]]
    three, g_gain_one, g_gain_two, g_skip, g_taps, g_decay, g_mask, g_one, g_bias, g_two = flat[8:]
    return (
        mixed_out,
        grad_tokens,
        g_mask[0],
        g_gain_one,
        grads[0],
        grads[1],
        g_taps,
        g_skip,
        g_decay,
        g_one.transpose(1, 0, 2),
        g_bias,
        g_two,
        three,
        grads[2],
        grads[3],
        g_gain_two,
        grads[4],
        grads[5],
        grads[6],
        grads[7],
    )


def solution(mesh):
    placed = (
        P("narrow", "wide"),
        P("wide"),
        P("wide", None),
        P("narrow", "wide"),
        P("narrow"),
        P(None, "narrow"),
        P(None, "narrow", None),
        P(None, "narrow", None),
        P(None, None, "narrow", None),
        P(None, "narrow"),
        P(None, "narrow"),
        P(),
        P(),
        P(),
        P(None, "narrow", None),
        P(None, "narrow", None),
        P(None, "narrow", None),
        P(None, "narrow"),
        P(None, "narrow", None),
        P(None, "narrow", None),
        P(None, "narrow", None),
        P(None, "narrow", None),
    )
    return jax.shard_map(
        local,
        mesh=mesh,
        in_specs=placed,
        out_specs=(
            P("narrow", "wide"),
            P("narrow", "wide"),
            P("narrow"),
            P(None, "narrow"),
            P(None, "narrow", None),
            P(None, "narrow", None),
            P(None, None, "narrow", None),
            P(None, "narrow"),
            P(None, "narrow"),
            P(),
            P(),
            P(),
            P(None, "narrow", None),
            P(None, "narrow", None),
            P(None, "narrow", None),
            P(None, "narrow"),
            P(None, "narrow", None),
            P(None, "narrow", None),
            P(None, "narrow", None),
            P(None, "narrow", None),
        ),
        check_vma=False,
    )
```
